256 devices in a mesh: seq: 64 (over y, z, core), head: 4 (over x).
Axes of the slice: x: 4, y: 4, z: 8, core: 2. Of those that a mesh axis runs over, the one named last changes fastest.
Arguments:
- queries: bfloat16 [32768, 2048], P('seq', 'head'), may hold values from -6 to 6
- key_vectors: bfloat16 [32768, 2048], P('seq', 'head'), may hold values from -8 to 8
- value_vectors: bfloat16 [32768, 2048], P('seq', 'head'), may hold values from -40 to 40
- norm_gain: float32 [2048], P('head'), may hold values from 0.25 to 1.75
- out_weight: bfloat16 [2048, 2048], P('head'), may hold values from -0.125 to 0.125
Outputs:
- projected: bfloat16 [32768, 2048], P(('seq', 'head'))
The draws below stay inside these ranges and needn't reach their ends.
All inputs are finite; a program needn't handle non-finite values.
Results may differ from the reference program's by a relative error of at most 0.013.
Values may be sent and summed in bfloat16 or wider, within the bound.
A program may use at most 128 MiB of HBM per device.

```python
import math
import jax
import jax.numpy as jnp
from jax import lax

D = 2048
HEADS = 16
DH = 128
TOKENS = 32768


def draw_key_vectors(key, part):
    key_noise, key_mixing = jax.random.split(jax.random.fold_in(key, 11))
    noise = jax.random.normal(key_noise, (TOKENS, HEADS, DH), jnp.float32)
    mixing = jax.random.normal(key_mixing, (HEADS, DH, DH), jnp.float32) * DH ** (-0.5)
    mixed_keys = jnp.einsum('thd,hde->the', noise, mixing)
    return jnp.clip(mixed_keys, -8.0, 8.0).reshape(TOKENS, HEADS * DH).astype(jnp.bfloat16)


def draw_value_vectors(key, part):
    key_base, key_column = jax.random.split(jax.random.fold_in(key, 23), 2)
    feature_count = HEADS * DH
    column = jnp.exp(jax.random.uniform(key_column, (feature_count,), jnp.float32, 0.0, math.log(10.0)))
    sample = jax.random.normal(key_base, (TOKENS, feature_count), jnp.float32)
    return jnp.clip(sample * column, -40.0, 40.0).astype(jnp.bfloat16)


def level_of(rng, dims, cuts, least, top_value):
    def one(dim, shards_of):
        draws = jax.random.uniform(jax.random.fold_in(jax.random.fold_in(rng, 6), dim), (shards_of,), jnp.float32, least / len(cuts), top_value / len(cuts))
        return jnp.repeat(jnp.exp(draws), dims[dim] // shards_of).reshape((-1,) + (1,) * (len(dims) - dim - 1))

    gain = one(*cuts[0])
    for cut in cuts[1:]:
        gain = gain * one(*cut)
    return gain


def normal_values(key, shape, scale, limit, cuts=(), kind=jnp.bfloat16):
    loudness = level_of(key, shape, cuts, -0.22, 0.18) if cuts else 1.0
    drawn = jax.random.normal(key, shape, jnp.float32) * scale * loudness
    return jnp.minimum(jnp.maximum(drawn, -limit), limit).astype(kind)


def setup_inputs(seed: int = 0) -> dict:
    seeds = jax.random.split(jax.random.key(seed), 6)
    return {
        "queries": normal_values(seeds[0], (TOKENS, HEADS * DH), 1.0, 6.0, ((0, 64), (1, 4))),
        "key_vectors": draw_key_vectors(jax.random.fold_in(seeds[5], 71), 0),
        "value_vectors": draw_value_vectors(jax.random.fold_in(seeds[5], 71), 0),
        "norm_gain": jnp.clip(1.0 + 0.15 * jax.random.normal(seeds[3], (HEADS * DH,), jnp.float32), 0.25, 1.75),
        "out_weight": normal_values(seeds[4], (HEADS * DH, D), (HEADS * DH) ** -0.5, 0.125, ((0, 4),)),
    }


highest = lax.Precision.HIGHEST

def attend_all(queries, key_vectors, value_vectors):
    token_rows = queries.shape[0]
    head_count = queries.shape[1] // DH
    block_len = math.gcd(token_rows, 256)
    block_count = token_rows // block_len

    def blocked(array):
        return array.astype(jnp.float32).reshape(block_count, block_len, head_count, DH)
    position = jnp.arange(block_len)
    lower_mask = (position[None, :] <= position[:, None]).astype(jnp.float32)
    strict_mask = (position[:, None] < position[None, :]).astype(jnp.float32)

    def block_step(carried, block):
        keys_gram, query_value, pair_state = carried
        query_float, key_float, value_float = block
        scores = jnp.einsum('thd,ihd->hti', query_float, key_float, precision=highest)
        paired = jnp.swapaxes(scores, 1, 2) * strict_mask
        inner_pairs = jnp.einsum('hti,hij->htj', scores, paired, precision=highest)
        query_state = jnp.einsum('thd,hde->hte', query_float, keys_gram, precision=highest)
        cross_terms = jnp.einsum('hte,jhe->htj', query_state, query_float, precision=highest)
        mixing = (inner_pairs + cross_terms) * lower_mask
        result = jnp.einsum('htj,jhd->thd', mixing, value_float, precision=highest)
        result = result + jnp.einsum('thd,hde->the', query_float, pair_state, precision=highest)
        gram_block = jnp.einsum('thd,the->hde', key_float, key_float, precision=highest)
        cross_block = jnp.einsum('thd,the->hde', query_float, value_float, precision=highest)
        paired_values = jnp.einsum('hij,jhe->hie', paired, value_float, precision=highest)
        pair_block = jnp.einsum('ihd,hie->hde', key_float, paired_values, precision=highest)
        pair_next = pair_state + pair_block + jnp.einsum('hde,hef->hdf', keys_gram, cross_block, precision=highest)
        return ((keys_gram + gram_block, query_value + cross_block, pair_next), result)
    zero_state = jnp.zeros((head_count, DH, DH), jnp.float32)
    unused, results = lax.scan(block_step, (zero_state, zero_state, zero_state), (blocked(queries), blocked(key_vectors), blocked(value_vectors)))
    return results.reshape(token_rows, head_count, DH)

def reference(queries, key_vectors, value_vectors, norm_gain, out_weight):
    attended = attend_all(queries, key_vectors, value_vectors)
    head_count = attended.shape[1]
    mean_square = lax.optimization_barrier(jnp.mean(attended * attended, axis=-1, keepdims=True))
    normed = attended * lax.rsqrt(mean_square + 1e-06) * norm_gain.reshape(head_count, DH)
    normed = normed.astype(jnp.bfloat16).reshape(attended.shape[0], head_count * DH)
    return jnp.dot(normed, out_weight, preferred_element_type=jnp.float32).astype(jnp.bfloat16)
```

```python
import functools

import jax
import jax.numpy as jnp
from jax import lax
from jax.experimental import pallas as pl
from jax.experimental.pallas import tpu as pltpu
from jax.sharding import Mesh
from jax.sharding import PartitionSpec as P

DH = 128
SEQ = ("seq_0", "seq_1", "seq_2")
SEQ_HEAD = ("seq_0", "seq_1", "seq_2", "head")
F32 = jnp.float32
BF16 = jnp.bfloat16
CHUNK = 256
EPS = 1e-06

X_PIECES = ((-1, 0), (1, 1), (-1, 1), (1, 0), (2, 0), (2, 1))


def dot(a, b, ca, cb):
    return lax.dot_general(a, b, (((ca,), (cb,)), ((), ())), preferred_element_type=F32)


def kernel(
    ny,
    nz,
    nx,
    q_hbm,
    k_hbm,
    v_hbm,
    gain_ref,
    w_hbm,
    out_ref,
    q,
    k,
    v,
    w,
    s_first,
    s_out,
    s_in,
    s_back,
    s_pre,
    p_out,
    p_in,
    p_back,
    p_pre,
    running,
    y_out,
    y_in,
    f_loc,
    p_loc,
    c_loc,
    p_first,
    o_part,
    p_fin,
    n_out,
    n_in,
    acc,
    load_sem,
    z_send,
    z_recv,
    y_send,
    y_recv,
    n_send,
    n_recv,
    w_send,
    w_recv,
):
    tokens, width = q.shape
    heads = width // DH
    group = 2 * nz
    per_head = group // heads if group >= heads else 0
    y, z, c, x = (lax.axis_index(name) for name in SEQ_HEAD)
    me = z * 2 + c

    def modx(i):
        return lax.rem(x + i + nx, nx)

    def mody(i):
        return lax.rem(y + i + ny, ny)

    barrier = pltpu.get_barrier_semaphore()

    def greet_group(d, carry):
        peer = lax.rem(me + d, group)
        pl.semaphore_signal(
            barrier, inc=1, device_id={"seq_1": peer // 2, "seq_2": lax.rem(peer, 2)}, device_id_type=pl.DeviceIdType.MESH
        )
        return carry

    lax.fori_loop(1, group, greet_group, 0)
    for d in range(1, ny):
        pl.semaphore_signal(barrier, inc=1, device_id={"seq_0": mody(d)}, device_id_type=pl.DeviceIdType.MESH)
    for d in range(1, nx):
        pl.semaphore_signal(barrier, inc=1, device_id={"head": modx(d)}, device_id_type=pl.DeviceIdType.MESH)

    loads = [
        pltpu.make_async_copy(src, dst, load_sem.at[i])
        for i, (src, dst) in enumerate(((k_hbm, k), (q_hbm, q), (v_hbm, v), (w_hbm, w.at[x])))
    ]
    for copy in loads:
        copy.start()

    def chunk(ref, h, j):
        return ref[j * CHUNK : (j + 1) * CHUNK, h * DH : (h + 1) * DH]

    def head_state(ref, h):
        rows = ref.shape[1]
        n = DH // rows
        return ref[h * n : (h + 1) * n].reshape(DH, DH)

    def set_head_state(ref, h, value):
        rows = ref.shape[1]
        n = DH // rows
        ref[h * n : (h + 1) * n] = value.reshape(n, rows, DH).astype(ref.dtype)

    def exchange(phase, src, dst, peer, slot):
        return pltpu.make_async_remote_copy(
            src_ref=src.at[peer],
            dst_ref=dst.at[slot],
            send_sem=z_send.at[phase, peer],
            recv_sem=z_recv.at[phase, slot],
            device_id={"seq_1": peer // 2, "seq_2": lax.rem(peer, 2)},
            device_id_type=pl.DeviceIdType.MESH,
        )

    def exchange_start(phase, src, dst):
        def step(d, carry):
            exchange(phase, src, dst, lax.rem(me + d, group), me).start()
            return carry

        lax.fori_loop(1, group, step, 0)
        dst[me] = src[me]

    def exchange_wait(phase, src, dst):
        def step(d, carry):
            peer = lax.rem(me + d, group)
            exchange(phase, src, dst, peer, peer).wait_recv()
            return carry

        lax.fori_loop(1, group, step, 0)

    def exchange_drain(phase, src, dst):
        def step(d, carry):
            peer = lax.rem(me + d, group)
            exchange(phase, src, dst, peer, peer).wait_send()
            return carry

        lax.fori_loop(1, group, step, 0)

    def total_copy(which, d, slot):
        return pltpu.make_async_remote_copy(
            src_ref=y_out.at[which],
            dst_ref=y_in.at[which, slot],
            send_sem=y_send.at[which, d],
            recv_sem=y_recv.at[which, slot],
            device_id={"seq_0": mody(d)},
            device_id_type=pl.DeviceIdType.MESH,
        )

    def scan_totals(which, arrived):
        total = jnp.zeros(arrived.shape[1:], F32)
        for r in range(group):
            running[r] = total
            total = total + arrived[r].astype(F32)
        y_out[which] = total.astype(BF16)
        for d in range(1, ny):
            total_copy(which, d, y).start()

    def scan_finish(which, prefixes):
        base = jnp.zeros(running.shape[1:], F32)
        for d in range(1, ny):
            other = mody(d)
            total_copy(which, d, other).wait_recv()
            base = base + jnp.where(other < y, y_in[which, other].astype(F32), 0.0)
        for r in range(group):
            prefixes[r] = (running[r] + base).astype(BF16)

    colour = lax.rem(y, 2)
    piece_rows = w.shape[1] // 8

    def piece(i, colour_of, core_of):
        offset, half = X_PIECES[i]
        start = colour_of * (4 * piece_rows) + core_of * (2 * piece_rows) + half * piece_rows
        return w.at[modx(offset), pl.ds(pl.multiple_of(start, piece_rows), piece_rows)]

    def w_copy(number, src, dst, device_id):
        return pltpu.make_async_remote_copy(
            src_ref=src,
            dst_ref=dst,
            send_sem=w_send.at[number],
            recv_sem=w_recv.at[number],
            device_id=device_id,
            device_id_type=pl.DeviceIdType.MESH,
        )

    def own_piece(half):
        start = colour * (4 * piece_rows) + c * (2 * piece_rows) + half * piece_rows
        rows = pl.ds(pl.multiple_of(start, piece_rows), piece_rows)
        return w_hbm.at[rows], w.at[x, rows]

    def x_send(number):
        offset, half = X_PIECES[number]
        if number < 4:
            src, dst = own_piece(half)
            return w_copy(number, src, dst, {"head": modx(-offset)})
        src = piece(0 if number == 4 else 1, colour, c)
        return w_copy(number, src, src, {"head": modx(1 if number == 4 else -1)})

    def x_arrival(number):
        ref = piece(number, colour, c)
        return w_copy(number, ref, ref, {"head": modx(1)})

    def core_send(number):
        ref = piece(number, colour, c)
        return w_copy(6 + number, ref, ref, {"seq_2": 1 - c})

    def core_arrival(number):
        ref = piece(number, colour, 1 - c)
        return w_copy(6 + number, ref, ref, {"seq_2": 1 - c})

    def y_step(number):
        return 1 if X_PIECES[number][1] == 0 else -1

    def y_piece_send(number):
        ref = piece(number, colour, c)
        return w_copy(12 + number, ref, ref, {"seq_0": mody(y_step(number))})

    def y_piece_arrival(number):
        ref = piece(number, 1 - colour, c)
        return w_copy(12 + number, ref, ref, {"seq_0": mody(y_step(number))})

    def core2_send(number):
        ref = piece(number, 1 - colour, c)
        return w_copy(18 + number, ref, ref, {"seq_2": 1 - c})

    def core2_arrival(number):
        ref = piece(number, 1 - colour, 1 - c)
        return w_copy(18 + number, ref, ref, {"seq_2": 1 - c})

    def relay_x(numbers):
        for number in numbers:
            x_arrival(number).wait_recv()
            if number < 2:
                x_send(4 + number).start()
            y_piece_send(number).start()
            core_send(number).start()

    def relay_y(numbers):
        for number in numbers:
            y_piece_arrival(number).wait_recv()
            core2_send(number).start()

    loads[0].wait()
    for h in range(heads):
        first = dot(chunk(k, h, 0), chunk(k, h, 0), 0, 0)
        s_first[h] = first.astype(BF16)
        set_head_state(s_out, h, first + dot(chunk(k, h, 1), chunk(k, h, 1), 0, 0))

    pl.semaphore_wait(barrier, group - 1 + ny - 1 + nx - 1)
    exchange_start(0, s_out, s_in)
    for number in range(4):
        x_send(number).start()
    loads[1].wait()
    loads[2].wait()

    row = lax.broadcasted_iota(jnp.int32, (CHUNK, CHUNK), 0)
    col = lax.broadcasted_iota(jnp.int32, (CHUNK, CHUNK), 1)

    def local_pairs(h):
        pair = jnp.zeros((DH, DH), F32)
        cross = jnp.zeros((DH, DH), F32)
        for j in range(2):
            qc, kc, vc = chunk(q, h, j), chunk(k, h, j), chunk(v, h, j)
            scores = jnp.where(col < row, dot(qc, kc, 1, 1), 0.0).astype(BF16)
            f = dot(scores, kc, 1, 0)
            if j == 1:
                f = f + dot(qc, s_first[h], 1, 0)
            f_loc[j * CHUNK : (j + 1) * CHUNK, h * DH : (h + 1) * DH] = f
            pair = pair + dot(f.astype(BF16), vc, 0, 0)
            cross = cross + dot(qc, vc, 0, 0)
        p_loc[h] = pair
        c_loc[h] = cross.astype(BF16)

    def local_out(h):
        s_h = head_state(s_pre, h)
        for j in range(2):
            qc, vc = chunk(q, h, j), chunk(v, h, j)
            f = (chunk(f_loc, h, j) + dot(qc, s_h, 1, 0)).astype(BF16)
            mixing = jnp.where(col <= row, dot(qc, f, 1, 1), 0.0).astype(BF16)
            o_part[j * CHUNK : (j + 1) * CHUNK, h * DH : (h + 1) * DH] = dot(mixing, vc, 1, 0)
            if j == 0:
                p_first[h] = dot(f, vc, 0, 0)

    for h in range(heads):
        local_pairs(h)

    exchange_wait(0, s_out, s_in)
    scan_totals(0, s_in)
    scan_finish(0, s_back)
    exchange_start(1, s_back, s_pre)
    exchange_wait(1, s_back, s_pre)

    for h in range(heads):
        set_head_state(p_out, h, p_loc[h] + dot(head_state(s_pre, h), c_loc[h], 1, 0))
    exchange_start(2, p_out, p_in)
    relay_x((0, 1))
    for h in range(heads // 2):
        local_out(h)
    exchange_wait(2, p_out, p_in)
    scan_totals(1, p_in)
    scan_finish(1, p_back)
    exchange_start(3, p_back, p_pre)
    relay_x((2, 3))
    relay_y((0, 1))
    for h in range(heads // 2, heads):
        local_out(h)
    exchange_wait(3, p_back, p_pre)
    for h in range(heads):
        p_h = head_state(p_pre, h)
        p_fin[0, h] = p_h
        p_fin[1, h] = (p_h.astype(F32) + p_first[h]).astype(BF16)

    rows_x = tokens // nx

    def n_copy(d, slot):
        return pltpu.make_async_remote_copy(
            src_ref=n_out.at[d],
            dst_ref=n_in.at[slot],
            send_sem=n_send.at[d],
            recv_sem=n_recv.at[slot],
            device_id={"head": modx(d)},
            device_id_type=pl.DeviceIdType.MESH,
        )

    for d in (2, 1, 3, 0):
        target = modx(d)
        rows = pl.ds(pl.multiple_of(target * rows_x, rows_x), rows_x)
        part = target // (CHUNK // rows_x)
        for h in range(heads):
            cols = slice(h * DH, (h + 1) * DH)
            attended = o_part[rows, cols] + dot(q[rows, cols], p_fin[part, h], 1, 0)
            mean_square = jnp.mean(attended * attended, axis=-1, keepdims=True)
            n_out[d, :, cols] = (attended * lax.rsqrt(mean_square + EPS) * gain_ref[:, cols]).astype(BF16)
        if d:
            n_copy(d, x).start()
    relay_x((4, 5))
    relay_y((2, 3))

    loads[3].wait()
    tile = 512
    n_cols = out_ref.shape[1]

    def project(rows_in, quarter, first, last):
        for start in range(0, n_cols, tile):
            cols = slice(start, start + tile)
            part = dot(rows_in, w[quarter, :, cols], 1, 0)
            if not first:
                part = part + acc[:, cols]
            if last:
                out_ref[:, cols] = part.astype(BF16)
            else:
                acc[:, cols] = part

    project(n_out[0], x, True, False)
    relay_y((4, 5))
    for offset in (-1, 1, 2):
        quarter = modx(offset)
        for number, (of, half) in enumerate(X_PIECES):
            if of == offset:
                core_arrival(number).wait_recv()
                core2_arrival(number).wait_recv()
        n_copy(offset % nx, quarter).wait_recv()
        project(n_in[quarter], quarter, False, offset == 2)

    exchange_drain(0, s_out, s_in)
    exchange_drain(1, s_back, s_pre)
    exchange_drain(2, p_out, p_in)
    exchange_drain(3, p_back, p_pre)
    for which in range(2):
        for d in range(1, ny):
            total_copy(which, d, y).wait_send()
    for d in range(1, nx):
        n_copy(d, x).wait_send()
    for number in range(6):
        x_send(number).wait_send()
        core_send(number).wait_send()
        y_piece_send(number).wait_send()
        core2_send(number).wait_send()


def shards(ny, nz, nx, queries, key_vectors, value_vectors, norm_gain, out_weight):
    tokens, width = queries.shape
    heads = width // DH
    depth, n_cols = out_weight.shape
    group = 2 * nz
    rows = heads * DH // group
    state = pltpu.VMEM((group, rows, DH), BF16)
    matrices = (heads, DH, DH)
    any_spec = pl.BlockSpec(memory_space=pl.ANY)
    vmem_spec = pl.BlockSpec(memory_space=pltpu.VMEM)
    return pl.pallas_call(
        functools.partial(kernel, ny, nz, nx),
        out_shape=jax.ShapeDtypeStruct((tokens // nx, n_cols), BF16),
        in_specs=[any_spec, any_spec, any_spec, vmem_spec, any_spec],
        out_specs=vmem_spec,
        scratch_shapes=[
            pltpu.VMEM((tokens, width), BF16),
            pltpu.VMEM((tokens, width), BF16),
            pltpu.VMEM((tokens, width), BF16),
            pltpu.VMEM((nx, depth, n_cols), BF16),
            pltpu.VMEM(matrices, BF16),
            state,
            state,
            state,
            state,
            state,
            state,
            state,
            state,
            pltpu.VMEM((group, rows, DH), F32),
            pltpu.VMEM((2, rows, DH), BF16),
            pltpu.VMEM((2, ny, rows, DH), BF16),
            pltpu.VMEM((tokens, width), F32),
            pltpu.VMEM(matrices, F32),
            pltpu.VMEM(matrices, BF16),
            pltpu.VMEM(matrices, F32),
            pltpu.VMEM((tokens, width), F32),
            pltpu.VMEM((2,) + matrices, BF16),
            pltpu.VMEM((nx, tokens // nx, width), BF16),
            pltpu.VMEM((nx, tokens // nx, width), BF16),
            pltpu.VMEM((tokens // nx, n_cols), F32),
            pltpu.SemaphoreType.DMA((4,)),
            pltpu.SemaphoreType.DMA((4, group)),
            pltpu.SemaphoreType.DMA((4, group)),
            pltpu.SemaphoreType.DMA((2, ny)),
            pltpu.SemaphoreType.DMA((2, ny)),
            pltpu.SemaphoreType.DMA((nx,)),
            pltpu.SemaphoreType.DMA((nx,)),
            pltpu.SemaphoreType.DMA((24,)),
            pltpu.SemaphoreType.DMA((24,)),
        ],
        compiler_params=pltpu.CompilerParams(
            collective_id=0, has_side_effects=True, vmem_limit_bytes=48 * 1024 * 1024
        ),
    )(queries, key_vectors, value_vectors, norm_gain.reshape(1, width), out_weight)


def solution(mesh):
    seq, nx = mesh.shape["seq"], mesh.shape["head"]
    ny = 4 if seq == 64 else 2
    nz = seq // (2 * ny)
    split = Mesh(mesh.devices.reshape(ny, nz, 2, nx), SEQ_HEAD)
    in_specs = (P(SEQ, "head"), P(SEQ, "head"), P(SEQ, "head"), P("head"), P("head", None))
    out_specs = P(SEQ_HEAD, None)
    return jax.shard_map(
        functools.partial(shards, ny, nz, nx), mesh=split, in_specs=in_specs, out_specs=out_specs, check_vma=False
    )
```

```python
import functools

import jax
import jax.numpy as jnp
from jax import lax
from jax.experimental import pallas as pl
from jax.experimental.pallas import tpu as pltpu
from jax.sharding import Mesh
from jax.sharding import PartitionSpec as P

DH = 128
SEQ = ("seq_0", "seq_1", "seq_2")
SEQ_HEAD = ("seq_0", "seq_1", "seq_2", "head")
F32 = jnp.float32
BF16 = jnp.bfloat16
CHUNK = 256
EPS = 1e-06
FAR_FIRST = (4, 3, 5, 2, 6, 1, 7)

X_PIECES = ((-1, 0), (1, 1), (-1, 1), (1, 0), (2, 0), (2, 1))


def dot(a, b, ca, cb):
    return lax.dot_general(a, b, (((ca,), (cb,)), ((), ())), preferred_element_type=F32)


def kernel(
    ny,
    nz,
    nx,
    q_hbm,
    k_hbm,
    v_hbm,
    gain_hbm,
    w_hbm,
    out_ref,
    q,
    k,
    v,
    w,
    gain,
    s_first,
    s_loc,
    cp_loc,
    s_sib,
    cp_sib,
    s_chip,
    cp_chip,
    s_arr,
    cp_arr,
    running,
    s_back,
    p_back,
    y_out,
    y_in,
    s_pre,
    p_pre,
    p_step,
    s_other,
    p_other,
    s_mine,
    p_mine,
    f_loc,
    p_first,
    o_part,
    p_fin,
    n_out,
    n_in,
    acc,
    load_sem,
    core_send,
    core_recv,
    in_send,
    in_recv,
    back_send,
    back_recv,
    y_send,
    y_recv,
    n_send,
    n_recv,
    w_send,
    w_recv,
):
    tokens, width = q.shape
    heads = width // DH
    pair = heads // 2
    y, z, c, x = (lax.axis_index(name) for name in SEQ_HEAD)

    def modx(i):
        return lax.rem(x + i + nx, nx)

    def mody(i):
        return lax.rem(y + i + ny, ny)

    def modz(i):
        return lax.rem(z + i, nz)

    pending = []

    def remote(src, dst, send_sem, recv_sem, device_id):
        return pltpu.make_async_remote_copy(
            src_ref=src,
            dst_ref=dst,
            send_sem=send_sem,
            recv_sem=recv_sem,
            device_id=device_id,
            device_id_type=pl.DeviceIdType.MESH,
        )

    def start(copy):
        copy.start()
        pending.append(copy.wait_send)

    barrier = pltpu.get_barrier_semaphore()
    greeted = [{"seq_1": modz(d)} for d in range(1, nz)] + [{"seq_2": 1 - c}]
    greeted += [{"seq_0": mody(d)} for d in range(1, ny)] + [{"head": modx(d)} for d in range(1, nx)]
    for peer in greeted:
        pl.semaphore_signal(barrier, inc=1, device_id=peer, device_id_type=pl.DeviceIdType.MESH)

    loads = [
        pltpu.make_async_copy(src, dst, load_sem.at[i])
        for i, (src, dst) in enumerate(((k_hbm, k), (q_hbm, q), (v_hbm, v), (w_hbm, w.at[x]), (gain_hbm, gain)))
    ]
    for copy in loads:
        copy.start()

    def chunk(ref, h, j):
        return ref[j * CHUNK : (j + 1) * CHUNK, h * DH : (h + 1) * DH]

    spacing = nz // heads
    is_worker = (lax.rem(z, spacing) == 0) & (z // (spacing * pair) == c)
    my_head = lax.rem(z // spacing, pair)

    def worker_z(i):
        return (c * pair + i) * spacing

    def in_copy(kind, i, slot, device_id):
        src, dst = ((s_chip, s_arr), (cp_chip, cp_arr))[kind]
        return remote(src.at[i], dst.at[slot], in_send.at[kind, i], in_recv.at[kind, slot], device_id)

    def send_in(kind):
        for i in range(pair):
            here = z == worker_z(i)
            copy = in_copy(kind, i, z, {"seq_1": worker_z(i)})

            @pl.when(jnp.logical_not(here))
            def _(copy=copy):
                copy.start()

            @pl.when(here)
            def _(i=i):
                src, dst = ((s_chip, s_arr), (cp_chip, cp_arr))[kind]
                dst[z] = src[i]

    def drain_in(kind):
        for i in range(pair):
            @pl.when(z != worker_z(i))
            def _(i=i):
                in_copy(kind, i, z, {"seq_1": worker_z(i)}).wait_send()

    def wait_in(kind):
        for d in range(1, nz):
            in_copy(kind, 0, modz(d), {"seq_1": modz(d)}).wait_recv()

    def back_copy(kind, i, d):
        src, dst = ((s_back, s_pre), (p_back, p_pre))[kind]
        return remote(src.at[modz(d)], dst.at[i], back_send.at[kind, d], back_recv.at[kind, i], {"seq_1": modz(d)})

    def send_back(kind):
        src, dst = ((s_back, s_pre), (p_back, p_pre))[kind]
        for d in FAR_FIRST:
            if d < nz:
                back_copy(kind, my_head, d).start()
        dst[my_head] = src[z]

    def wait_back(kind):
        for i in range(pair):
            @pl.when(z != worker_z(i))
            def _(i=i):
                back_copy(kind, i, 1).wait_recv()

    def total_copy(kind, d, slot):
        return remote(
            y_out.at[kind], y_in.at[kind, slot], y_send.at[kind, d], y_recv.at[kind, slot], {"seq_0": mody(d)}
        )

    def send_total(kind, total):
        y_out[kind] = total.astype(BF16)
        for d in range(1, ny):
            total_copy(kind, d, y).start()

    def wait_totals(kind):
        base = jnp.zeros((DH, DH), F32)
        for d in range(1, ny):
            other = mody(d)
            total_copy(kind, d, other).wait_recv()
            base = base + jnp.where(other < y, y_in[kind, other].astype(F32), 0.0)
        return base

    colour = lax.rem(y, 2)
    piece_rows = w.shape[1] // 8

    def rows_of(colour_of, core_of, half):
        first = colour_of * (4 * piece_rows) + core_of * (2 * piece_rows) + half * piece_rows
        return pl.ds(pl.multiple_of(first, piece_rows), piece_rows)

    def piece(i, colour_of, core_of):
        offset, half = X_PIECES[i]
        return w.at[modx(offset), rows_of(colour_of, core_of, half)]

    def w_copy(number, src, dst, device_id):
        return remote(src, dst, w_send.at[number], w_recv.at[number], device_id)

    def x_send(number):
        offset, half = X_PIECES[number]
        if number < 4:
            rows = rows_of(colour, c, half)
            return w_copy(number, w_hbm.at[rows], w.at[x, rows], {"head": modx(-offset)})
        src = piece(number - 4, colour, c)
        return w_copy(number, src, src, {"head": modx(1 if number == 4 else -1)})

    def x_arrival(number):
        ref = piece(number, colour, c)
        return w_copy(number, ref, ref, {"head": modx(1)})

    def core_copy(number, core_of):
        ref = piece(number, colour, core_of)
        return w_copy(6 + number, ref, ref, {"seq_2": 1 - c})

    def y_copy(number, colour_of):
        ref = piece(number, colour_of, c)
        return w_copy(12 + number, ref, ref, {"seq_0": mody(1 if X_PIECES[number][1] == 0 else -1)})

    def core_y_copy(number, core_of):
        ref = piece(number, 1 - colour, core_of)
        return w_copy(18 + number, ref, ref, {"seq_2": 1 - c})

    def relay_x(numbers):
        for number in numbers:
            x_arrival(number).wait_recv()
            if number < 2:
                start(x_send(4 + number))
            start(y_copy(number, colour))
            start(core_copy(number, c))

    def relay_y(numbers):
        for number in numbers:
            y_copy(number, 1 - colour).wait_recv()
            start(core_y_copy(number, c))

    row = lax.broadcasted_iota(jnp.int32, (CHUNK, CHUNK), 0)
    col = lax.broadcasted_iota(jnp.int32, (CHUNK, CHUNK), 1)
    loads[0].wait()
    for h in range(heads):
        first = dot(chunk(k, h, 0), chunk(k, h, 0), 0, 0)
        s_first[h] = first.astype(BF16)
        s_loc[h // pair, h % pair] = (first + dot(chunk(k, h, 1), chunk(k, h, 1), 0, 0)).astype(BF16)
    loads[1].wait()
    loads[2].wait()
    for h in range(heads):
        pairs = jnp.zeros((DH, DH), F32)
        cross = jnp.zeros((DH, DH), F32)
        for j in range(2):
            qc, kc, vc = chunk(q, h, j), chunk(k, h, j), chunk(v, h, j)
            scores = jnp.where(col < row, dot(qc, kc, 1, 1), 0.0).astype(BF16)
            f = dot(scores, kc, 1, 0)
            if j == 1:
                f = f + dot(qc, s_first[h], 1, 0)
            f_loc[j * CHUNK : (j + 1) * CHUNK, h * DH : (h + 1) * DH] = f
            pairs = pairs + dot(f.astype(BF16), vc, 0, 0)
            cross = cross + dot(qc, vc, 0, 0)
        cp_loc[h // pair, h % pair, 0] = cross.astype(BF16)
        cp_loc[h // pair, h % pair, 1] = pairs.astype(BF16)

    pl.semaphore_wait(barrier, len(greeted))
    sibling = {"seq_2": 1 - c}
    s_core = remote(s_loc.at[1 - c], s_sib, core_send.at[0], core_recv.at[0], sibling)
    cp_core = remote(cp_loc.at[1 - c], cp_sib, core_send.at[1], core_recv.at[1], sibling)
    start(s_core)
    start(cp_core)
    for number in range(4):
        start(x_send(number))
    s_core.wait_recv()
    for i in range(pair):
        s_chip[i] = (s_loc[c, i].astype(F32) + s_sib[i].astype(F32)).astype(BF16)
    send_in(0)
    cp_core.wait_recv()
    for i in range(pair):
        mine, other = cp_loc[c, i], cp_sib[i]
        early = jnp.where(c == 0, s_loc[c, i], s_sib[i])
        late = jnp.where(c == 0, other[0], mine[0])
        cp_chip[i, 0] = (mine[0].astype(F32) + other[0].astype(F32)).astype(BF16)
        cp_chip[i, 1] = (mine[1].astype(F32) + other[1].astype(F32) + dot(early, late, 1, 0)).astype(BF16)
    send_in(1)

    @pl.when(is_worker)
    def _():
        wait_in(0)
        total = jnp.zeros((DH, DH), F32)
        for r in range(nz):
            running[r] = total
            total = total + s_arr[r].astype(F32)
        send_total(0, total)

    relay_x((0, 1))

    @pl.when(is_worker)
    def _():
        base = wait_totals(0)
        for r in range(nz):
            s_back[r] = (running[r] + base).astype(BF16)
        send_back(0)
        wait_in(1)
        total = jnp.zeros((DH, DH), F32)
        for r in range(nz):
            running[r] = total
            total = total + cp_arr[r, 1].astype(F32) + dot(s_back[r], cp_arr[r, 0], 1, 0)
        send_total(1, total)

    relay_x((2, 3))
    relay_y((0, 1))

    @pl.when(is_worker)
    def _():
        base = wait_totals(1)
        for r in range(nz):
            p_back[r] = (running[r] + base).astype(BF16)
        send_back(1)

    wait_back(0)
    for i in range(pair):
        mine, other = cp_loc[c, i], cp_sib[i]
        chip = s_pre[i]
        early = jnp.where(c == 0, s_loc[c, i], s_sib[i])
        later = (chip.astype(F32) + early.astype(F32)).astype(BF16)
        s_mine[c, i] = jnp.where(c == 0, chip, later)
        s_other[i] = jnp.where(c == 0, later, chip)
        p_step[i] = jnp.where(c == 0, mine[1], other[1]).astype(F32) + dot(
            chip, jnp.where(c == 0, mine[0], other[0]), 1, 0
        )
    s_swap = remote(s_other, s_mine.at[c], core_send.at[2], core_recv.at[2], sibling)
    start(s_swap)
    s_swap_in = remote(s_other, s_mine.at[1 - c], core_send.at[2], core_recv.at[2], sibling)
    s_swap_in.wait_recv()

    for h in range(heads):
        s_h = s_mine[h // pair, h % pair]
        for j in range(2):
            qc, vc = chunk(q, h, j), chunk(v, h, j)
            f = (chunk(f_loc, h, j) + dot(qc, s_h, 1, 0)).astype(BF16)
            mixing = jnp.where(col <= row, dot(qc, f, 1, 1), 0.0).astype(BF16)
            o_part[j * CHUNK : (j + 1) * CHUNK, h * DH : (h + 1) * DH] = dot(mixing, vc, 1, 0)
            if j == 0:
                p_first[h] = dot(f, vc, 0, 0)

    wait_back(1)
    for i in range(pair):
        chip = p_pre[i]
        later = (chip.astype(F32) + p_step[i]).astype(BF16)
        p_mine[c, i] = jnp.where(c == 0, chip, later)
        p_other[i] = jnp.where(c == 0, later, chip)
    p_swap = remote(p_other, p_mine.at[c], core_send.at[3], core_recv.at[3], sibling)
    start(p_swap)
    p_swap_in = remote(p_other, p_mine.at[1 - c], core_send.at[3], core_recv.at[3], sibling)
    p_swap_in.wait_recv()
    for h in range(heads):
        p_h = p_mine[h // pair, h % pair]
        p_fin[0, h] = p_h
        p_fin[1, h] = (p_h.astype(F32) + p_first[h]).astype(BF16)

    rows_x = tokens // nx
    loads[4].wait()

    def n_copy(d, slot):
        return remote(n_out.at[d], n_in.at[slot], n_send.at[d], n_recv.at[slot], {"head": modx(d)})

    for d in (2, 1, 3, 0):
        target = modx(d)
        rows = pl.ds(pl.multiple_of(target * rows_x, rows_x), rows_x)
        part = target // (CHUNK // rows_x)
        for h in range(heads):
            cols = slice(h * DH, (h + 1) * DH)
            attended = o_part[rows, cols] + dot(q[rows, cols], p_fin[part, h], 1, 0)
            mean_square = jnp.mean(attended * attended, axis=-1, keepdims=True)
            n_out[d, :, cols] = (attended * lax.rsqrt(mean_square + EPS) * gain[:, cols]).astype(BF16)
        if d:
            start(n_copy(d, x))
    relay_x((4, 5))
    relay_y((2, 3))

    loads[3].wait()
    tile = 512
    n_cols = out_ref.shape[1]

    def project(rows_in, quarter, first, last):
        for begin in range(0, n_cols, tile):
            cols = slice(begin, begin + tile)
            part = dot(rows_in, w[quarter, :, cols], 1, 0)
            if not first:
                part = part + acc[:, cols]
            if last:
                out_ref[:, cols] = part.astype(BF16)
            else:
                acc[:, cols] = part

    project(n_out[0], x, True, False)
    relay_y((4, 5))
    for offset in (-1, 1, 2):
        quarter = modx(offset)
        for number, (of, half) in enumerate(X_PIECES):
            if of == offset:
                core_copy(number, 1 - c).wait_recv()
                core_y_copy(number, 1 - c).wait_recv()
        n_copy(offset % nx, quarter).wait_recv()
        project(n_in[quarter], quarter, False, offset == 2)

    for wait in pending:
        wait()
    drain_in(0)
    drain_in(1)

    @pl.when(is_worker)
    def _():
        for kind in range(2):
            for d in range(1, nz):
                back_copy(kind, my_head, d).wait_send()
            for d in range(1, ny):
                total_copy(kind, d, y).wait_send()


def shards(ny, nz, nx, queries, key_vectors, value_vectors, norm_gain, out_weight):
    tokens, width = queries.shape
    heads = width // DH
    pair = heads // 2
    depth, n_cols = out_weight.shape

    def matrices(*lead, kind=BF16):
        return pltpu.VMEM(lead + (DH, DH), kind)

    return pl.pallas_call(
        functools.partial(kernel, ny, nz, nx),
        out_shape=jax.ShapeDtypeStruct((tokens // nx, n_cols), BF16),
        in_specs=[pl.BlockSpec(memory_space=pltpu.HBM)] * 5,
        out_specs=pl.BlockSpec(memory_space=pltpu.VMEM),
        scratch_shapes=[
            pltpu.VMEM((tokens, width), BF16),
            pltpu.VMEM((tokens, width), BF16),
            pltpu.VMEM((tokens, width), BF16),
            pltpu.VMEM((nx, depth, n_cols), BF16),
            pltpu.VMEM((1, width), F32),
            matrices(heads),
            matrices(2, pair),
            matrices(2, pair, 2),
            matrices(pair),
            matrices(pair, 2),
            matrices(pair),
            matrices(pair, 2),
            matrices(nz),
            matrices(nz, 2),
            matrices(nz, kind=F32),
            matrices(nz),
            matrices(nz),
            matrices(2),
            matrices(2, ny),
            matrices(pair),
            matrices(pair),
            matrices(pair, kind=F32),
            matrices(pair),
            matrices(pair),
            matrices(2, pair),
            matrices(2, pair),
            pltpu.VMEM((tokens, width), F32),
            matrices(heads, kind=F32),
            pltpu.VMEM((tokens, width), F32),
            matrices(2, heads),
            pltpu.VMEM((nx, tokens // nx, width), BF16),
            pltpu.VMEM((nx, tokens // nx, width), BF16),
            pltpu.VMEM((tokens // nx, n_cols), F32),
            pltpu.SemaphoreType.DMA((5,)),
            pltpu.SemaphoreType.DMA((4,)),
            pltpu.SemaphoreType.DMA((4,)),
            pltpu.SemaphoreType.DMA((2, pair)),
            pltpu.SemaphoreType.DMA((2, nz)),
            pltpu.SemaphoreType.DMA((2, nz)),
            pltpu.SemaphoreType.DMA((2, pair)),
            pltpu.SemaphoreType.DMA((2, ny)),
            pltpu.SemaphoreType.DMA((2, ny)),
            pltpu.SemaphoreType.DMA((nx,)),
            pltpu.SemaphoreType.DMA((nx,)),
            pltpu.SemaphoreType.DMA((24,)),
            pltpu.SemaphoreType.DMA((24,)),
        ],
        compiler_params=pltpu.CompilerParams(
            collective_id=0, has_side_effects=True, vmem_limit_bytes=63 * 1024 * 1024
        ),
    )(queries, key_vectors, value_vectors, norm_gain.reshape(1, width), out_weight)


def solution(mesh):
    seq, nx = mesh.shape["seq"], mesh.shape["head"]
    ny = 4 if seq == 64 else 2
    nz = seq // (2 * ny)
    split = Mesh(mesh.devices.reshape(ny, nz, 2, nx), SEQ_HEAD)
    in_specs = (P(SEQ, "head"), P(SEQ, "head"), P(SEQ, "head"), P("head"), P("head", None))
    out_specs = P(SEQ_HEAD, None)
    return jax.shard_map(
        functools.partial(shards, ny, nz, nx), mesh=split, in_specs=in_specs, out_specs=out_specs, check_vma=False
    )
```

```python
import functools

import jax
import jax.numpy as jnp
from jax import lax
from jax.experimental import pallas as pl
from jax.experimental.pallas import tpu as pltpu
from jax.sharding import Mesh
from jax.sharding import PartitionSpec as P

DH = 128
SEQ = ("seq_0", "seq_1", "seq_2")
SEQ_HEAD = ("seq_0", "seq_1", "seq_2", "head")
F32 = jnp.float32
BF16 = jnp.bfloat16
CHUNK = 256
EPS = 1e-06
FAR_FIRST = (4, 3, 5, 2, 6, 1, 7)

X_PIECES = ((-1, 0), (1, 1), (-1, 1), (1, 0), (2, 0), (2, 1))


def dot(a, b, ca, cb):
    return lax.dot_general(a, b, (((ca,), (cb,)), ((), ())), preferred_element_type=F32)


def kernel(
    ny,
    nz,
    nx,
    q_hbm,
    k_hbm,
    v_hbm,
    gain_hbm,
    w_hbm,
    out_ref,
    q,
    k,
    v,
    w,
    gain,
    s_first,
    s_loc,
    cp_loc,
    s_sib,
    cp_sib,
    s_chip,
    cp_chip,
    s_arr,
    cp_arr,
    running,
    s_back,
    p_back,
    y_out,
    y_in,
    s_pre,
    p_pre,
    p_step,
    s_other,
    p_other,
    s_mine,
    p_mine,
    v_t,
    f_loc,
    p_first,
    o_part,
    p_fin,
    n_out,
    n_in,
    acc,
    load_sem,
    core_send,
    core_recv,
    in_send,
    in_recv,
    back_send,
    back_recv,
    y_send,
    y_recv,
    n_send,
    n_recv,
    w_send,
    w_recv,
):
    tokens, width = q.shape
    heads = width // DH
    pair = heads // 2
    y, z, c, x = (lax.axis_index(name) for name in SEQ_HEAD)

    def modx(i):
        return lax.rem(x + i + nx, nx)

    def mody(i):
        return lax.rem(y + i + ny, ny)

    def modz(i):
        return lax.rem(z + i, nz)

    pending = []

    def remote(src, dst, send_sem, recv_sem, device_id):
        return pltpu.make_async_remote_copy(
            src_ref=src,
            dst_ref=dst,
            send_sem=send_sem,
            recv_sem=recv_sem,
            device_id=device_id,
            device_id_type=pl.DeviceIdType.MESH,
        )

    def start(copy):
        copy.start()
        pending.append(copy.wait_send)

    barrier = pltpu.get_barrier_semaphore()
    greeted = [{"seq_1": modz(d)} for d in range(1, nz)] + [{"seq_2": 1 - c}]
    greeted += [{"seq_0": mody(d)} for d in range(1, ny)] + [{"head": modx(d)} for d in range(1, nx)]
    for peer in greeted:
        pl.semaphore_signal(barrier, inc=1, device_id=peer, device_id_type=pl.DeviceIdType.MESH)

    loads = [
        pltpu.make_async_copy(src, dst, load_sem.at[i])
        for i, (src, dst) in enumerate(((k_hbm, k), (q_hbm, q), (v_hbm, v), (w_hbm, w.at[x]), (gain_hbm, gain)))
    ]
    for copy in loads:
        copy.start()

    def chunk(ref, h, j):
        return ref[j * CHUNK : (j + 1) * CHUNK, h * DH : (h + 1) * DH]

    spacing = nz // heads
    is_worker = (lax.rem(z, spacing) == 0) & (z // (spacing * pair) == c)
    my_head = lax.rem(z // spacing, pair)

    def worker_z(i):
        return (c * pair + i) * spacing

    def in_copy(kind, i, slot, device_id):
        src, dst = ((s_chip, s_arr), (cp_chip, cp_arr))[kind]
        return remote(src.at[i], dst.at[slot], in_send.at[kind, i], in_recv.at[kind, slot], device_id)

    def send_in(kind):
        for i in range(pair):
            here = z == worker_z(i)
            copy = in_copy(kind, i, z, {"seq_1": worker_z(i)})

            @pl.when(jnp.logical_not(here))
            def _(copy=copy):
                copy.start()

            @pl.when(here)
            def _(i=i):
                src, dst = ((s_chip, s_arr), (cp_chip, cp_arr))[kind]
                dst[z] = src[i]

    def drain_in(kind):
        for i in range(pair):
            @pl.when(z != worker_z(i))
            def _(i=i):
                in_copy(kind, i, z, {"seq_1": worker_z(i)}).wait_send()

    def wait_in(kind):
        for d in range(1, nz):
            in_copy(kind, 0, modz(d), {"seq_1": modz(d)}).wait_recv()

    def back_copy(kind, i, d):
        src, dst = ((s_back, s_pre), (p_back, p_pre))[kind]
        return remote(src.at[modz(d)], dst.at[i], back_send.at[kind, d], back_recv.at[kind, i], {"seq_1": modz(d)})

    def send_back(kind):
        src, dst = ((s_back, s_pre), (p_back, p_pre))[kind]
        for d in FAR_FIRST:
            if d < nz:
                back_copy(kind, my_head, d).start()
        dst[my_head] = src[z]

    def wait_back(kind):
        for i in range(pair):
            @pl.when(z != worker_z(i))
            def _(i=i):
                back_copy(kind, i, 1).wait_recv()

    def total_copy(kind, d, slot):
        return remote(
            y_out.at[kind], y_in.at[kind, slot], y_send.at[kind, d], y_recv.at[kind, slot], {"seq_0": mody(d)}
        )

    def send_total(kind, total):
        y_out[kind] = total.astype(BF16)
        for d in (2, 1, 3):
            if d < ny:
                total_copy(kind, d, y).start()

    def wait_totals(kind):
        base = jnp.zeros((DH, DH), F32)
        for d in range(1, ny):
            other = mody(d)
            total_copy(kind, d, other).wait_recv()
            base = base + jnp.where(other < y, y_in[kind, other].astype(F32), 0.0)
        return base

    colour = lax.rem(y, 2)
    piece_rows = w.shape[1] // 8

    def rows_of(colour_of, core_of, half):
        first = colour_of * (4 * piece_rows) + core_of * (2 * piece_rows) + half * piece_rows
        return pl.ds(pl.multiple_of(first, piece_rows), piece_rows)

    def piece(i, colour_of, core_of):
        offset, half = X_PIECES[i]
        return w.at[modx(offset), rows_of(colour_of, core_of, half)]

    def w_copy(number, src, dst, device_id):
        return remote(src, dst, w_send.at[number], w_recv.at[number], device_id)

    def x_send(number):
        offset, half = X_PIECES[number]
        if number < 4:
            rows = rows_of(colour, c, half)
            return w_copy(number, w_hbm.at[rows], w.at[x, rows], {"head": modx(-offset)})
        src = piece(number - 4, colour, c)
        return w_copy(number, src, src, {"head": modx(1 if number == 4 else -1)})

    def x_arrival(number):
        ref = piece(number, colour, c)
        return w_copy(number, ref, ref, {"head": modx(1)})

    def core_copy(number, core_of):
        ref = piece(number, colour, core_of)
        return w_copy(6 + number, ref, ref, {"seq_2": 1 - c})

    def y_copy(number, colour_of):
        ref = piece(number, colour_of, c)
        return w_copy(12 + number, ref, ref, {"seq_0": mody(1 if X_PIECES[number][1] == 0 else -1)})

    def core_y_copy(number, core_of):
        ref = piece(number, 1 - colour, core_of)
        return w_copy(18 + number, ref, ref, {"seq_2": 1 - c})

    def relay_x(numbers):
        for number in numbers:
            x_arrival(number).wait_recv()
            if number < 2:
                start(x_send(4 + number))
            start(y_copy(number, colour))
            start(core_copy(number, c))

    def relay_y(numbers):
        for number in numbers:
            y_copy(number, 1 - colour).wait_recv()
            start(core_y_copy(number, c))

    row = lax.broadcasted_iota(jnp.int32, (CHUNK, CHUNK), 0)
    col = lax.broadcasted_iota(jnp.int32, (CHUNK, CHUNK), 1)
    loads[0].wait()
    for h in range(heads):
        first = dot(chunk(k, h, 0), chunk(k, h, 0), 0, 0)
        s_first[h] = first.astype(BF16)
        s_loc[h // pair, h % pair] = (first + dot(chunk(k, h, 1), chunk(k, h, 1), 0, 0)).astype(BF16)
    loads[1].wait()
    loads[2].wait()
    strict, causal = col < row, col <= row
    blocks = [(h, j) for h in range(heads) for j in range(2)]
    for h in range(heads):
        v_t[h] = v[:, h * DH : (h + 1) * DH].T
    scores = [jnp.where(strict, dot(chunk(q, h, j), chunk(k, h, j), 1, 1), 0.0).astype(BF16) for h, j in blocks]
    fs = []
    for n, (h, j) in enumerate(blocks):
        f = dot(scores[n], chunk(k, h, j), 1, 0)
        if j == 1:
            f = f + dot(chunk(q, h, j), s_first[h], 1, 0)
        f_loc[j * CHUNK : (j + 1) * CHUNK, h * DH : (h + 1) * DH] = f
        fs.append(f.astype(BF16))
    for h in range(heads):
        cross = dot(v_t[h], q[:, h * DH : (h + 1) * DH], 1, 0)
        pairs = dot(v_t[h, :, :CHUNK], fs[2 * h], 1, 0) + dot(v_t[h, :, CHUNK:], fs[2 * h + 1], 1, 0)
        cp_loc[h // pair, h % pair, 0] = cross.astype(BF16)
        cp_loc[h // pair, h % pair, 1] = pairs.astype(BF16)

    pl.semaphore_wait(barrier, len(greeted))
    sibling = {"seq_2": 1 - c}
    s_core = remote(s_loc.at[1 - c], s_sib, core_send.at[0], core_recv.at[0], sibling)
    cp_core = remote(cp_loc.at[1 - c], cp_sib, core_send.at[1], core_recv.at[1], sibling)
    start(s_core)
    start(cp_core)
    for number in range(4):
        start(x_send(number))
    s_core.wait_recv()
    for i in range(pair):
        s_chip[i] = (s_loc[c, i].astype(F32) + s_sib[i].astype(F32)).astype(BF16)
    send_in(0)
    cp_core.wait_recv()
    for i in range(pair):
        mine, other = cp_loc[c, i], cp_sib[i]
        early = jnp.where(c == 0, s_loc[c, i], s_sib[i])
        late = jnp.where(c == 0, other[0], mine[0])
        cp_chip[i, 0] = (mine[0].astype(F32) + other[0].astype(F32)).astype(BF16)
        cp_chip[i, 1] = (mine[1].astype(F32) + other[1].astype(F32) + dot(late, early, 1, 0)).astype(BF16)
    send_in(1)

    @pl.when(is_worker)
    def _():
        wait_in(0)
        total = jnp.zeros((DH, DH), F32)
        for r in range(nz):
            running[r] = total
            total = total + s_arr[r].astype(F32)
        send_total(0, total)

    relay_x((0, 1))

    @pl.when(is_worker)
    def _():
        base = wait_totals(0)
        for r in range(nz):
            s_back[r] = (running[r] + base).astype(BF16)
        send_back(0)
        wait_in(1)
        total = jnp.zeros((DH, DH), F32)
        for r in range(nz):
            running[r] = total
            total = total + cp_arr[r, 1].astype(F32) + dot(cp_arr[r, 0], s_back[r], 1, 0)
        send_total(1, total)

    relay_x((2, 3))
    relay_y((0, 1))

    @pl.when(is_worker)
    def _():
        base = wait_totals(1)
        for r in range(nz):
            p_back[r] = (running[r] + base).astype(BF16)
        send_back(1)

    wait_back(0)
    for i in range(pair):
        mine, other = cp_loc[c, i], cp_sib[i]
        chip = s_pre[i]
        early = jnp.where(c == 0, s_loc[c, i], s_sib[i])
        later = (chip.astype(F32) + early.astype(F32)).astype(BF16)
        s_mine[c, i] = jnp.where(c == 0, chip, later)
        s_other[i] = jnp.where(c == 0, later, chip)
        p_step[i] = jnp.where(c == 0, mine[1], other[1]).astype(F32) + dot(
            jnp.where(c == 0, mine[0], other[0]), chip, 1, 0
        )
    s_swap = remote(s_other, s_mine.at[c], core_send.at[2], core_recv.at[2], sibling)
    start(s_swap)
    relay_x((4, 5))
    s_swap_in = remote(s_other, s_mine.at[1 - c], core_send.at[2], core_recv.at[2], sibling)
    s_swap_in.wait_recv()

    fs = []
    for h, j in blocks:
        f = chunk(f_loc, h, j) + dot(chunk(q, h, j), s_mine[h // pair, h % pair], 1, 0)
        fs.append(f.astype(BF16))
    mixing = [
        jnp.where(causal, dot(chunk(q, h, j), fs[n], 1, 1), 0.0).astype(BF16) for n, (h, j) in enumerate(blocks)
    ]
    for n, (h, j) in enumerate(blocks):
        o_part[j * CHUNK : (j + 1) * CHUNK, h * DH : (h + 1) * DH] = dot(mixing[n], chunk(v, h, j), 1, 0)
    for h in range(heads):
        p_first[h // pair, h % pair] = dot(v_t[h, :, :CHUNK], fs[2 * h], 1, 0)
    relay_y((2, 3))

    wait_back(1)
    for i in range(pair):
        chip = p_pre[i]
        later = (chip.astype(F32) + p_step[i]).astype(BF16)
        p_mine[c, i] = jnp.where(c == 0, chip, later)
        p_other[i] = jnp.where(c == 0, later, chip)
    p_swap = remote(p_other, p_mine.at[c], core_send.at[3], core_recv.at[3], sibling)
    start(p_swap)
    p_swap_in = remote(p_other, p_mine.at[1 - c], core_send.at[3], core_recv.at[3], sibling)

    rows_x = tokens // nx
    loads[4].wait()

    def n_copy(d, g, slot):
        return remote(n_out.at[d, g], n_in.at[slot, g], n_send.at[d, g], n_recv.at[slot, g], {"head": modx(d)})

    for step in range(2):
        g = c if step == 0 else 1 - c
        if step == 1:
            p_swap_in.wait_recv()
        for i in range(pair):
            p_h = p_mine[g, i]
            p_fin[0, i] = p_h
            p_fin[1, i] = (p_h.astype(F32) + p_first[g, i]).astype(BF16)
        for d in (2, 1, 3, 0):
            target = modx(d)
            rows = pl.ds(pl.multiple_of(target * rows_x, rows_x), rows_x)
            part = target // (CHUNK // rows_x)
            for i in range(pair):
                cols = pl.ds(pl.multiple_of(g * (pair * DH) + i * DH, DH), DH)
                attended = o_part[rows, cols] + dot(q[rows, cols], p_fin[part, i], 1, 1)
                mean_square = jnp.mean(attended * attended, axis=-1, keepdims=True)
                n_out[d, g, :, i * DH : (i + 1) * DH] = (
                    attended * lax.rsqrt(mean_square + EPS) * gain[:, cols]
                ).astype(BF16)
            if d:
                start(n_copy(d, g, x))

    loads[3].wait()
    tile = 512
    n_cols = out_ref.shape[1]

    half = w.shape[1] // 2

    def project(rows_in, slot, quarter, first, last):
        for begin in range(0, n_cols, tile):
            cols = slice(begin, begin + tile)
            part = dot(rows_in[slot, 0], w[quarter, :half, cols], 1, 0)
            part = part + dot(rows_in[slot, 1], w[quarter, half:, cols], 1, 0)
            if not first:
                part = part + acc[:, cols]
            if last:
                out_ref[:, cols] = part.astype(BF16)
            else:
                acc[:, cols] = part

    project(n_out, 0, x, True, False)
    relay_y((4, 5))
    for offset in (-1, 1, 2):
        quarter = modx(offset)
        for number, (of, _) in enumerate(X_PIECES):
            if of == offset:
                core_copy(number, 1 - c).wait_recv()
                core_y_copy(number, 1 - c).wait_recv()
        for g in range(2):
            n_copy(offset % nx, g, quarter).wait_recv()
        project(n_in, quarter, quarter, False, offset == 2)

    for wait in pending:
        wait()
    drain_in(0)
    drain_in(1)

    @pl.when(is_worker)
    def _():
        for kind in range(2):
            for d in range(1, nz):
                back_copy(kind, my_head, d).wait_send()
            for d in range(1, ny):
                total_copy(kind, d, y).wait_send()


def shards(ny, nz, nx, queries, key_vectors, value_vectors, norm_gain, out_weight):
    tokens, width = queries.shape
    heads = width // DH
    pair = heads // 2
    depth, n_cols = out_weight.shape

    def matrices(*lead, kind=BF16):
        return pltpu.VMEM(lead + (DH, DH), kind)

    operands = (queries, key_vectors, value_vectors, norm_gain.reshape(1, width), out_weight)
    return pl.pallas_call(
        functools.partial(kernel, ny, nz, nx),
        out_shape=jax.ShapeDtypeStruct((tokens // nx, n_cols), BF16),
        in_specs=[pl.BlockSpec(memory_space=pltpu.HBM)] * 5,
        out_specs=pl.BlockSpec(memory_space=pltpu.VMEM),
        scratch_shapes=[
            pltpu.VMEM((tokens, width), BF16),
            pltpu.VMEM((tokens, width), BF16),
            pltpu.VMEM((tokens, width), BF16),
            pltpu.VMEM((nx, depth, n_cols), BF16),
            pltpu.VMEM((1, width), F32),
            matrices(heads),
            matrices(2, pair),
            matrices(2, pair, 2),
            matrices(pair),
            matrices(pair, 2),
            matrices(pair),
            matrices(pair, 2),
            matrices(nz),
            matrices(nz, 2),
            matrices(nz, kind=F32),
            matrices(nz),
            matrices(nz),
            matrices(2),
            matrices(2, ny),
            matrices(pair),
            matrices(pair),
            matrices(pair, kind=F32),
            matrices(pair),
            matrices(pair),
            matrices(2, pair),
            matrices(2, pair),
            pltpu.VMEM((heads, DH, tokens), BF16),
            pltpu.VMEM((tokens, width), F32),
            matrices(2, pair, kind=F32),
            pltpu.VMEM((tokens, width), F32),
            matrices(2, pair),
            pltpu.VMEM((nx, 2, tokens // nx, width // 2), BF16),
            pltpu.VMEM((nx, 2, tokens // nx, width // 2), BF16),
            pltpu.VMEM((tokens // nx, n_cols), F32),
            pltpu.SemaphoreType.DMA((5,)),
            pltpu.SemaphoreType.DMA((4,)),
            pltpu.SemaphoreType.DMA((4,)),
            pltpu.SemaphoreType.DMA((2, pair)),
            pltpu.SemaphoreType.DMA((2, nz)),
            pltpu.SemaphoreType.DMA((2, nz)),
            pltpu.SemaphoreType.DMA((2, pair)),
            pltpu.SemaphoreType.DMA((2, ny)),
            pltpu.SemaphoreType.DMA((2, ny)),
            pltpu.SemaphoreType.DMA((nx, 2)),
            pltpu.SemaphoreType.DMA((nx, 2)),
            pltpu.SemaphoreType.DMA((24,)),
            pltpu.SemaphoreType.DMA((24,)),
        ],
        compiler_params=pltpu.CompilerParams(
            collective_id=0, has_side_effects=True, vmem_limit_bytes=48 * 1024 * 1024
        ),
    )(*[pltpu.with_memory_space_constraint(array, pltpu.HBM) for array in operands])


def solution(mesh):
    seq, nx = mesh.shape["seq"], mesh.shape["head"]
    ny = 4 if seq == 64 else 2
    nz = seq // (2 * ny)
    split = Mesh(mesh.devices.reshape(ny, nz, 2, nx), SEQ_HEAD)
    in_specs = (P(SEQ, "head"), P(SEQ, "head"), P(SEQ, "head"), P("head"), P("head", None))
    out_specs = P(SEQ_HEAD, None)
    return jax.shard_map(
        functools.partial(shards, ny, nz, nx), mesh=split, in_specs=in_specs, out_specs=out_specs, check_vma=False
    )
```

```python
import functools

import jax
import jax.numpy as jnp
from jax import lax
from jax.experimental import pallas as pl
from jax.experimental.pallas import tpu as pltpu
from jax.sharding import Mesh
from jax.sharding import PartitionSpec as P

DH = 128
SEQ = ("seq_0", "seq_1", "seq_2")
SEQ_HEAD = ("seq_0", "seq_1", "seq_2", "head")
F32 = jnp.float32
BF16 = jnp.bfloat16
CHUNK = 256
EPS = 1e-06
FAR_FIRST = (4, 3, 5, 2, 6, 1, 7)

X_PIECES = ((-1, 0), (1, 1), (-1, 1), (1, 0), (2, 0), (2, 1))


def dot(a, b, ca, cb):
    return lax.dot_general(a, b, (((ca,), (cb,)), ((), ())), preferred_element_type=F32)


def kernel(
    ny,
    nz,
    nx,
    q_hbm,
    k_hbm,
    v_hbm,
    gain_hbm,
    w_hbm,
    out_ref,
    q,
    k,
    v,
    w,
    gain,
    s_first,
    s_loc,
    cp_loc,
    s_sib,
    cp_sib,
    s_chip,
    cp_chip,
    s_arr,
    cp_arr,
    s_run,
    p_run,
    c_run,
    s_back,
    p_back,
    y_out,
    y_in,
    s_pre,
    p_pre,
    p_step,
    s_other,
    p_other,
    s_mine,
    p_mine,
    v_t,
    f_loc,
    p_first,
    o_part,
    p_fin,
    n_out,
    n_in,
    acc,
    load_sem,
    core_send,
    core_recv,
    in_send,
    in_recv,
    back_send,
    back_recv,
    y_send,
    y_recv,
    n_send,
    n_recv,
    w_send,
    w_recv,
):
    tokens, width = q.shape
    heads = width // DH
    pair = heads // 2
    y, z, c, x = (lax.axis_index(name) for name in SEQ_HEAD)

    def modx(i):
        return lax.rem(x + i + nx, nx)

    def mody(i):
        return lax.rem(y + i + ny, ny)

    def modz(i):
        return lax.rem(z + i, nz)

    pending = []

    def remote(src, dst, send_sem, recv_sem, device_id):
        return pltpu.make_async_remote_copy(
            src_ref=src,
            dst_ref=dst,
            send_sem=send_sem,
            recv_sem=recv_sem,
            device_id=device_id,
            device_id_type=pl.DeviceIdType.MESH,
        )

    def start(copy):
        copy.start()
        pending.append(copy.wait_send)

    spacing = nz // heads
    is_worker = (lax.rem(z, spacing) == 0) & (z // (spacing * pair) == c)
    my_head = lax.rem(z // spacing, pair)

    barrier = pltpu.get_barrier_semaphore()

    def greet(peer):
        pl.semaphore_signal(barrier, inc=1, device_id=peer, device_id_type=pl.DeviceIdType.MESH)

    for d in range(1, ny):
        greet({"seq_0": mody(d)})
    for d in range(1, nx):
        greet({"head": modx(d)})
    greet({"seq_2": 1 - c})

    @pl.when(is_worker)
    def _():
        for d in FAR_FIRST:
            if d < nz:
                greet({"seq_1": modz(d)})

    loads = [
        pltpu.make_async_copy(src, dst, load_sem.at[i])
        for i, (src, dst) in enumerate(((k_hbm, k), (q_hbm, q), (v_hbm, v), (w_hbm, w.at[x]), (gain_hbm, gain)))
    ]
    for copy in loads:
        copy.start()

    def chunk(ref, h, j):
        return ref[j * CHUNK : (j + 1) * CHUNK, h * DH : (h + 1) * DH]

    def worker_z(i):
        return (c * pair + i) * spacing

    def in_copy(kind, i, slot, device_id):
        src, dst = ((s_chip, s_arr), (cp_chip, cp_arr))[kind]
        return remote(src.at[i], dst.at[slot], in_send.at[kind, i], in_recv.at[kind, slot], device_id)

    def distance(i):
        ahead = lax.rem(worker_z(i) - z + nz, nz)
        return jnp.minimum(ahead, nz - ahead)

    farther = jnp.where(distance(0) < distance(pair - 1), pair - 1, 0)

    def send_in(kind):
        for n in range(pair):
            i = lax.rem(farther + n, pair)
            here = z == worker_z(i)
            copy = in_copy(kind, i, z, {"seq_1": worker_z(i)})

            @pl.when(jnp.logical_not(here))
            def _(copy=copy):
                copy.start()

            @pl.when(here)
            def _(i=i):
                src, dst = ((s_chip, s_arr), (cp_chip, cp_arr))[kind]
                dst[z] = src[i]

    def drain_in(kind):
        for i in range(pair):
            @pl.when(z != worker_z(i))
            def _(i=i):
                in_copy(kind, i, z, {"seq_1": worker_z(i)}).wait_send()

    def wait_in(kind):
        for d in range(1, nz):
            in_copy(kind, 0, modz(d), {"seq_1": modz(d)}).wait_recv()

    def back_copy(kind, i, d):
        src, dst = ((s_back, s_pre), (p_back, p_pre))[kind]
        return remote(src.at[modz(d)], dst.at[i], back_send.at[kind, d], back_recv.at[kind, i], {"seq_1": modz(d)})

    def send_back(kind):
        src, dst = ((s_back, s_pre), (p_back, p_pre))[kind]
        for d in FAR_FIRST:
            if d < nz:
                back_copy(kind, my_head, d).start()
        dst[my_head] = src[z]

    def wait_back(kind):
        for i in range(pair):
            @pl.when(z != worker_z(i))
            def _(i=i):
                back_copy(kind, i, 1).wait_recv()

    def total_copy(kind, d, slot):
        part = (pl.ds(0, 1), pl.ds(1, 2))[kind]
        return remote(
            y_out.at[part], y_in.at[slot, part], y_send.at[kind, d], y_recv.at[kind, slot], {"seq_0": mody(d)}
        )

    def send_totals(kind):
        for d in (2, 1, 3):
            if d < ny:
                total_copy(kind, d, y).start()

    def wait_totals(kind):
        for d in range(1, ny):
            total_copy(kind, d, mody(d)).wait_recv()

    def s_base_until(limit):
        base = jnp.zeros((DH, DH), F32)
        for r in range(ny - 1):
            base = base + jnp.where(r < limit, y_in[r, 0].astype(F32), 0.0)
        return base

    colour = lax.rem(y, 2)
    piece_rows = w.shape[1] // 8

    def rows_of(colour_of, core_of, half):
        first = colour_of * (4 * piece_rows) + core_of * (2 * piece_rows) + half * piece_rows
        return pl.ds(pl.multiple_of(first, piece_rows), piece_rows)

    def piece(i, colour_of, core_of):
        offset, half = X_PIECES[i]
        return w.at[modx(offset), rows_of(colour_of, core_of, half)]

    def w_copy(number, src, dst, device_id):
        return remote(src, dst, w_send.at[number], w_recv.at[number], device_id)

    def x_send(number):
        offset, half = X_PIECES[number]
        if number < 4:
            rows = rows_of(colour, c, half)
            return w_copy(number, w_hbm.at[rows], w.at[x, rows], {"head": modx(-offset)})
        src = piece(number - 4, colour, c)
        return w_copy(number, src, src, {"head": modx(1 if number == 4 else -1)})

    def x_arrival(number):
        ref = piece(number, colour, c)
        return w_copy(number, ref, ref, {"head": modx(1)})

    def core_copy(number, core_of):
        ref = piece(number, colour, core_of)
        return w_copy(6 + number, ref, ref, {"seq_2": 1 - c})

    def y_copy(number, colour_of):
        ref = piece(number, colour_of, c)
        return w_copy(12 + number, ref, ref, {"seq_0": mody(1 if X_PIECES[number][1] == 0 else -1)})

    def core_y_copy(number, core_of):
        ref = piece(number, 1 - colour, core_of)
        return w_copy(18 + number, ref, ref, {"seq_2": 1 - c})

    def relay_x(numbers):
        for number in numbers:
            x_arrival(number).wait_recv()
            if number < 2:
                start(x_send(4 + number))
            start(y_copy(number, colour))
            start(core_copy(number, c))

    def relay_y(numbers):
        for number in numbers:
            y_copy(number, 1 - colour).wait_recv()
            start(core_y_copy(number, c))

    row = lax.broadcasted_iota(jnp.int32, (CHUNK, CHUNK), 0)
    col = lax.broadcasted_iota(jnp.int32, (CHUNK, CHUNK), 1)
    loads[0].wait()
    for h in range(heads):
        first = dot(chunk(k, h, 0), chunk(k, h, 0), 0, 0)
        s_first[h] = first.astype(BF16)
        s_loc[h // pair, h % pair] = (first + dot(chunk(k, h, 1), chunk(k, h, 1), 0, 0)).astype(BF16)
    loads[1].wait()
    loads[2].wait()
    strict, causal = col < row, col <= row
    blocks = [(h, j) for h in range(heads) for j in range(2)]
    for h in range(heads):
        v_t[h] = v[:, h * DH : (h + 1) * DH].T
    scores = [jnp.where(strict, dot(chunk(q, h, j), chunk(k, h, j), 1, 1), 0.0).astype(BF16) for h, j in blocks]
    fs = []
    for n, (h, j) in enumerate(blocks):
        f = dot(scores[n], chunk(k, h, j), 1, 0)
        if j == 1:
            f = f + dot(chunk(q, h, j), s_first[h], 1, 0)
        f_loc[j * CHUNK : (j + 1) * CHUNK, h * DH : (h + 1) * DH] = f
        fs.append(f.astype(BF16))
    for h in range(heads):
        cross = dot(v_t[h], q[:, h * DH : (h + 1) * DH], 1, 0)
        pairs = dot(v_t[h, :, :CHUNK], fs[2 * h], 1, 0) + dot(v_t[h, :, CHUNK:], fs[2 * h + 1], 1, 0)
        cp_loc[h // pair, h % pair, 0] = cross.astype(BF16)
        cp_loc[h // pair, h % pair, 1] = pairs.astype(BF16)

    pl.semaphore_wait(barrier, nx - 1 + ny - 1 + 1 + pair - is_worker.astype(jnp.int32))
    sibling = {"seq_2": 1 - c}
    s_core = remote(s_loc.at[1 - c], s_sib, core_send.at[0], core_recv.at[0], sibling)
    cp_core = remote(cp_loc.at[1 - c], cp_sib, core_send.at[1], core_recv.at[1], sibling)
    start(s_core)
    start(cp_core)
    for number in range(4):
        start(x_send(number))
    s_core.wait_recv()
    for i in range(pair):
        s_chip[i] = (s_loc[c, i].astype(F32) + s_sib[i].astype(F32)).astype(BF16)
    send_in(0)
    cp_core.wait_recv()
    for i in range(pair):
        mine, other = cp_loc[c, i], cp_sib[i]
        early = jnp.where(c == 0, s_loc[c, i], s_sib[i])
        late = jnp.where(c == 0, other[0], mine[0])
        cp_chip[i, 0] = (mine[0].astype(F32) + other[0].astype(F32)).astype(BF16)
        cp_chip[i, 1] = (mine[1].astype(F32) + other[1].astype(F32) + dot(late, early, 1, 0)).astype(BF16)
    send_in(1)

    @pl.when(is_worker)
    def _():
        wait_in(0)
        total = jnp.zeros((DH, DH), F32)
        for r in range(nz):
            s_run[r] = total
            total = total + s_arr[r].astype(F32)
        y_out[0] = total.astype(BF16)
        send_totals(0)
        y_in[y, 0] = total.astype(BF16)

    relay_x((0, 1))

    @pl.when(is_worker)
    def _():
        wait_in(1)
        pairs = jnp.zeros((DH, DH), F32)
        cross = jnp.zeros((DH, DH), F32)
        for r in range(nz):
            p_run[r] = pairs
            c_run[r] = cross.astype(BF16)
            pairs = pairs + (cp_arr[r, 1].astype(F32) + dot(cp_arr[r, 0], s_run[r].astype(BF16), 1, 0))
            cross = cross + cp_arr[r, 0].astype(F32)
        y_out[1] = cross.astype(BF16)
        y_out[2] = pairs.astype(BF16)
        send_totals(1)
        y_in[y, 1] = cross.astype(BF16)
        y_in[y, 2] = pairs.astype(BF16)
        wait_totals(0)
        s_base = s_base_until(y)
        for r in range(nz):
            s_back[r] = (s_run[r] + s_base).astype(BF16)
        send_back(0)
        s_base = s_base.astype(BF16)
        for r in range(nz):
            p_run[r] = p_run[r] + dot(c_run[r], s_base, 1, 0)
        before = [s_base_until(r).astype(BF16) for r in range(ny - 1)]
        wait_totals(1)
        p_base = jnp.zeros((DH, DH), F32)
        for r in range(ny - 1):
            line = y_in[r, 2].astype(F32) + dot(y_in[r, 1], before[r], 1, 0)
            p_base = p_base + jnp.where(r < y, line, 0.0)
        for r in range(nz):
            p_back[r] = (p_run[r] + p_base).astype(BF16)
        send_back(1)

    relay_x((2, 3))
    relay_y((0, 1))

    wait_back(0)
    for i in range(pair):
        mine, other = cp_loc[c, i], cp_sib[i]
        chip = s_pre[i]
        early = jnp.where(c == 0, s_loc[c, i], s_sib[i])
        later = (chip.astype(F32) + early.astype(F32)).astype(BF16)
        s_mine[c, i] = jnp.where(c == 0, chip, later)
        s_other[i] = jnp.where(c == 0, later, chip)
        p_step[i] = jnp.where(c == 0, mine[1], other[1]).astype(F32) + dot(
            jnp.where(c == 0, mine[0], other[0]), chip, 1, 0
        )
    s_swap = remote(s_other, s_mine.at[c], core_send.at[2], core_recv.at[2], sibling)
    start(s_swap)
    relay_x((4, 5))
    s_swap_in = remote(s_other, s_mine.at[1 - c], core_send.at[2], core_recv.at[2], sibling)
    s_swap_in.wait_recv()

    fs = []
    for h, j in blocks:
        f = chunk(f_loc, h, j) + dot(chunk(q, h, j), s_mine[h // pair, h % pair], 1, 0)
        fs.append(f.astype(BF16))
    mixing = [
        jnp.where(causal, dot(chunk(q, h, j), fs[n], 1, 1), 0.0).astype(BF16) for n, (h, j) in enumerate(blocks)
    ]
    for n, (h, j) in enumerate(blocks):
        o_part[j * CHUNK : (j + 1) * CHUNK, h * DH : (h + 1) * DH] = dot(mixing[n], chunk(v, h, j), 1, 0)
    for h in range(heads):
        p_first[h // pair, h % pair] = dot(v_t[h, :, :CHUNK], fs[2 * h], 1, 0)
    relay_y((2, 3))

    wait_back(1)
    for i in range(pair):
        chip = p_pre[i]
        later = (chip.astype(F32) + p_step[i]).astype(BF16)
        p_mine[c, i] = jnp.where(c == 0, chip, later)
        p_other[i] = jnp.where(c == 0, later, chip)
    p_swap = remote(p_other, p_mine.at[c], core_send.at[3], core_recv.at[3], sibling)
    start(p_swap)
    p_swap_in = remote(p_other, p_mine.at[1 - c], core_send.at[3], core_recv.at[3], sibling)

    rows_x = tokens // nx
    loads[4].wait()

    def n_copy(d, g, slot):
        return remote(n_out.at[d, g], n_in.at[slot, g], n_send.at[d, g], n_recv.at[slot, g], {"head": modx(d)})

    for step in range(2):
        g = c if step == 0 else 1 - c
        if step == 1:
            p_swap_in.wait_recv()
        for i in range(pair):
            p_h = p_mine[g, i]
            p_fin[0, i] = p_h
            p_fin[1, i] = (p_h.astype(F32) + p_first[g, i]).astype(BF16)
        for d in (2, 1, 3, 0):
            target = modx(d)
            rows = pl.ds(pl.multiple_of(target * rows_x, rows_x), rows_x)
            part = target // (CHUNK // rows_x)
            for i in range(pair):
                cols = pl.ds(pl.multiple_of(g * (pair * DH) + i * DH, DH), DH)
                attended = o_part[rows, cols] + dot(q[rows, cols], p_fin[part, i], 1, 1)
                mean_square = jnp.mean(attended * attended, axis=-1, keepdims=True)
                n_out[d, g, :, i * DH : (i + 1) * DH] = (
                    attended * lax.rsqrt(mean_square + EPS) * gain[:, cols]
                ).astype(BF16)
            if d:
                start(n_copy(d, g, x))

    loads[3].wait()
    tile = 512
    n_cols = out_ref.shape[1]

    half = w.shape[1] // 2

    def project(rows_in, slot, quarter, first, last):
        for begin in range(0, n_cols, tile):
            cols = slice(begin, begin + tile)
            part = dot(rows_in[slot, 0], w[quarter, :half, cols], 1, 0)
            part = part + dot(rows_in[slot, 1], w[quarter, half:, cols], 1, 0)
            if not first:
                part = part + acc[:, cols]
            if last:
                out_ref[:, cols] = part.astype(BF16)
            else:
                acc[:, cols] = part

    project(n_out, 0, x, True, False)
    relay_y((4, 5))
    for offset in (-1, 1, 2):
        quarter = modx(offset)
        for number, (of, _) in enumerate(X_PIECES):
            if of == offset:
                core_copy(number, 1 - c).wait_recv()
                core_y_copy(number, 1 - c).wait_recv()
        for g in range(2):
            n_copy(offset % nx, g, quarter).wait_recv()
        project(n_in, quarter, quarter, False, offset == 2)

    for wait in pending:
        wait()
    drain_in(0)
    drain_in(1)

    @pl.when(is_worker)
    def _():
        for kind in range(2):
            for d in range(1, nz):
                back_copy(kind, my_head, d).wait_send()
            for d in range(1, ny):
                total_copy(kind, d, y).wait_send()


def shards(ny, nz, nx, queries, key_vectors, value_vectors, norm_gain, out_weight):
    tokens, width = queries.shape
    heads = width // DH
    pair = heads // 2
    depth, n_cols = out_weight.shape

    def matrices(*lead, kind=BF16):
        return pltpu.VMEM(lead + (DH, DH), kind)

    operands = (queries, key_vectors, value_vectors, norm_gain.reshape(1, width), out_weight)
    return pl.pallas_call(
        functools.partial(kernel, ny, nz, nx),
        out_shape=jax.ShapeDtypeStruct((tokens // nx, n_cols), BF16),
        in_specs=[pl.BlockSpec(memory_space=pltpu.HBM)] * 5,
        out_specs=pl.BlockSpec(memory_space=pltpu.VMEM),
        scratch_shapes=[
            pltpu.VMEM((tokens, width), BF16),
            pltpu.VMEM((tokens, width), BF16),
            pltpu.VMEM((tokens, width), BF16),
            pltpu.VMEM((nx, depth, n_cols), BF16),
            pltpu.VMEM((1, width), F32),
            matrices(heads),
            matrices(2, pair),
            matrices(2, pair, 2),
            matrices(pair),
            matrices(pair, 2),
            matrices(pair),
            matrices(pair, 2),
            matrices(nz),
            matrices(nz, 2),
            matrices(nz, kind=F32),
            matrices(nz, kind=F32),
            matrices(nz),
            matrices(nz),
            matrices(nz),
            matrices(3),
            matrices(ny, 3),
            matrices(pair),
            matrices(pair),
            matrices(pair, kind=F32),
            matrices(pair),
            matrices(pair),
            matrices(2, pair),
            matrices(2, pair),
            pltpu.VMEM((heads, DH, tokens), BF16),
            pltpu.VMEM((tokens, width), F32),
            matrices(2, pair, kind=F32),
            pltpu.VMEM((tokens, width), F32),
            matrices(2, pair),
            pltpu.VMEM((nx, 2, tokens // nx, width // 2), BF16),
            pltpu.VMEM((nx, 2, tokens // nx, width // 2), BF16),
            pltpu.VMEM((tokens // nx, n_cols), F32),
            pltpu.SemaphoreType.DMA((5,)),
            pltpu.SemaphoreType.DMA((4,)),
            pltpu.SemaphoreType.DMA((4,)),
            pltpu.SemaphoreType.DMA((2, pair)),
            pltpu.SemaphoreType.DMA((2, nz)),
            pltpu.SemaphoreType.DMA((2, nz)),
            pltpu.SemaphoreType.DMA((2, pair)),
            pltpu.SemaphoreType.DMA((2, ny)),
            pltpu.SemaphoreType.DMA((2, ny)),
            pltpu.SemaphoreType.DMA((nx, 2)),
            pltpu.SemaphoreType.DMA((nx, 2)),
            pltpu.SemaphoreType.DMA((24,)),
            pltpu.SemaphoreType.DMA((24,)),
        ],
        compiler_params=pltpu.CompilerParams(
            collective_id=0, has_side_effects=True, vmem_limit_bytes=48 * 1024 * 1024
        ),
    )(*[pltpu.with_memory_space_constraint(array, pltpu.HBM) for array in operands])


def solution(mesh):
    seq, nx = mesh.shape["seq"], mesh.shape["head"]
    ny = 4 if seq == 64 else 2
    nz = seq // (2 * ny)
    split = Mesh(mesh.devices.reshape(ny, nz, 2, nx), SEQ_HEAD)
    in_specs = (P(SEQ, "head"), P(SEQ, "head"), P(SEQ, "head"), P("head"), P("head", None))
    out_specs = P(SEQ_HEAD, None)
    return jax.shard_map(
        functools.partial(shards, ny, nz, nx), mesh=split, in_specs=in_specs, out_specs=out_specs, check_vma=False
    )
```

```python
import functools

import jax
import jax.numpy as jnp
from jax import lax
from jax.experimental import pallas as pl
from jax.experimental.pallas import tpu as pltpu
from jax.sharding import Mesh
from jax.sharding import PartitionSpec as P

DH = 128
SEQ = ("seq_0", "seq_1", "seq_2")
SEQ_HEAD = ("seq_0", "seq_1", "seq_2", "head")
F32 = jnp.float32
BF16 = jnp.bfloat16
CHUNK = 256
EPS = 1e-06
FAR_FIRST = (4, 3, 5, 2, 6, 1, 7)

X_PIECES = ((-1, 0), (1, 1), (-1, 1), (1, 0), (2, 0), (2, 1))


def dot(a, b, ca, cb):
    return lax.dot_general(a, b, (((ca,), (cb,)), ((), ())), preferred_element_type=F32)


def kernel(
    ny,
    nz,
    nx,
    q_hbm,
    k_hbm,
    v_hbm,
    gain_hbm,
    w_hbm,
    out_ref,
    q,
    k,
    v,
    w,
    gain,
    s_first,
    s_loc,
    cp_loc,
    s_sib,
    cp_sib,
    s_chip,
    cp_chip,
    s_arr,
    cp_arr,
    s_run,
    p_run,
    c_run,
    s_back,
    p_back,
    y_out,
    y_in,
    s_pre,
    p_pre,
    p_step,
    s_other,
    p_other,
    s_mine,
    p_mine,
    v_t,
    f_loc,
    p_first,
    o_part,
    p_fin,
    n_out,
    n_in,
    acc,
    load_sem,
    core_send,
    core_recv,
    in_send,
    in_recv,
    back_send,
    back_recv,
    y_send,
    y_recv,
    n_send,
    n_recv,
    w_send,
    w_recv,
):
    tokens, width = q.shape
    heads = width // DH
    pair = heads // 2
    y, z, c, x = (lax.axis_index(name) for name in SEQ_HEAD)

    def modx(i):
        return lax.rem(x + i + nx, nx)

    def mody(i):
        return lax.rem(y + i + ny, ny)

    def modz(i):
        return lax.rem(z + i, nz)

    pending = []

    def remote(src, dst, send_sem, recv_sem, device_id):
        return pltpu.make_async_remote_copy(
            src_ref=src,
            dst_ref=dst,
            send_sem=send_sem,
            recv_sem=recv_sem,
            device_id=device_id,
            device_id_type=pl.DeviceIdType.MESH,
        )

    def start(copy):
        copy.start()
        pending.append(copy.wait_send)

    spacing = nz // heads
    is_worker = (lax.rem(z, spacing) == 0) & (z // (spacing * pair) == c)
    my_head = lax.rem(z // spacing, pair)

    barrier = pltpu.get_barrier_semaphore()

    def greet(peer):
        pl.semaphore_signal(barrier, inc=1, device_id=peer, device_id_type=pl.DeviceIdType.MESH)

    for d in range(1, ny):
        greet({"seq_0": mody(d)})
    for d in range(1, nx):
        greet({"head": modx(d)})
    greet({"seq_2": 1 - c})

    @pl.when(is_worker)
    def _():
        for d in FAR_FIRST:
            if d < nz:
                greet({"seq_1": modz(d)})

    loads = [
        pltpu.make_async_copy(src, dst, load_sem.at[i])
        for i, (src, dst) in enumerate(((k_hbm, k), (q_hbm, q), (v_hbm, v), (w_hbm, w.at[x]), (gain_hbm, gain)))
    ]
    for copy in loads:
        copy.start()

    def chunk(ref, h, j):
        return ref[j * CHUNK : (j + 1) * CHUNK, h * DH : (h + 1) * DH]

    def worker_z(i):
        return (c * pair + i) * spacing

    def in_copy(kind, i, slot, device_id):
        src, dst = ((s_chip, s_arr), (cp_chip, cp_arr))[kind]
        return remote(src.at[i], dst.at[slot], in_send.at[kind, i], in_recv.at[kind, slot], device_id)

    def distance(i):
        ahead = lax.rem(worker_z(i) - z + nz, nz)
        return jnp.minimum(ahead, nz - ahead)

    farther = jnp.where(distance(0) < distance(pair - 1), pair - 1, 0)

    def send_in(kind):
        for n in range(pair):
            i = lax.rem(farther + n, pair)
            here = z == worker_z(i)
            copy = in_copy(kind, i, z, {"seq_1": worker_z(i)})

            @pl.when(jnp.logical_not(here))
            def _(copy=copy):
                copy.start()

            @pl.when(here)
            def _(i=i):
                src, dst = ((s_chip, s_arr), (cp_chip, cp_arr))[kind]
                dst[z] = src[i]

    def drain_in(kind):
        for i in range(pair):
            @pl.when(z != worker_z(i))
            def _(i=i):
                in_copy(kind, i, z, {"seq_1": worker_z(i)}).wait_send()

    def wait_in(kind):
        for d in range(1, nz):
            in_copy(kind, 0, modz(d), {"seq_1": modz(d)}).wait_recv()

    def back_copy(kind, i, d):
        src, dst = ((s_back, s_pre), (p_back, p_pre))[kind]
        return remote(src.at[modz(d)], dst.at[i], back_send.at[kind, d], back_recv.at[kind, i], {"seq_1": modz(d)})

    def send_back(kind):
        src, dst = ((s_back, s_pre), (p_back, p_pre))[kind]
        for d in FAR_FIRST:
            if d < nz:
                back_copy(kind, my_head, d).start()
        dst[my_head] = src[z]

    def wait_back(kind):
        for i in range(pair):
            @pl.when(z != worker_z(i))
            def _(i=i):
                back_copy(kind, i, 1).wait_recv()

    def total_copy(kind, d, slot):
        part = (pl.ds(0, 1), pl.ds(1, 2))[kind]
        return remote(
            y_out.at[part], y_in.at[slot, part], y_send.at[kind, d], y_recv.at[kind, slot], {"seq_0": mody(d)}
        )

    def send_totals(kind):
        for d in (2, 1, 3):
            if d < ny:
                total_copy(kind, d, y).start()

    def wait_totals(kind):
        for d in range(1, ny):
            total_copy(kind, d, mody(d)).wait_recv()

    def s_base_until(limit):
        base = jnp.zeros((DH, DH), F32)
        for r in range(ny - 1):
            base = base + jnp.where(r < limit, y_in[r, 0].astype(F32), 0.0)
        return base

    colour = lax.rem(y + z, 2)
    piece_rows = w.shape[1] // 8

    def rows_of(colour_of, core_of, half, part=None):
        first = colour_of * (4 * piece_rows) + core_of * (2 * piece_rows) + half * piece_rows
        count = piece_rows
        if part is not None:
            count = piece_rows // 2
            first = first + part * count
        return pl.ds(pl.multiple_of(first, count), count)

    def piece(i, colour_of, core_of, part=None):
        offset, half = X_PIECES[i]
        return w.at[modx(offset), rows_of(colour_of, core_of, half, part)]

    def w_copy(number, src, dst, device_id):
        return remote(src, dst, w_send.at[number], w_recv.at[number], device_id)

    def x_send(number):
        offset, half = X_PIECES[number]
        if number < 4:
            rows = rows_of(colour, c, half)
            return w_copy(number, w_hbm.at[rows], w.at[x, rows], {"head": modx(-offset)})
        src = piece(number - 4, colour, c)
        return w_copy(number, src, src, {"head": modx(1 if number == 4 else -1)})

    def x_arrival(number):
        ref = piece(number, colour, c)
        return w_copy(number, ref, ref, {"head": modx(1)})

    def core_copy(number, core_of):
        ref = piece(number, colour, core_of)
        return w_copy(6 + number, ref, ref, {"seq_2": 1 - c})

    def parts_of(number):
        return (None,) if number < 4 else (0, 1)

    def plane_copy(number, colour_of, part):
        ref = piece(number, colour_of, c, part)
        step = 1 if X_PIECES[number][1] == 0 else -1
        if part == 1:
            return w_copy(20 + number, ref, ref, {"seq_1": modz(step + nz)})
        return w_copy(12 + number, ref, ref, {"seq_0": mody(step)})

    def core_plane_copy(number, core_of, part):
        ref = piece(number, 1 - colour, core_of, part)
        return w_copy((22 if part == 1 else 18) + number, ref, ref, {"seq_2": 1 - c})

    def relay_x(numbers):
        for number in numbers:
            x_arrival(number).wait_recv()
            if number < 2:
                start(x_send(4 + number))
            for part in parts_of(number):
                start(plane_copy(number, colour, part))
            start(core_copy(number, c))

    def relay_plane(numbers):
        for number in numbers:
            for part in parts_of(number):
                plane_copy(number, 1 - colour, part).wait_recv()
                start(core_plane_copy(number, c, part))

    row = lax.broadcasted_iota(jnp.int32, (CHUNK, CHUNK), 0)
    col = lax.broadcasted_iota(jnp.int32, (CHUNK, CHUNK), 1)
    loads[0].wait()
    for h in range(heads):
        first = dot(chunk(k, h, 0), chunk(k, h, 0), 0, 0)
        s_first[h] = first.astype(BF16)
        s_loc[h // pair, h % pair] = (first + dot(chunk(k, h, 1), chunk(k, h, 1), 0, 0)).astype(BF16)
    loads[1].wait()
    loads[2].wait()
    strict, causal = col < row, col <= row
    blocks = [(h, j) for h in range(heads) for j in range(2)]
    for h in range(heads):
        v_t[h] = v[:, h * DH : (h + 1) * DH].T
    scores = [jnp.where(strict, dot(chunk(q, h, j), chunk(k, h, j), 1, 1), 0.0).astype(BF16) for h, j in blocks]
    fs = []
    for n, (h, j) in enumerate(blocks):
        f = dot(scores[n], chunk(k, h, j), 1, 0)
        if j == 1:
            f = f + dot(chunk(q, h, j), s_first[h], 1, 0)
        f_loc[j * CHUNK : (j + 1) * CHUNK, h * DH : (h + 1) * DH] = f
        fs.append(f.astype(BF16))
    for h in range(heads):
        cross = dot(v_t[h], q[:, h * DH : (h + 1) * DH], 1, 0)
        pairs = dot(v_t[h, :, :CHUNK], fs[2 * h], 1, 0) + dot(v_t[h, :, CHUNK:], fs[2 * h + 1], 1, 0)
        cp_loc[h // pair, h % pair, 0] = cross.astype(BF16)
        cp_loc[h // pair, h % pair, 1] = pairs.astype(BF16)

    pl.semaphore_wait(barrier, nx - 1 + ny - 1 + 1 + pair - is_worker.astype(jnp.int32))
    sibling = {"seq_2": 1 - c}
    s_core = remote(s_loc.at[1 - c], s_sib, core_send.at[0], core_recv.at[0], sibling)
    cp_core = remote(cp_loc.at[1 - c], cp_sib, core_send.at[1], core_recv.at[1], sibling)
    start(s_core)
    start(cp_core)
    for number in range(4):
        start(x_send(number))
    s_core.wait_recv()
    for i in range(pair):
        s_chip[i] = (s_loc[c, i].astype(F32) + s_sib[i].astype(F32)).astype(BF16)
    send_in(0)
    cp_core.wait_recv()
    for i in range(pair):
        mine, other = cp_loc[c, i], cp_sib[i]
        early = jnp.where(c == 0, s_loc[c, i], s_sib[i])
        late = jnp.where(c == 0, other[0], mine[0])
        cp_chip[i, 0] = (mine[0].astype(F32) + other[0].astype(F32)).astype(BF16)
        cp_chip[i, 1] = (mine[1].astype(F32) + other[1].astype(F32) + dot(late, early, 1, 0)).astype(BF16)
    send_in(1)

    @pl.when(is_worker)
    def _():
        wait_in(0)
        total = jnp.zeros((DH, DH), F32)
        for r in range(nz):
            s_run[r] = total
            total = total + s_arr[r].astype(F32)
        y_out[0] = total.astype(BF16)
        send_totals(0)
        y_in[y, 0] = total.astype(BF16)

    relay_x((0, 1))

    @pl.when(is_worker)
    def _():
        wait_in(1)
        pairs = jnp.zeros((DH, DH), F32)
        cross = jnp.zeros((DH, DH), F32)
        for r in range(nz):
            p_run[r] = pairs
            c_run[r] = cross.astype(BF16)
            pairs = pairs + (cp_arr[r, 1].astype(F32) + dot(cp_arr[r, 0], s_run[r].astype(BF16), 1, 0))
            cross = cross + cp_arr[r, 0].astype(F32)
        y_out[1] = cross.astype(BF16)
        y_out[2] = pairs.astype(BF16)
        send_totals(1)
        y_in[y, 1] = cross.astype(BF16)
        y_in[y, 2] = pairs.astype(BF16)
        wait_totals(0)
        s_base = s_base_until(y)
        for r in range(nz):
            s_back[r] = (s_run[r] + s_base).astype(BF16)
        send_back(0)
        s_base = s_base.astype(BF16)
        for r in range(nz):
            p_run[r] = p_run[r] + dot(c_run[r], s_base, 1, 0)

    relay_x((2, 3))

    @pl.when(is_worker)
    def _():
        before = [s_base_until(r).astype(BF16) for r in range(ny - 1)]
        wait_totals(1)
        p_base = jnp.zeros((DH, DH), F32)
        for r in range(ny - 1):
            line = y_in[r, 2].astype(F32) + dot(y_in[r, 1], before[r], 1, 0)
            p_base = p_base + jnp.where(r < y, line, 0.0)
        for r in range(nz):
            p_back[r] = (p_run[r] + p_base).astype(BF16)
        send_back(1)

    relay_plane((0, 1))

    wait_back(0)
    for i in range(pair):
        mine, other = cp_loc[c, i], cp_sib[i]
        chip = s_pre[i]
        early = jnp.where(c == 0, s_loc[c, i], s_sib[i])
        later = (chip.astype(F32) + early.astype(F32)).astype(BF16)
        s_mine[c, i] = jnp.where(c == 0, chip, later)
        s_other[i] = jnp.where(c == 0, later, chip)
        p_step[i] = jnp.where(c == 0, mine[1], other[1]).astype(F32) + dot(
            jnp.where(c == 0, mine[0], other[0]), chip, 1, 0
        )
    s_swap = remote(s_other, s_mine.at[c], core_send.at[2], core_recv.at[2], sibling)
    start(s_swap)
    s_swap_in = remote(s_other, s_mine.at[1 - c], core_send.at[2], core_recv.at[2], sibling)
    s_swap_in.wait_recv()

    fs = []
    for h, j in blocks:
        f = chunk(f_loc, h, j) + dot(chunk(q, h, j), s_mine[h // pair, h % pair], 1, 0)
        fs.append(f.astype(BF16))
    mixing = [
        jnp.where(causal, dot(chunk(q, h, j), fs[n], 1, 1), 0.0).astype(BF16) for n, (h, j) in enumerate(blocks)
    ]
    for n, (h, j) in enumerate(blocks):
        o_part[j * CHUNK : (j + 1) * CHUNK, h * DH : (h + 1) * DH] = dot(mixing[n], chunk(v, h, j), 1, 0)
    for h in range(heads):
        p_first[h // pair, h % pair] = dot(v_t[h, :, :CHUNK], fs[2 * h], 1, 0)
    relay_x((4, 5))

    wait_back(1)
    for i in range(pair):
        chip = p_pre[i]
        later = (chip.astype(F32) + p_step[i]).astype(BF16)
        p_mine[c, i] = jnp.where(c == 0, chip, later)
        p_other[i] = jnp.where(c == 0, later, chip)
    p_swap = remote(p_other, p_mine.at[c], core_send.at[3], core_recv.at[3], sibling)
    start(p_swap)
    p_swap_in = remote(p_other, p_mine.at[1 - c], core_send.at[3], core_recv.at[3], sibling)

    rows_x = tokens // nx
    loads[4].wait()

    def n_copy(d, g, slot):
        return remote(n_out.at[d, g], n_in.at[slot, g], n_send.at[d, g], n_recv.at[slot, g], {"head": modx(d)})

    for step in range(2):
        g = c if step == 0 else 1 - c
        if step == 1:
            p_swap_in.wait_recv()
        for i in range(pair):
            p_h = p_mine[g, i]
            p_fin[0, i] = p_h
            p_fin[1, i] = (p_h.astype(F32) + p_first[g, i]).astype(BF16)
        for d in (2, 1, 3, 0):
            target = modx(d)
            rows = pl.ds(pl.multiple_of(target * rows_x, rows_x), rows_x)
            part = target // (CHUNK // rows_x)
            for i in range(pair):
                cols = pl.ds(pl.multiple_of(g * (pair * DH) + i * DH, DH), DH)
                attended = o_part[rows, cols] + dot(q[rows, cols], p_fin[part, i], 1, 1)
                mean_square = jnp.mean(attended * attended, axis=-1, keepdims=True)
                n_out[d, g, :, i * DH : (i + 1) * DH] = (
                    attended * lax.rsqrt(mean_square + EPS) * gain[:, cols]
                ).astype(BF16)
            if d:
                start(n_copy(d, g, x))

    relay_plane((2, 3))

    loads[3].wait()
    tile = 512
    n_cols = out_ref.shape[1]

    half = w.shape[1] // 2

    def project(rows_in, slot, quarter, first, last):
        for begin in range(0, n_cols, tile):
            cols = slice(begin, begin + tile)
            part = dot(rows_in[slot, 0], w[quarter, :half, cols], 1, 0)
            part = part + dot(rows_in[slot, 1], w[quarter, half:, cols], 1, 0)
            if not first:
                part = part + acc[:, cols]
            if last:
                out_ref[:, cols] = part.astype(BF16)
            else:
                acc[:, cols] = part

    project(n_out, 0, x, True, False)
    relay_plane((4, 5))
    for offset in (-1, 1, 2):
        quarter = modx(offset)
        for number, (of, _) in enumerate(X_PIECES):
            if of == offset:
                core_copy(number, 1 - c).wait_recv()
                for part in parts_of(number):
                    core_plane_copy(number, 1 - c, part).wait_recv()
        for g in range(2):
            n_copy(offset % nx, g, quarter).wait_recv()
        project(n_in, quarter, quarter, False, offset == 2)

    for wait in pending:
        wait()
    drain_in(0)
    drain_in(1)

    @pl.when(is_worker)
    def _():
        for kind in range(2):
            for d in range(1, nz):
                back_copy(kind, my_head, d).wait_send()
            for d in range(1, ny):
                total_copy(kind, d, y).wait_send()


def shards(ny, nz, nx, queries, key_vectors, value_vectors, norm_gain, out_weight):
    tokens, width = queries.shape
    heads = width // DH
    pair = heads // 2
    depth, n_cols = out_weight.shape

    def matrices(*lead, kind=BF16):
        return pltpu.VMEM(lead + (DH, DH), kind)

    operands = (queries, key_vectors, value_vectors, norm_gain.reshape(1, width), out_weight)
    return pl.pallas_call(
        functools.partial(kernel, ny, nz, nx),
        out_shape=jax.ShapeDtypeStruct((tokens // nx, n_cols), BF16),
        in_specs=[pl.BlockSpec(memory_space=pltpu.HBM)] * 5,
        out_specs=pl.BlockSpec(memory_space=pltpu.VMEM),
        scratch_shapes=[
            pltpu.VMEM((tokens, width), BF16),
            pltpu.VMEM((tokens, width), BF16),
            pltpu.VMEM((tokens, width), BF16),
            pltpu.VMEM((nx, depth, n_cols), BF16),
            pltpu.VMEM((1, width), F32),
            matrices(heads),
            matrices(2, pair),
            matrices(2, pair, 2),
            matrices(pair),
            matrices(pair, 2),
            matrices(pair),
            matrices(pair, 2),
            matrices(nz),
            matrices(nz, 2),
            matrices(nz, kind=F32),
            matrices(nz, kind=F32),
            matrices(nz),
            matrices(nz),
            matrices(nz),
            matrices(3),
            matrices(ny, 3),
            matrices(pair),
            matrices(pair),
            matrices(pair, kind=F32),
            matrices(pair),
            matrices(pair),
            matrices(2, pair),
            matrices(2, pair),
            pltpu.VMEM((heads, DH, tokens), BF16),
            pltpu.VMEM((tokens, width), F32),
            matrices(2, pair, kind=F32),
            pltpu.VMEM((tokens, width), F32),
            matrices(2, pair),
            pltpu.VMEM((nx, 2, tokens // nx, width // 2), BF16),
            pltpu.VMEM((nx, 2, tokens // nx, width // 2), BF16),
            pltpu.VMEM((tokens // nx, n_cols), F32),
            pltpu.SemaphoreType.DMA((5,)),
            pltpu.SemaphoreType.DMA((4,)),
            pltpu.SemaphoreType.DMA((4,)),
            pltpu.SemaphoreType.DMA((2, pair)),
            pltpu.SemaphoreType.DMA((2, nz)),
            pltpu.SemaphoreType.DMA((2, nz)),
            pltpu.SemaphoreType.DMA((2, pair)),
            pltpu.SemaphoreType.DMA((2, ny)),
            pltpu.SemaphoreType.DMA((2, ny)),
            pltpu.SemaphoreType.DMA((nx, 2)),
            pltpu.SemaphoreType.DMA((nx, 2)),
            pltpu.SemaphoreType.DMA((28,)),
            pltpu.SemaphoreType.DMA((28,)),
        ],
        compiler_params=pltpu.CompilerParams(
            collective_id=0, has_side_effects=True, vmem_limit_bytes=48 * 1024 * 1024
        ),
    )(*[pltpu.with_memory_space_constraint(array, pltpu.HBM) for array in operands])


def solution(mesh):
    seq, nx = mesh.shape["seq"], mesh.shape["head"]
    ny = 4 if seq == 64 else 2
    nz = seq // (2 * ny)
    split = Mesh(mesh.devices.reshape(ny, nz, 2, nx), SEQ_HEAD)
    in_specs = (P(SEQ, "head"), P(SEQ, "head"), P(SEQ, "head"), P("head"), P("head", None))
    out_specs = P(SEQ_HEAD, None)
    return jax.shard_map(
        functools.partial(shards, ny, nz, nx), mesh=split, in_specs=in_specs, out_specs=out_specs, check_vma=False
    )
```

```python
import functools

import jax
import jax.numpy as jnp
from jax import lax
from jax.experimental import pallas as pl
from jax.experimental.pallas import tpu as pltpu
from jax.sharding import Mesh
from jax.sharding import PartitionSpec as P

DH = 128
SEQ = ("seq_0", "seq_1", "seq_2")
SEQ_HEAD = ("seq_0", "seq_1", "seq_2", "head")
F32 = jnp.float32
BF16 = jnp.bfloat16
CHUNK = 256
EPS = 1e-06
FAR_FIRST = (4, 3, 5, 2, 6, 1, 7)

PARTS = ((0, 1), (0, 1), (None,), (None,), (0, 1), (0, 1))
X_PIECES = ((-1, 0), (1, 1), (-1, 1), (1, 0), (2, 0), (2, 1))


def dot(a, b, ca, cb):
    return lax.dot_general(a, b, (((ca,), (cb,)), ((), ())), preferred_element_type=F32)


def kernel(
    ny,
    nz,
    nx,
    q_hbm,
    k_hbm,
    v_hbm,
    gain_hbm,
    w_hbm,
    out_ref,
    q,
    k,
    v,
    w,
    gain,
    s_first,
    s_loc,
    cp_loc,
    s_sib,
    cp_sib,
    s_chip,
    cp_chip,
    s_arr,
    cp_arr,
    s_run,
    p_run,
    c_run,
    s_back,
    p_back,
    y_out,
    y_in,
    s_pre,
    p_pre,
    p_step,
    s_other,
    p_other,
    s_mine,
    p_mine,
    v_t,
    f_loc,
    p_first,
    o_part,
    p_fin,
    n_out,
    n_in,
    acc,
    load_sem,
    core_send,
    core_recv,
    in_send,
    in_recv,
    back_send,
    back_recv,
    y_send,
    y_recv,
    n_send,
    n_recv,
    w_send,
    w_recv,
):
    tokens, width = q.shape
    heads = width // DH
    pair = heads // 2
    y, z, c, x = (lax.axis_index(name) for name in SEQ_HEAD)

    def modx(i):
        return lax.rem(x + i + nx, nx)

    def mody(i):
        return lax.rem(y + i + ny, ny)

    def modz(i):
        return lax.rem(z + i, nz)

    pending = []

    def remote(src, dst, send_sem, recv_sem, device_id):
        return pltpu.make_async_remote_copy(
            src_ref=src,
            dst_ref=dst,
            send_sem=send_sem,
            recv_sem=recv_sem,
            device_id=device_id,
            device_id_type=pl.DeviceIdType.MESH,
        )

    def start(copy):
        copy.start()
        pending.append(copy.wait_send)

    spacing = nz // heads
    is_worker = (lax.rem(z, spacing) == 0) & (z // (spacing * pair) == c)
    my_head = lax.rem(z // spacing, pair)

    barrier = pltpu.get_barrier_semaphore()

    def greet(peer):
        pl.semaphore_signal(barrier, inc=1, device_id=peer, device_id_type=pl.DeviceIdType.MESH)

    for d in range(1, ny):
        greet({"seq_0": mody(d)})
    for d in range(1, nx):
        greet({"head": modx(d)})
    greet({"seq_2": 1 - c})

    @pl.when(is_worker)
    def _():
        for d in FAR_FIRST:
            if d < nz:
                greet({"seq_1": modz(d)})

    loads = [
        pltpu.make_async_copy(src, dst, load_sem.at[i])
        for i, (src, dst) in enumerate(((k_hbm, k), (q_hbm, q), (v_hbm, v), (w_hbm, w.at[x]), (gain_hbm, gain)))
    ]
    for copy in loads:
        copy.start()

    def chunk(ref, h, j):
        return ref[j * CHUNK : (j + 1) * CHUNK, h * DH : (h + 1) * DH]

    def worker_z(i):
        return (c * pair + i) * spacing

    def in_copy(kind, i, slot, device_id):
        src, dst = ((s_chip, s_arr), (cp_chip, cp_arr))[kind]
        return remote(src.at[i], dst.at[slot], in_send.at[kind, i], in_recv.at[kind, slot], device_id)

    def distance(i):
        ahead = lax.rem(worker_z(i) - z + nz, nz)
        return jnp.minimum(ahead, nz - ahead)

    farther = jnp.where(distance(0) < distance(pair - 1), pair - 1, 0)

    def send_in(kind):
        for n in range(pair):
            i = lax.rem(farther + n, pair)
            here = z == worker_z(i)
            copy = in_copy(kind, i, z, {"seq_1": worker_z(i)})

            @pl.when(jnp.logical_not(here))
            def _(copy=copy):
                copy.start()

            @pl.when(here)
            def _(i=i):
                src, dst = ((s_chip, s_arr), (cp_chip, cp_arr))[kind]
                dst[z] = src[i]

    def drain_in(kind):
        for i in range(pair):
            @pl.when(z != worker_z(i))
            def _(i=i):
                in_copy(kind, i, z, {"seq_1": worker_z(i)}).wait_send()

    def wait_in(kind):
        for d in range(1, nz):
            in_copy(kind, 0, modz(d), {"seq_1": modz(d)}).wait_recv()

    def back_copy(kind, i, d):
        src, dst = ((s_back, s_pre), (p_back, p_pre))[kind]
        return remote(src.at[modz(d)], dst.at[i], back_send.at[kind, d], back_recv.at[kind, i], {"seq_1": modz(d)})

    def send_back(kind):
        src, dst = ((s_back, s_pre), (p_back, p_pre))[kind]
        for d in FAR_FIRST:
            if d < nz:
                back_copy(kind, my_head, d).start()
        dst[my_head] = src[z]

    def wait_back(kind):
        for i in range(pair):
            @pl.when(z != worker_z(i))
            def _(i=i):
                back_copy(kind, i, 1).wait_recv()

    def total_copy(kind, d, slot):
        part = (pl.ds(0, 1), pl.ds(1, 2))[kind]
        return remote(
            y_out.at[part], y_in.at[slot, part], y_send.at[kind, d], y_recv.at[kind, slot], {"seq_0": mody(d)}
        )

    def send_totals(kind):
        for d in (2, 1, 3):
            if d < ny:
                total_copy(kind, d, y).start()

    def wait_totals(kind):
        for d in range(1, ny):
            total_copy(kind, d, mody(d)).wait_recv()

    def s_base_until(limit):
        base = jnp.zeros((DH, DH), F32)
        for r in range(ny - 1):
            base = base + jnp.where(r < limit, y_in[r, 0].astype(F32), 0.0)
        return base

    colour = lax.rem(y + z, 2)
    piece_rows = w.shape[1] // 8

    def rows_of(colour_of, core_of, half, part=None):
        first = colour_of * (4 * piece_rows) + core_of * (2 * piece_rows) + half * piece_rows
        count = piece_rows
        if part is not None:
            count = piece_rows // 2
            first = first + part * count
        return pl.ds(pl.multiple_of(first, count), count)

    def piece(i, colour_of, core_of, part=None):
        offset, half = X_PIECES[i]
        return w.at[modx(offset), rows_of(colour_of, core_of, half, part)]

    def w_copy(number, src, dst, device_id):
        return remote(src, dst, w_send.at[number], w_recv.at[number], device_id)

    def unit(number, part):
        return 2 * number + (part or 0)

    def x_send(number, part):
        offset, half = X_PIECES[number]
        if number < 4:
            rows = rows_of(colour, c, half, part)
            return w_copy(unit(number, part), w_hbm.at[rows], w.at[x, rows], {"head": modx(-offset)})
        src = piece(number - 4, colour, c, part)
        return w_copy(unit(number, part), src, src, {"head": modx(1 if number == 4 else -1)})

    def x_arrival(number, part):
        ref = piece(number, colour, c, part)
        return w_copy(unit(number, part), ref, ref, {"head": modx(1)})

    def plane_copy(number, part, colour_of):
        ref = piece(number, colour_of, c, part)
        step = 1 if X_PIECES[number][1] == 0 else -1
        peer = {"seq_1": modz(step + nz)} if number >= 4 and part == 1 else {"seq_0": mody(step)}
        return w_copy(12 + unit(number, part), ref, ref, peer)

    def core_copy(number, core_of):
        ref = piece(number, colour, core_of)
        return w_copy(24 + number, ref, ref, {"seq_2": 1 - c})

    def core_plane_copy(number, part, core_of):
        ref = piece(number, 1 - colour, core_of, part)
        return w_copy(30 + unit(number, part), ref, ref, {"seq_2": 1 - c})

    def relay_x(*units):
        for number, part in units:
            x_arrival(number, part).wait_recv()
            if number < 2:
                start(x_send(4 + number, part))
            start(plane_copy(number, part, colour))
        for number, part in units:
            if part != 0:
                start(core_copy(number, c))

    def arrive_plane(number):
        for part in PARTS[number]:
            plane_copy(number, part, 1 - colour).wait_recv()
            if number >= 4:
                start(core_plane_copy(number, part, c))
        if number < 4:
            start(core_plane_copy(number, None, c))

    row = lax.broadcasted_iota(jnp.int32, (CHUNK, CHUNK), 0)
    col = lax.broadcasted_iota(jnp.int32, (CHUNK, CHUNK), 1)
    loads[0].wait()
    for h in range(heads):
        first = dot(chunk(k, h, 0), chunk(k, h, 0), 0, 0)
        s_first[h] = first.astype(BF16)
        s_loc[h // pair, h % pair] = (first + dot(chunk(k, h, 1), chunk(k, h, 1), 0, 0)).astype(BF16)
    loads[1].wait()
    loads[2].wait()
    strict, causal = col < row, col <= row
    blocks = [(h, j) for h in range(heads) for j in range(2)]
    for h in range(heads):
        v_t[h] = v[:, h * DH : (h + 1) * DH].T
    scores = [jnp.where(strict, dot(chunk(q, h, j), chunk(k, h, j), 1, 1), 0.0).astype(BF16) for h, j in blocks]
    fs = []
    for n, (h, j) in enumerate(blocks):
        f = dot(scores[n], chunk(k, h, j), 1, 0)
        if j == 1:
            f = f + dot(chunk(q, h, j), s_first[h], 1, 0)
        f_loc[j * CHUNK : (j + 1) * CHUNK, h * DH : (h + 1) * DH] = f
        fs.append(f.astype(BF16))
    for h in range(heads):
        cross = dot(v_t[h], q[:, h * DH : (h + 1) * DH], 1, 0)
        pairs = dot(v_t[h, :, :CHUNK], fs[2 * h], 1, 0) + dot(v_t[h, :, CHUNK:], fs[2 * h + 1], 1, 0)
        cp_loc[h // pair, h % pair, 0] = cross.astype(BF16)
        cp_loc[h // pair, h % pair, 1] = pairs.astype(BF16)

    pl.semaphore_wait(barrier, nx - 1 + ny - 1 + 1 + pair - is_worker.astype(jnp.int32))
    sibling = {"seq_2": 1 - c}
    s_core = remote(s_loc.at[1 - c], s_sib, core_send.at[0], core_recv.at[0], sibling)
    cp_core = remote(cp_loc.at[1 - c], cp_sib, core_send.at[1], core_recv.at[1], sibling)
    start(s_core)
    start(cp_core)
    for number, part in ((0, 0), (1, 0), (0, 1), (1, 1), (2, None), (3, None)):
        start(x_send(number, part))
    s_core.wait_recv()
    for i in range(pair):
        s_chip[i] = (s_loc[c, i].astype(F32) + s_sib[i].astype(F32)).astype(BF16)
    send_in(0)
    cp_core.wait_recv()
    for i in range(pair):
        mine, other = cp_loc[c, i], cp_sib[i]
        early = jnp.where(c == 0, s_loc[c, i], s_sib[i])
        late = jnp.where(c == 0, other[0], mine[0])
        cp_chip[i, 0] = (mine[0].astype(F32) + other[0].astype(F32)).astype(BF16)
        cp_chip[i, 1] = (mine[1].astype(F32) + other[1].astype(F32) + dot(late, early, 1, 0)).astype(BF16)
    send_in(1)

    relay_x((0, 0), (1, 0))

    @pl.when(is_worker)
    def _():
        wait_in(0)
        total = jnp.zeros((DH, DH), F32)
        for r in range(nz):
            s_run[r] = total
            total = total + s_arr[r].astype(F32)
        y_out[0] = total.astype(BF16)
        send_totals(0)
        y_in[y, 0] = total.astype(BF16)

    relay_x((0, 1), (1, 1))

    @pl.when(is_worker)
    def _():
        wait_in(1)
        pairs = jnp.zeros((DH, DH), F32)
        cross = jnp.zeros((DH, DH), F32)
        for r in range(nz):
            p_run[r] = pairs
            c_run[r] = cross.astype(BF16)
            pairs = pairs + (cp_arr[r, 1].astype(F32) + dot(cp_arr[r, 0], s_run[r].astype(BF16), 1, 0))
            cross = cross + cp_arr[r, 0].astype(F32)
        y_out[1] = cross.astype(BF16)
        y_out[2] = pairs.astype(BF16)
        send_totals(1)
        y_in[y, 1] = cross.astype(BF16)
        y_in[y, 2] = pairs.astype(BF16)
        wait_totals(0)
        s_base = s_base_until(y)
        for r in range(nz):
            s_back[r] = (s_run[r] + s_base).astype(BF16)
        send_back(0)
        s_base = s_base.astype(BF16)
        for r in range(nz):
            p_run[r] = p_run[r] + dot(c_run[r], s_base, 1, 0)
        before = [s_base_until(r).astype(BF16) for r in range(ny - 1)]
        wait_totals(1)
        p_base = jnp.zeros((DH, DH), F32)
        for r in range(ny - 1):
            line = y_in[r, 2].astype(F32) + dot(y_in[r, 1], before[r], 1, 0)
            p_base = p_base + jnp.where(r < y, line, 0.0)
        for r in range(nz):
            p_back[r] = (p_run[r] + p_base).astype(BF16)
        send_back(1)

    wait_back(0)
    for i in range(pair):
        mine, other = cp_loc[c, i], cp_sib[i]
        chip = s_pre[i]
        early = jnp.where(c == 0, s_loc[c, i], s_sib[i])
        later = (chip.astype(F32) + early.astype(F32)).astype(BF16)
        s_mine[c, i] = jnp.where(c == 0, chip, later)
        s_other[i] = jnp.where(c == 0, later, chip)
        p_step[i] = jnp.where(c == 0, mine[1], other[1]).astype(F32) + dot(
            jnp.where(c == 0, mine[0], other[0]), chip, 1, 0
        )
    s_swap = remote(s_other, s_mine.at[c], core_send.at[2], core_recv.at[2], sibling)
    start(s_swap)
    relay_x((2, None), (3, None))
    arrive_plane(0)
    arrive_plane(1)
    s_swap_in = remote(s_other, s_mine.at[1 - c], core_send.at[2], core_recv.at[2], sibling)
    s_swap_in.wait_recv()

    fs = []
    for h, j in blocks:
        f = chunk(f_loc, h, j) + dot(chunk(q, h, j), s_mine[h // pair, h % pair], 1, 0)
        fs.append(f.astype(BF16))
    mixing = [
        jnp.where(causal, dot(chunk(q, h, j), fs[n], 1, 1), 0.0).astype(BF16) for n, (h, j) in enumerate(blocks)
    ]
    for n, (h, j) in enumerate(blocks):
        o_part[j * CHUNK : (j + 1) * CHUNK, h * DH : (h + 1) * DH] = dot(mixing[n], chunk(v, h, j), 1, 0)
    for h in range(heads):
        p_first[h // pair, h % pair] = dot(v_t[h, :, :CHUNK], fs[2 * h], 1, 0)
    relay_x((4, 0), (5, 0), (4, 1), (5, 1))

    wait_back(1)
    for i in range(pair):
        chip = p_pre[i]
        later = (chip.astype(F32) + p_step[i]).astype(BF16)
        p_mine[c, i] = jnp.where(c == 0, chip, later)
        p_other[i] = jnp.where(c == 0, later, chip)
    p_swap = remote(p_other, p_mine.at[c], core_send.at[3], core_recv.at[3], sibling)
    start(p_swap)
    p_swap_in = remote(p_other, p_mine.at[1 - c], core_send.at[3], core_recv.at[3], sibling)

    rows_x = tokens // nx
    loads[4].wait()

    def n_copy(d, g, slot):
        return remote(n_out.at[d, g], n_in.at[slot, g], n_send.at[d, g], n_recv.at[slot, g], {"head": modx(d)})

    for step in range(2):
        g = c if step == 0 else 1 - c
        if step == 1:
            p_swap_in.wait_recv()
        for i in range(pair):
            p_h = p_mine[g, i]
            p_fin[0, i] = p_h
            p_fin[1, i] = (p_h.astype(F32) + p_first[g, i]).astype(BF16)
        for d in (2, 1, 3, 0):
            target = modx(d)
            rows = pl.ds(pl.multiple_of(target * rows_x, rows_x), rows_x)
            part = target // (CHUNK // rows_x)
            for i in range(pair):
                cols = pl.ds(pl.multiple_of(g * (pair * DH) + i * DH, DH), DH)
                attended = o_part[rows, cols] + dot(q[rows, cols], p_fin[part, i], 1, 1)
                mean_square = jnp.mean(attended * attended, axis=-1, keepdims=True)
                n_out[d, g, :, i * DH : (i + 1) * DH] = (
                    attended * lax.rsqrt(mean_square + EPS) * gain[:, cols]
                ).astype(BF16)
            if d:
                start(n_copy(d, g, x))

    arrive_plane(2)
    arrive_plane(3)

    loads[3].wait()
    tile = 512
    n_cols = out_ref.shape[1]

    half = w.shape[1] // 2

    def project(rows_in, slot, quarter, first, last):
        for begin in range(0, n_cols, tile):
            cols = slice(begin, begin + tile)
            part = dot(rows_in[slot, 0], w[quarter, :half, cols], 1, 0)
            part = part + dot(rows_in[slot, 1], w[quarter, half:, cols], 1, 0)
            if not first:
                part = part + acc[:, cols]
            if last:
                out_ref[:, cols] = part.astype(BF16)
            else:
                acc[:, cols] = part

    project(n_out, 0, x, True, False)
    arrive_plane(4)
    arrive_plane(5)
    for offset in (-1, 1, 2):
        quarter = modx(offset)
        for number, (of, _) in enumerate(X_PIECES):
            if of == offset:
                core_copy(number, 1 - c).wait_recv()
                for part in PARTS[number] if number >= 4 else (None,):
                    core_plane_copy(number, part, 1 - c).wait_recv()
        for g in range(2):
            n_copy(offset % nx, g, quarter).wait_recv()
        project(n_in, quarter, quarter, False, offset == 2)

    for wait in pending:
        wait()
    drain_in(0)
    drain_in(1)

    @pl.when(is_worker)
    def _():
        for kind in range(2):
            for d in range(1, nz):
                back_copy(kind, my_head, d).wait_send()
            for d in range(1, ny):
                total_copy(kind, d, y).wait_send()


def shards(ny, nz, nx, queries, key_vectors, value_vectors, norm_gain, out_weight):
    tokens, width = queries.shape
    heads = width // DH
    pair = heads // 2
    depth, n_cols = out_weight.shape

    def matrices(*lead, kind=BF16):
        return pltpu.VMEM(lead + (DH, DH), kind)

    operands = (queries, key_vectors, value_vectors, norm_gain.reshape(1, width), out_weight)
    return pl.pallas_call(
        functools.partial(kernel, ny, nz, nx),
        out_shape=jax.ShapeDtypeStruct((tokens // nx, n_cols), BF16),
        in_specs=[pl.BlockSpec(memory_space=pltpu.HBM)] * 5,
        out_specs=pl.BlockSpec(memory_space=pltpu.VMEM),
        scratch_shapes=[
            pltpu.VMEM((tokens, width), BF16),
            pltpu.VMEM((tokens, width), BF16),
            pltpu.VMEM((tokens, width), BF16),
            pltpu.VMEM((nx, depth, n_cols), BF16),
            pltpu.VMEM((1, width), F32),
            matrices(heads),
            matrices(2, pair),
            matrices(2, pair, 2),
            matrices(pair),
            matrices(pair, 2),
            matrices(pair),
            matrices(pair, 2),
            matrices(nz),
            matrices(nz, 2),
            matrices(nz, kind=F32),
            matrices(nz, kind=F32),
            matrices(nz),
            matrices(nz),
            matrices(nz),
            matrices(3),
            matrices(ny, 3),
            matrices(pair),
            matrices(pair),
            matrices(pair, kind=F32),
            matrices(pair),
            matrices(pair),
            matrices(2, pair),
            matrices(2, pair),
            pltpu.VMEM((heads, DH, tokens), BF16),
            pltpu.VMEM((tokens, width), F32),
            matrices(2, pair, kind=F32),
            pltpu.VMEM((tokens, width), F32),
            matrices(2, pair),
            pltpu.VMEM((nx, 2, tokens // nx, width // 2), BF16),
            pltpu.VMEM((nx, 2, tokens // nx, width // 2), BF16),
            pltpu.VMEM((tokens // nx, n_cols), F32),
            pltpu.SemaphoreType.DMA((5,)),
            pltpu.SemaphoreType.DMA((4,)),
            pltpu.SemaphoreType.DMA((4,)),
            pltpu.SemaphoreType.DMA((2, pair)),
            pltpu.SemaphoreType.DMA((2, nz)),
            pltpu.SemaphoreType.DMA((2, nz)),
            pltpu.SemaphoreType.DMA((2, pair)),
            pltpu.SemaphoreType.DMA((2, ny)),
            pltpu.SemaphoreType.DMA((2, ny)),
            pltpu.SemaphoreType.DMA((nx, 2)),
            pltpu.SemaphoreType.DMA((nx, 2)),
            pltpu.SemaphoreType.DMA((42,)),
            pltpu.SemaphoreType.DMA((42,)),
        ],
        compiler_params=pltpu.CompilerParams(
            collective_id=0, has_side_effects=True, vmem_limit_bytes=48 * 1024 * 1024
        ),
    )(*[pltpu.with_memory_space_constraint(array, pltpu.HBM) for array in operands])


def solution(mesh):
    seq, nx = mesh.shape["seq"], mesh.shape["head"]
    ny = 4 if seq == 64 else 2
    nz = seq // (2 * ny)
    split = Mesh(mesh.devices.reshape(ny, nz, 2, nx), SEQ_HEAD)
    in_specs = (P(SEQ, "head"), P(SEQ, "head"), P(SEQ, "head"), P("head"), P("head", None))
    out_specs = P(SEQ_HEAD, None)
    return jax.shard_map(
        functools.partial(shards, ny, nz, nx), mesh=split, in_specs=in_specs, out_specs=out_specs, check_vma=False
    )
```

```python
import functools

import jax
import jax.numpy as jnp
from jax import lax
from jax.experimental import pallas as pl
from jax.experimental.pallas import tpu as pltpu
from jax.sharding import Mesh
from jax.sharding import PartitionSpec as P

DH = 128
SEQ = ("seq_0", "seq_1", "seq_2")
SEQ_HEAD = ("seq_0", "seq_1", "seq_2", "head")
F32 = jnp.float32
BF16 = jnp.bfloat16
CHUNK = 256
EPS = 1e-06
FAR_FIRST = (4, 3, 5, 2, 6, 1, 7)

PARTS = ((0, 1), (0, 1), (None,), (None,), (0, 1), (0, 1))
X_PIECES = ((-1, 0), (1, 1), (-1, 1), (1, 0), (2, 0), (2, 1))


def dot(a, b, ca, cb):
    return lax.dot_general(a, b, (((ca,), (cb,)), ((), ())), preferred_element_type=F32)


def kernel(
    ny,
    nz,
    nx,
    q_hbm,
    k_hbm,
    v_hbm,
    gain_hbm,
    w_hbm,
    out_ref,
    q,
    k,
    v,
    w,
    gain,
    s_first,
    s_loc,
    cp_loc,
    s_sib,
    cp_sib,
    s_chip,
    cp_chip,
    s_arr,
    cp_arr,
    s_run,
    p_run,
    c_run,
    s_back,
    p_back,
    y_out,
    y_in,
    s_pre,
    p_pre,
    p_step,
    s_other,
    p_other,
    s_mine,
    p_mine,
    v_t,
    f_loc,
    p_first,
    o_part,
    p_fin,
    n_out,
    n_in,
    acc,
    load_sem,
    core_send,
    core_recv,
    in_send,
    in_recv,
    back_send,
    back_recv,
    y_send,
    y_recv,
    n_send,
    n_recv,
    w_send,
    w_recv,
):
    tokens, width = q.shape
    heads = width // DH
    pair = heads // 2
    y, z, c, x = (lax.axis_index(name) for name in SEQ_HEAD)

    def modx(i):
        return lax.rem(x + i + nx, nx)

    def mody(i):
        return lax.rem(y + i + ny, ny)

    def modz(i):
        return lax.rem(z + i, nz)

    pending = []

    def remote(src, dst, send_sem, recv_sem, device_id):
        return pltpu.make_async_remote_copy(
            src_ref=src,
            dst_ref=dst,
            send_sem=send_sem,
            recv_sem=recv_sem,
            device_id=device_id,
            device_id_type=pl.DeviceIdType.MESH,
        )

    def start(copy):
        copy.start()
        pending.append(copy.wait_send)

    spacing = nz // heads
    is_worker = (lax.rem(z, spacing) == 0) & (z // (spacing * pair) == c)
    my_head = lax.rem(z // spacing, pair)

    barrier = pltpu.get_barrier_semaphore()

    def greet(peer):
        pl.semaphore_signal(barrier, inc=1, device_id=peer, device_id_type=pl.DeviceIdType.MESH)

    for d in range(1, ny):
        greet({"seq_0": mody(d)})
    for d in range(1, nx):
        greet({"head": modx(d)})
    greet({"seq_2": 1 - c})

    @pl.when(is_worker)
    def _():
        for d in FAR_FIRST:
            if d < nz:
                greet({"seq_1": modz(d)})

    loads = [
        pltpu.make_async_copy(src, dst, load_sem.at[i])
        for i, (src, dst) in enumerate(((k_hbm, k), (q_hbm, q), (v_hbm, v), (w_hbm, w.at[x]), (gain_hbm, gain)))
    ]
    for copy in loads[:3]:
        copy.start()

    def chunk(ref, h, j):
        return ref[j * CHUNK : (j + 1) * CHUNK, h * DH : (h + 1) * DH]

    def worker_z(i):
        return (c * pair + i) * spacing

    def in_copy(kind, i, slot, device_id):
        src, dst = ((s_chip, s_arr), (cp_chip, cp_arr))[kind]
        return remote(src.at[i], dst.at[slot], in_send.at[kind, i], in_recv.at[kind, slot], device_id)

    def send_in(kind):
        for i in range(pair):
            here = z == worker_z(i)
            copy = in_copy(kind, i, z, {"seq_1": worker_z(i)})

            @pl.when(jnp.logical_not(here))
            def _(copy=copy):
                copy.start()

            @pl.when(here)
            def _(i=i):
                src, dst = ((s_chip, s_arr), (cp_chip, cp_arr))[kind]
                dst[z] = src[i]

    def drain_in(kind):
        for i in range(pair):
            @pl.when(z != worker_z(i))
            def _(i=i):
                in_copy(kind, i, z, {"seq_1": worker_z(i)}).wait_send()

    def wait_in(kind):
        for d in range(1, nz):
            in_copy(kind, 0, modz(d), {"seq_1": modz(d)}).wait_recv()

    def back_copy(kind, i, d):
        src, dst = ((s_back, s_pre), (p_back, p_pre))[kind]
        return remote(src.at[modz(d)], dst.at[i], back_send.at[kind, d], back_recv.at[kind, i], {"seq_1": modz(d)})

    def send_back(kind):
        src, dst = ((s_back, s_pre), (p_back, p_pre))[kind]
        for d in FAR_FIRST:
            if d < nz:
                back_copy(kind, my_head, d).start()
        dst[my_head] = src[z]

    def wait_back(kind, i):
        @pl.when(z != worker_z(i))
        def _():
            back_copy(kind, i, 1).wait_recv()

    def total_copy(kind, d, slot):
        part = (pl.ds(0, 1), pl.ds(1, 2))[kind]
        return remote(
            y_out.at[part], y_in.at[slot, part], y_send.at[kind, d], y_recv.at[kind, slot], {"seq_0": mody(d)}
        )

    def send_totals(kind):
        for d in FAR_FIRST:
            if d < ny:

                @pl.when(y + d < ny)
                def _(d=d):
                    total_copy(kind, d, y).start()

    def wait_totals(kind):
        for d in range(1, ny):

            @pl.when(y >= d)
            def _(d=d):
                total_copy(kind, d, y - d).wait_recv()

    def drain_totals(kind):
        for d in range(1, ny):

            @pl.when(y + d < ny)
            def _(d=d):
                total_copy(kind, d, y).wait_send()

    def s_base_until(limit):
        base = jnp.zeros((DH, DH), F32)
        for r in range(ny - 1):
            base = base + jnp.where(r < limit, y_in[r, 0].astype(F32), 0.0)
        return base

    colour = lax.rem(y + z, 2)
    piece_rows = w.shape[1] // 8

    def rows_of(colour_of, core_of, half, part=None):
        first = colour_of * (4 * piece_rows) + core_of * (2 * piece_rows) + half * piece_rows
        count = piece_rows
        if part is not None:
            count = piece_rows // 2
            first = first + part * count
        return pl.ds(pl.multiple_of(first, count), count)

    def piece(i, colour_of, core_of, part=None):
        offset, half = X_PIECES[i]
        return w.at[modx(offset), rows_of(colour_of, core_of, half, part)]

    def w_copy(number, src, dst, device_id):
        return remote(src, dst, w_send.at[number], w_recv.at[number], device_id)

    def unit(number, part):
        return 2 * number + (part or 0)

    def x_send(number, part):
        offset, half = X_PIECES[number]
        if number < 4:
            rows = rows_of(colour, c, half, part)
            return w_copy(unit(number, part), w_hbm.at[rows], w.at[x, rows], {"head": modx(-offset)})
        src = piece(number - 4, colour, c, part)
        return w_copy(unit(number, part), src, src, {"head": modx(1 if number == 4 else -1)})

    def x_arrival(number, part):
        ref = piece(number, colour, c, part)
        return w_copy(unit(number, part), ref, ref, {"head": modx(1)})

    def plane_copy(number, part, colour_of):
        ref = piece(number, colour_of, c, part)
        step = 1 if X_PIECES[number][1] == 0 else -1
        peer = {"seq_1": modz(step + nz)} if number >= 4 and part == 1 else {"seq_0": mody(step)}
        return w_copy(12 + unit(number, part), ref, ref, peer)

    def core_copy(number, core_of):
        ref = piece(number, colour, core_of)
        return w_copy(24 + number, ref, ref, {"seq_2": 1 - c})

    def core_plane_copy(number, part, core_of):
        ref = piece(number, 1 - colour, core_of, part)
        return w_copy(30 + unit(number, part), ref, ref, {"seq_2": 1 - c})

    def relay_x(*units):
        for number, part in units:
            x_arrival(number, part).wait_recv()
            if number < 2:
                start(x_send(4 + number, part))
            start(plane_copy(number, part, colour))
        for number, part in units:
            if part != 0:
                start(core_copy(number, c))

    def arrive_plane(number):
        for part in PARTS[number]:
            plane_copy(number, part, 1 - colour).wait_recv()
            if number >= 4:
                start(core_plane_copy(number, part, c))
        if number < 4:
            start(core_plane_copy(number, None, c))

    row = lax.broadcasted_iota(jnp.int32, (CHUNK, CHUNK), 0)
    col = lax.broadcasted_iota(jnp.int32, (CHUNK, CHUNK), 1)
    loads[0].wait()
    for h in range(heads):
        first = dot(chunk(k, h, 0), chunk(k, h, 0), 0, 0)
        s_first[h] = first.astype(BF16)
        s_loc[h // pair, h % pair] = (first + dot(chunk(k, h, 1), chunk(k, h, 1), 0, 0)).astype(BF16)
    loads[1].wait()
    loads[2].wait()
    strict, causal = col < row, col <= row
    blocks = [(h, j) for h in range(heads) for j in range(2)]
    for h in range(heads):
        v_t[h] = v[:, h * DH : (h + 1) * DH].T
    scores = [jnp.where(strict, dot(chunk(q, h, j), chunk(k, h, j), 1, 1), 0.0).astype(BF16) for h, j in blocks]
    fs = []
    for n, (h, j) in enumerate(blocks):
        f = dot(scores[n], chunk(k, h, j), 1, 0)
        if j == 1:
            f = f + dot(chunk(q, h, j), s_first[h], 1, 0)
        f_loc[j * CHUNK : (j + 1) * CHUNK, h * DH : (h + 1) * DH] = f
        fs.append(f.astype(BF16))
    for h in range(heads):
        cross = dot(v_t[h], q[:, h * DH : (h + 1) * DH], 1, 0)
        pairs = dot(v_t[h, :, :CHUNK], fs[2 * h], 1, 0) + dot(v_t[h, :, CHUNK:], fs[2 * h + 1], 1, 0)
        cp_loc[h // pair, h % pair, 0] = cross.astype(BF16)
        cp_loc[h // pair, h % pair, 1] = pairs.astype(BF16)

    pl.semaphore_wait(barrier, nx - 1 + ny - 1 + 1 + pair - is_worker.astype(jnp.int32))
    for copy in loads[3:]:
        copy.start()
    sibling = {"seq_2": 1 - c}
    s_core = remote(s_loc.at[1 - c], s_sib, core_send.at[0], core_recv.at[0], sibling)
    cp_core = remote(cp_loc.at[1 - c], cp_sib, core_send.at[1], core_recv.at[1], sibling)
    start(s_core)
    start(cp_core)
    for number, part in ((0, 0), (1, 0), (0, 1), (1, 1), (2, None), (3, None)):
        start(x_send(number, part))
    s_core.wait_recv()
    for i in range(pair):
        s_chip[i] = (s_loc[c, i].astype(F32) + s_sib[i].astype(F32)).astype(BF16)
    send_in(0)
    cp_core.wait_recv()
    for i in range(pair):
        mine, other = cp_loc[c, i], cp_sib[i]
        early = jnp.where(c == 0, s_loc[c, i], s_sib[i])
        late = jnp.where(c == 0, other[0], mine[0])
        cp_chip[i, 0] = (mine[0].astype(F32) + other[0].astype(F32)).astype(BF16)
        cp_chip[i, 1] = (mine[1].astype(F32) + other[1].astype(F32) + dot(late, early, 1, 0)).astype(BF16)
    send_in(1)

    relay_x((0, 0), (1, 0))

    @pl.when(is_worker)
    def _():
        wait_in(0)
        total = jnp.zeros((DH, DH), F32)
        for r in range(nz):
            s_run[r] = total
            total = total + s_arr[r].astype(F32)
        y_out[0] = total.astype(BF16)
        send_totals(0)
        y_in[y, 0] = total.astype(BF16)

    relay_x((0, 1), (1, 1))

    @pl.when(is_worker)
    def _():
        wait_in(1)
        pairs = jnp.zeros((DH, DH), F32)
        cross = jnp.zeros((DH, DH), F32)
        for r in range(nz):
            p_run[r] = pairs
            c_run[r] = cross.astype(BF16)
            pairs = pairs + (cp_arr[r, 1].astype(F32) + dot(cp_arr[r, 0], s_run[r].astype(BF16), 1, 0))
            cross = cross + cp_arr[r, 0].astype(F32)
        y_out[1] = cross.astype(BF16)
        y_out[2] = pairs.astype(BF16)
        send_totals(1)
        y_in[y, 1] = cross.astype(BF16)
        y_in[y, 2] = pairs.astype(BF16)
        wait_totals(0)
        s_base = s_base_until(y)
        for r in range(nz):
            s_back[r] = (s_run[r] + s_base).astype(BF16)
        send_back(0)
        s_base = s_base.astype(BF16)
        for r in range(nz):
            p_run[r] = p_run[r] + dot(c_run[r], s_base, 1, 0)
        before = [s_base_until(r).astype(BF16) for r in range(ny - 1)]
        wait_totals(1)
        p_base = jnp.zeros((DH, DH), F32)
        for r in range(ny - 1):
            line = y_in[r, 2].astype(F32) + dot(y_in[r, 1], before[r], 1, 0)
            p_base = p_base + jnp.where(r < y, line, 0.0)
        for r in range(nz):
            p_back[r] = (p_run[r] + p_base).astype(BF16)
        send_back(1)

    for i in range(pair):
        wait_back(0, i)
        mine, other = cp_loc[c, i], cp_sib[i]
        chip = s_pre[i]
        early = jnp.where(c == 0, s_loc[c, i], s_sib[i])
        later = (chip.astype(F32) + early.astype(F32)).astype(BF16)
        s_mine[c, i] = jnp.where(c == 0, chip, later)
        s_other[i] = jnp.where(c == 0, later, chip)
        p_step[i] = jnp.where(c == 0, mine[1], other[1]).astype(F32) + dot(
            jnp.where(c == 0, mine[0], other[0]), chip, 1, 0
        )
    s_swap = remote(s_other, s_mine.at[c], core_send.at[2], core_recv.at[2], sibling)
    start(s_swap)
    relay_x((2, None), (3, None))
    arrive_plane(0)
    arrive_plane(1)
    s_swap_in = remote(s_other, s_mine.at[1 - c], core_send.at[2], core_recv.at[2], sibling)
    s_swap_in.wait_recv()

    fs = []
    for h, j in blocks:
        f = chunk(f_loc, h, j) + dot(chunk(q, h, j), s_mine[h // pair, h % pair], 1, 0)
        fs.append(f.astype(BF16))
    mixing = [
        jnp.where(causal, dot(chunk(q, h, j), fs[n], 1, 1), 0.0).astype(BF16) for n, (h, j) in enumerate(blocks)
    ]
    for n, (h, j) in enumerate(blocks):
        o_part[j * CHUNK : (j + 1) * CHUNK, h * DH : (h + 1) * DH] = dot(mixing[n], chunk(v, h, j), 1, 0)
    for h in range(heads):
        p_first[h // pair, h % pair] = dot(v_t[h, :, :CHUNK], fs[2 * h], 1, 0)
    relay_x((4, 0), (5, 0), (4, 1), (5, 1))

    rows_x = tokens // nx
    loads[4].wait()

    def swap_p(i, slot):
        return remote(p_other.at[i], p_mine.at[slot, i], core_send.at[3 + i], core_recv.at[3 + i], sibling)

    def head_cols(g, i):
        return pl.ds(pl.multiple_of(g * (pair * DH) + i * DH, DH), DH)

    def n_copy(d, g, i, slot):
        cols = head_cols(g, i)
        number = g * pair + i
        return remote(
            n_out.at[d, :, cols], n_in.at[slot, :, cols], n_send.at[d, number], n_recv.at[slot, number], {"head": modx(d)}
        )

    for i in range(pair):
        wait_back(1, i)
        chip = p_pre[i]
        later = (chip.astype(F32) + p_step[i]).astype(BF16)
        p_mine[c, i] = jnp.where(c == 0, chip, later)
        p_other[i] = jnp.where(c == 0, later, chip)
        start(swap_p(i, c))
        for g in (c, 1 - c):
            if g is not c:
                swap_p(i, g).wait_recv()
            cols = head_cols(g, i)
            p_h = p_mine[g, i]
            p_fin[0] = p_h
            p_fin[1] = (p_h.astype(F32) + p_first[g, i]).astype(BF16)
            for d in (2, 1, 3, 0):
                target = modx(d)
                rows = pl.ds(pl.multiple_of(target * rows_x, rows_x), rows_x)
                part = target // (CHUNK // rows_x)
                attended = o_part[rows, cols] + dot(q[rows, cols], p_fin[part], 1, 1)
                mean_square = jnp.mean(attended * attended, axis=-1, keepdims=True)
                n_out[d, :, cols] = (attended * lax.rsqrt(mean_square + EPS) * gain[:, cols]).astype(BF16)
                if d:
                    start(n_copy(d, g, i, x))

    arrive_plane(2)
    arrive_plane(3)

    loads[3].wait()
    tile = 512
    n_cols = out_ref.shape[1]

    def project(rows_in, slot, quarter, first, last):
        for begin in range(0, n_cols, tile):
            cols = slice(begin, begin + tile)
            part = dot(rows_in[slot], w[quarter, :, cols], 1, 0)
            if not first:
                part = part + acc[:, cols]
            if last:
                out_ref[:, cols] = part.astype(BF16)
            else:
                acc[:, cols] = part

    project(n_out, 0, x, True, False)
    arrive_plane(4)
    arrive_plane(5)
    for offset in (-1, 1, 2):
        quarter = modx(offset)
        for number, (of, _) in enumerate(X_PIECES):
            if of == offset:
                core_copy(number, 1 - c).wait_recv()
                for part in PARTS[number] if number >= 4 else (None,):
                    core_plane_copy(number, part, 1 - c).wait_recv()
        for head in range(heads):
            n_copy(offset % nx, head // pair, head % pair, quarter).wait_recv()
        project(n_in, quarter, quarter, False, offset == 2)

    for wait in pending:
        wait()
    drain_in(0)
    drain_in(1)

    @pl.when(is_worker)
    def _():
        for kind in range(2):
            for d in range(1, nz):
                back_copy(kind, my_head, d).wait_send()
            drain_totals(kind)


def shards(ny, nz, nx, queries, key_vectors, value_vectors, norm_gain, out_weight):
    tokens, width = queries.shape
    heads = width // DH
    pair = heads // 2
    depth, n_cols = out_weight.shape

    def matrices(*lead, kind=BF16):
        return pltpu.VMEM(lead + (DH, DH), kind)

    operands = (queries, key_vectors, value_vectors, norm_gain.reshape(1, width), out_weight)
    return pl.pallas_call(
        functools.partial(kernel, ny, nz, nx),
        out_shape=jax.ShapeDtypeStruct((tokens // nx, n_cols), BF16),
        in_specs=[pl.BlockSpec(memory_space=pltpu.HBM)] * 5,
        out_specs=pl.BlockSpec(memory_space=pltpu.VMEM),
        scratch_shapes=[
            pltpu.VMEM((tokens, width), BF16),
            pltpu.VMEM((tokens, width), BF16),
            pltpu.VMEM((tokens, width), BF16),
            pltpu.VMEM((nx, depth, n_cols), BF16),
            pltpu.VMEM((1, width), F32),
            matrices(heads),
            matrices(2, pair),
            matrices(2, pair, 2),
            matrices(pair),
            matrices(pair, 2),
            matrices(pair),
            matrices(pair, 2),
            matrices(nz),
            matrices(nz, 2),
            matrices(nz, kind=F32),
            matrices(nz, kind=F32),
            matrices(nz),
            matrices(nz),
            matrices(nz),
            matrices(3),
            matrices(ny, 3),
            matrices(pair),
            matrices(pair),
            matrices(pair, kind=F32),
            matrices(pair),
            matrices(pair),
            matrices(2, pair),
            matrices(2, pair),
            pltpu.VMEM((heads, DH, tokens), BF16),
            pltpu.VMEM((tokens, width), F32),
            matrices(2, pair, kind=F32),
            pltpu.VMEM((tokens, width), F32),
            matrices(2),
            pltpu.VMEM((nx, tokens // nx, width), BF16),
            pltpu.VMEM((nx, tokens // nx, width), BF16),
            pltpu.VMEM((tokens // nx, n_cols), F32),
            pltpu.SemaphoreType.DMA((5,)),
            pltpu.SemaphoreType.DMA((3 + pair,)),
            pltpu.SemaphoreType.DMA((3 + pair,)),
            pltpu.SemaphoreType.DMA((2, pair)),
            pltpu.SemaphoreType.DMA((2, nz)),
            pltpu.SemaphoreType.DMA((2, nz)),
            pltpu.SemaphoreType.DMA((2, pair)),
            pltpu.SemaphoreType.DMA((2, ny)),
            pltpu.SemaphoreType.DMA((2, ny)),
            pltpu.SemaphoreType.DMA((nx, heads)),
            pltpu.SemaphoreType.DMA((nx, heads)),
            pltpu.SemaphoreType.DMA((42,)),
            pltpu.SemaphoreType.DMA((42,)),
        ],
        compiler_params=pltpu.CompilerParams(
            collective_id=0, has_side_effects=True, vmem_limit_bytes=48 * 1024 * 1024
        ),
    )(*[pltpu.with_memory_space_constraint(array, pltpu.HBM) for array in operands])


def solution(mesh):
    seq, nx = mesh.shape["seq"], mesh.shape["head"]
    ny = 4 if seq == 64 else 2
    nz = seq // (2 * ny)
    split = Mesh(mesh.devices.reshape(ny, nz, 2, nx), SEQ_HEAD)
    in_specs = (P(SEQ, "head"), P(SEQ, "head"), P(SEQ, "head"), P("head"), P("head", None))
    out_specs = P(SEQ_HEAD, None)
    return jax.shard_map(
        functools.partial(shards, ny, nz, nx), mesh=split, in_specs=in_specs, out_specs=out_specs, check_vma=False
    )
```

```python
import functools

import jax
import jax.numpy as jnp
from jax import lax
from jax.experimental import pallas as pl
from jax.experimental.pallas import tpu as pltpu
from jax.sharding import Mesh
from jax.sharding import PartitionSpec as P

DH = 128
SEQ = ("seq_0", "seq_1", "seq_2")
SEQ_HEAD = ("seq_0", "seq_1", "seq_2", "head")
F32 = jnp.float32
BF16 = jnp.bfloat16
CHUNK = 256
EPS = 1e-06
FAR_FIRST = (4, 3, 5, 2, 6, 1, 7)

PARTS = ((0, 1), (0, 1), (None,), (None,), (0, 1), (0, 1))
X_PIECES = ((-1, 0), (1, 1), (-1, 1), (1, 0), (2, 0), (2, 1))


def dot(a, b, ca, cb):
    return lax.dot_general(a, b, (((ca,), (cb,)), ((), ())), preferred_element_type=F32)


def kernel(
    ny,
    nz,
    nx,
    q_hbm,
    k_hbm,
    v_hbm,
    gain_hbm,
    w_hbm,
    out_ref,
    q,
    k,
    v,
    w,
    gain,
    s_first,
    s_loc,
    cp_loc,
    s_sib,
    cp_sib,
    s_chip,
    cp_chip,
    s_arr,
    cp_arr,
    s_run,
    p_run,
    c_run,
    s_back,
    p_back,
    y_out,
    y_in,
    s_pre,
    p_pre,
    p_step,
    s_other,
    p_other,
    s_mine,
    p_mine,
    v_t,
    f_loc,
    p_first,
    o_part,
    p_fin,
    n_out,
    n_in,
    acc,
    load_sem,
    core_send,
    core_recv,
    in_send,
    in_recv,
    back_send,
    back_recv,
    y_send,
    y_recv,
    n_send,
    n_recv,
    w_send,
    w_recv,
):
    tokens, width = q.shape
    heads = width // DH
    pair = heads // 2
    y, z, c, x = (lax.axis_index(name) for name in SEQ_HEAD)

    def modx(i):
        return lax.rem(x + i + nx, nx)

    def mody(i):
        return lax.rem(y + i + ny, ny)

    def modz(i):
        return lax.rem(z + i, nz)

    pending = []

    def remote(src, dst, send_sem, recv_sem, device_id):
        return pltpu.make_async_remote_copy(
            src_ref=src,
            dst_ref=dst,
            send_sem=send_sem,
            recv_sem=recv_sem,
            device_id=device_id,
            device_id_type=pl.DeviceIdType.MESH,
        )

    def start(copy):
        copy.start()
        pending.append(copy.wait_send)

    spacing = nz // heads
    is_worker = (lax.rem(z, spacing) == 0) & (z // (spacing * pair) == c)
    my_head = lax.rem(z // spacing, pair)

    barrier = pltpu.get_barrier_semaphore()

    def greet(peer):
        pl.semaphore_signal(barrier, inc=1, device_id=peer, device_id_type=pl.DeviceIdType.MESH)

    for d in range(1, ny):
        greet({"seq_0": mody(d)})
    for d in range(1, nx):
        greet({"head": modx(d)})
    greet({"seq_2": 1 - c})

    @pl.when(is_worker)
    def _():
        for d in FAR_FIRST:
            if d < nz:
                greet({"seq_1": modz(d)})

    loads = [
        pltpu.make_async_copy(src, dst, load_sem.at[i])
        for i, (src, dst) in enumerate(((k_hbm, k), (q_hbm, q), (v_hbm, v), (w_hbm, w.at[x]), (gain_hbm, gain)))
    ]
    for copy in loads[:3]:
        copy.start()

    def chunk(ref, h, j):
        return ref[j * CHUNK : (j + 1) * CHUNK, h * DH : (h + 1) * DH]

    def worker_z(i):
        return (c * pair + i) * spacing

    def in_copy(kind, i, slot, device_id):
        src, dst = ((s_chip, s_arr), (cp_chip, cp_arr))[kind]
        return remote(src.at[i], dst.at[slot], in_send.at[kind, i], in_recv.at[kind, slot], device_id)

    def send_in(kind, i):
        here = z == worker_z(i)

        @pl.when(jnp.logical_not(here))
        def _():
            in_copy(kind, i, z, {"seq_1": worker_z(i)}).start()

        @pl.when(here)
        def _():
            src, dst = ((s_chip, s_arr), (cp_chip, cp_arr))[kind]
            dst[z] = src[i]

    def drain_in(kind):
        for i in range(pair):
            @pl.when(z != worker_z(i))
            def _(i=i):
                in_copy(kind, i, z, {"seq_1": worker_z(i)}).wait_send()

    def wait_in(kind):
        for d in range(1, nz):
            in_copy(kind, 0, modz(d), {"seq_1": modz(d)}).wait_recv()

    def back_copy(kind, i, d):
        src, dst = ((s_back, s_pre), (p_back, p_pre))[kind]
        return remote(src.at[modz(d)], dst.at[i], back_send.at[kind, d], back_recv.at[kind, i], {"seq_1": modz(d)})

    def send_back(kind):
        src, dst = ((s_back, s_pre), (p_back, p_pre))[kind]
        for d in FAR_FIRST:
            if d < nz:
                back_copy(kind, my_head, d).start()
        dst[my_head] = src[z]

    def wait_back(kind, i):
        @pl.when(z != worker_z(i))
        def _():
            back_copy(kind, i, 1).wait_recv()

    def total_copy(kind, d, slot):
        part = (pl.ds(0, 1), pl.ds(1, 2))[kind]
        return remote(
            y_out.at[part], y_in.at[slot, part], y_send.at[kind, d], y_recv.at[kind, slot], {"seq_0": mody(d)}
        )

    def send_totals(kind):
        for d in FAR_FIRST:
            if d < ny:

                @pl.when(y + d < ny)
                def _(d=d):
                    total_copy(kind, d, y).start()

    def wait_totals(kind):
        for d in range(1, ny):

            @pl.when(y >= d)
            def _(d=d):
                total_copy(kind, d, y - d).wait_recv()

    def drain_totals(kind):
        for d in range(1, ny):

            @pl.when(y + d < ny)
            def _(d=d):
                total_copy(kind, d, y).wait_send()

    def s_base_until(limit):
        base = jnp.zeros((DH, DH), F32)
        for r in range(ny - 1):
            base = base + jnp.where(r < limit, y_in[r, 0].astype(F32), 0.0)
        return base

    colour = lax.rem(y + z, 2)
    piece_rows = w.shape[1] // 8

    def rows_of(colour_of, core_of, half, part=None):
        first = colour_of * (4 * piece_rows) + core_of * (2 * piece_rows) + half * piece_rows
        count = piece_rows
        if part is not None:
            count = piece_rows // 2
            first = first + part * count
        return pl.ds(pl.multiple_of(first, count), count)

    def piece(i, colour_of, core_of, part=None):
        offset, half = X_PIECES[i]
        return w.at[modx(offset), rows_of(colour_of, core_of, half, part)]

    def w_copy(number, src, dst, device_id):
        return remote(src, dst, w_send.at[number], w_recv.at[number], device_id)

    def unit(number, part):
        return 2 * number + (part or 0)

    def x_send(number, part):
        offset, half = X_PIECES[number]
        if number < 4:
            rows = rows_of(colour, c, half, part)
            return w_copy(unit(number, part), w_hbm.at[rows], w.at[x, rows], {"head": modx(-offset)})
        src = piece(number - 4, colour, c, part)
        return w_copy(unit(number, part), src, src, {"head": modx(1 if number == 4 else -1)})

    def x_arrival(number, part):
        ref = piece(number, colour, c, part)
        return w_copy(unit(number, part), ref, ref, {"head": modx(1)})

    def plane_copy(number, part, colour_of):
        ref = piece(number, colour_of, c, part)
        step = 1 if X_PIECES[number][1] == 0 else -1
        peer = {"seq_1": modz(step + nz)} if number >= 4 and part == 1 else {"seq_0": mody(step)}
        return w_copy(12 + unit(number, part), ref, ref, peer)

    def core_copy(number, core_of):
        ref = piece(number, colour, core_of)
        return w_copy(24 + number, ref, ref, {"seq_2": 1 - c})

    def core_plane_copy(number, part, core_of):
        ref = piece(number, 1 - colour, core_of, part)
        return w_copy(30 + unit(number, part), ref, ref, {"seq_2": 1 - c})

    def relay_x(*units):
        for number, part in units:
            x_arrival(number, part).wait_recv()
            if number < 2:
                start(x_send(4 + number, part))
            start(plane_copy(number, part, colour))
        for number, part in units:
            if part != 0:
                start(core_copy(number, c))

    def arrive_plane(number):
        for part in PARTS[number]:
            plane_copy(number, part, 1 - colour).wait_recv()
            if number >= 4:
                start(core_plane_copy(number, part, c))
        if number < 4:
            start(core_plane_copy(number, None, c))

    row = lax.broadcasted_iota(jnp.int32, (CHUNK, CHUNK), 0)
    col = lax.broadcasted_iota(jnp.int32, (CHUNK, CHUNK), 1)
    loads[0].wait()
    for h in range(heads):
        first = dot(chunk(k, h, 0), chunk(k, h, 0), 0, 0)
        s_first[h] = first.astype(BF16)
        s_loc[h // pair, h % pair] = (first + dot(chunk(k, h, 1), chunk(k, h, 1), 0, 0)).astype(BF16)
    loads[1].wait()
    loads[2].wait()
    strict, causal = col < row, col <= row
    blocks = [(h, j) for h in range(heads) for j in range(2)]
    for h in range(heads):
        v_t[h] = v[:, h * DH : (h + 1) * DH].T
    scores = [jnp.where(strict, dot(chunk(q, h, j), chunk(k, h, j), 1, 1), 0.0).astype(BF16) for h, j in blocks]
    fs = []
    for n, (h, j) in enumerate(blocks):
        f = dot(scores[n], chunk(k, h, j), 1, 0)
        if j == 1:
            f = f + dot(chunk(q, h, j), s_first[h], 1, 0)
        f_loc[j * CHUNK : (j + 1) * CHUNK, h * DH : (h + 1) * DH] = f
        fs.append(f.astype(BF16))
    for h in range(heads):
        cross = dot(v_t[h], q[:, h * DH : (h + 1) * DH], 1, 0)
        pairs = dot(v_t[h, :, :CHUNK], fs[2 * h], 1, 0) + dot(v_t[h, :, CHUNK:], fs[2 * h + 1], 1, 0)
        cp_loc[h // pair, h % pair, 0] = cross.astype(BF16)
        cp_loc[h // pair, h % pair, 1] = pairs.astype(BF16)

    pl.semaphore_wait(barrier, nx - 1 + ny - 1 + 1 + pair - is_worker.astype(jnp.int32))
    for copy in loads[3:]:
        copy.start()
    sibling = {"seq_2": 1 - c}
    s_core = remote(s_loc.at[1 - c], s_sib, core_send.at[0], core_recv.at[0], sibling)
    cp_core = remote(cp_loc.at[1 - c], cp_sib, core_send.at[1], core_recv.at[1], sibling)
    start(s_core)
    start(cp_core)
    for number, part in ((0, 0), (1, 0), (0, 1), (1, 1), (2, None), (3, None)):
        start(x_send(number, part))
    s_core.wait_recv()
    for i in range(pair):
        s_chip[i] = (s_loc[c, i].astype(F32) + s_sib[i].astype(F32)).astype(BF16)
        send_in(0, i)
        if i == 0:
            cp_core.wait_recv()
        mine, other = cp_loc[c, i], cp_sib[i]
        early = jnp.where(c == 0, s_loc[c, i], s_sib[i])
        late = jnp.where(c == 0, other[0], mine[0])
        cp_chip[i, 0] = (mine[0].astype(F32) + other[0].astype(F32)).astype(BF16)
        cp_chip[i, 1] = (mine[1].astype(F32) + other[1].astype(F32) + dot(late, early, 1, 0)).astype(BF16)
        send_in(1, i)

    relay_x((0, 0), (1, 0))

    @pl.when(is_worker)
    def _():
        wait_in(0)
        total = jnp.zeros((DH, DH), F32)
        for r in range(nz):
            s_run[r] = total
            total = total + s_arr[r].astype(F32)
        y_out[0] = total.astype(BF16)
        send_totals(0)
        y_in[y, 0] = total.astype(BF16)

    relay_x((0, 1), (1, 1))

    @pl.when(is_worker)
    def _():
        wait_in(1)
        pairs = jnp.zeros((DH, DH), F32)
        cross = jnp.zeros((DH, DH), F32)
        for r in range(nz):
            p_run[r] = pairs
            c_run[r] = cross.astype(BF16)
            pairs = pairs + (cp_arr[r, 1].astype(F32) + dot(cp_arr[r, 0], s_run[r].astype(BF16), 1, 0))
            cross = cross + cp_arr[r, 0].astype(F32)
        y_out[1] = cross.astype(BF16)
        y_out[2] = pairs.astype(BF16)
        send_totals(1)
        y_in[y, 1] = cross.astype(BF16)
        y_in[y, 2] = pairs.astype(BF16)
        wait_totals(0)
        s_base = s_base_until(y)
        for r in range(nz):
            s_back[r] = (s_run[r] + s_base).astype(BF16)
        send_back(0)
        s_base = s_base.astype(BF16)
        for r in range(nz):
            p_run[r] = p_run[r] + dot(c_run[r], s_base, 1, 0)
        before = [s_base_until(r).astype(BF16) for r in range(ny - 1)]
        wait_totals(1)
        p_base = jnp.zeros((DH, DH), F32)
        for r in range(ny - 1):
            line = y_in[r, 2].astype(F32) + dot(y_in[r, 1], before[r], 1, 0)
            p_base = p_base + jnp.where(r < y, line, 0.0)
        for r in range(nz):
            p_back[r] = (p_run[r] + p_base).astype(BF16)
        send_back(1)

    def swap_s(i, slot):
        return remote(s_other.at[i], s_mine.at[slot, i], core_send.at[2 + i], core_recv.at[2 + i], sibling)

    for i in range(pair):
        wait_back(0, i)
        mine, other = cp_loc[c, i], cp_sib[i]
        chip = s_pre[i]
        early = jnp.where(c == 0, s_loc[c, i], s_sib[i])
        later = (chip.astype(F32) + early.astype(F32)).astype(BF16)
        s_mine[c, i] = jnp.where(c == 0, chip, later)
        s_other[i] = jnp.where(c == 0, later, chip)
        p_step[i] = jnp.where(c == 0, mine[1], other[1]).astype(F32) + dot(
            jnp.where(c == 0, mine[0], other[0]), chip, 1, 0
        )
        start(swap_s(i, c))
    relay_x((2, None), (3, None))
    arrive_plane(0)
    arrive_plane(1)

    def local_out(i):
        both = [(h, j) for h in (i, pair + i) for j in range(2)]
        fs = []
        for h, j in both:
            f = chunk(f_loc, h, j) + dot(chunk(q, h, j), s_mine[h // pair, h % pair], 1, 0)
            fs.append(f.astype(BF16))
        mixing = [
            jnp.where(causal, dot(chunk(q, h, j), fs[n], 1, 1), 0.0).astype(BF16) for n, (h, j) in enumerate(both)
        ]
        for n, (h, j) in enumerate(both):
            o_part[j * CHUNK : (j + 1) * CHUNK, h * DH : (h + 1) * DH] = dot(mixing[n], chunk(v, h, j), 1, 0)
        for n, h in enumerate((i, pair + i)):
            p_first[h // pair, h % pair] = dot(v_t[h, :, :CHUNK], fs[2 * n], 1, 0)

    swap_s(0, 1 - c).wait_recv()
    local_out(0)

    rows_x = tokens // nx
    loads[4].wait()

    def swap_p(i, slot):
        return remote(p_other.at[i], p_mine.at[slot, i], core_send.at[2 + pair + i], core_recv.at[2 + pair + i], sibling)

    def head_cols(g, i):
        return pl.ds(pl.multiple_of(g * (pair * DH) + i * DH, DH), DH)

    def n_copy(d, g, i, slot):
        cols = head_cols(g, i)
        number = g * pair + i
        return remote(
            n_out.at[d, :, cols], n_in.at[slot, :, cols], n_send.at[d, number], n_recv.at[slot, number], {"head": modx(d)}
        )

    for i in range(pair):
        wait_back(1, i)
        chip = p_pre[i]
        later = (chip.astype(F32) + p_step[i]).astype(BF16)
        p_mine[c, i] = jnp.where(c == 0, chip, later)
        p_other[i] = jnp.where(c == 0, later, chip)
        start(swap_p(i, c))
        for g in (c, 1 - c):
            if g is not c:
                if i + 1 < pair:
                    swap_s(i + 1, g).wait_recv()
                    local_out(i + 1)
                swap_p(i, g).wait_recv()
            cols = head_cols(g, i)
            p_h = p_mine[g, i]
            p_fin[0] = p_h
            p_fin[1] = (p_h.astype(F32) + p_first[g, i]).astype(BF16)
            for d in (2, 1, 3, 0):
                target = modx(d)
                rows = pl.ds(pl.multiple_of(target * rows_x, rows_x), rows_x)
                part = target // (CHUNK // rows_x)
                attended = o_part[rows, cols] + dot(q[rows, cols], p_fin[part], 1, 1)
                mean_square = jnp.mean(attended * attended, axis=-1, keepdims=True)
                n_out[d, :, cols] = (attended * lax.rsqrt(mean_square + EPS) * gain[:, cols]).astype(BF16)
                if d:
                    start(n_copy(d, g, i, x))
        if i == 0:
            relay_x((4, 0), (5, 0), (4, 1), (5, 1))

    arrive_plane(2)
    arrive_plane(3)

    loads[3].wait()
    tile = 512
    n_cols = out_ref.shape[1]

    def project(rows_in, slot, quarter, first, last):
        for begin in range(0, n_cols, tile):
            cols = slice(begin, begin + tile)
            part = dot(rows_in[slot], w[quarter, :, cols], 1, 0)
            if not first:
                part = part + acc[:, cols]
            if last:
                out_ref[:, cols] = part.astype(BF16)
            else:
                acc[:, cols] = part

    project(n_out, 0, x, True, False)
    arrive_plane(4)
    arrive_plane(5)
    for offset in (-1, 1, 2):
        quarter = modx(offset)
        for number, (of, _) in enumerate(X_PIECES):
            if of == offset:
                core_copy(number, 1 - c).wait_recv()
                for part in PARTS[number] if number >= 4 else (None,):
                    core_plane_copy(number, part, 1 - c).wait_recv()
        for head in range(heads):
            n_copy(offset % nx, head // pair, head % pair, quarter).wait_recv()
        project(n_in, quarter, quarter, False, offset == 2)

    for wait in pending:
        wait()
    drain_in(0)
    drain_in(1)

    @pl.when(is_worker)
    def _():
        for kind in range(2):
            for d in range(1, nz):
                back_copy(kind, my_head, d).wait_send()
            drain_totals(kind)


def shards(ny, nz, nx, queries, key_vectors, value_vectors, norm_gain, out_weight):
    tokens, width = queries.shape
    heads = width // DH
    pair = heads // 2
    depth, n_cols = out_weight.shape

    def matrices(*lead, kind=BF16):
        return pltpu.VMEM(lead + (DH, DH), kind)

    operands = (queries, key_vectors, value_vectors, norm_gain.reshape(1, width), out_weight)
    return pl.pallas_call(
        functools.partial(kernel, ny, nz, nx),
        out_shape=jax.ShapeDtypeStruct((tokens // nx, n_cols), BF16),
        in_specs=[pl.BlockSpec(memory_space=pltpu.HBM)] * 5,
        out_specs=pl.BlockSpec(memory_space=pltpu.VMEM),
        scratch_shapes=[
            pltpu.VMEM((tokens, width), BF16),
            pltpu.VMEM((tokens, width), BF16),
            pltpu.VMEM((tokens, width), BF16),
            pltpu.VMEM((nx, depth, n_cols), BF16),
            pltpu.VMEM((1, width), F32),
            matrices(heads),
            matrices(2, pair),
            matrices(2, pair, 2),
            matrices(pair),
            matrices(pair, 2),
            matrices(pair),
            matrices(pair, 2),
            matrices(nz),
            matrices(nz, 2),
            matrices(nz, kind=F32),
            matrices(nz, kind=F32),
            matrices(nz),
            matrices(nz),
            matrices(nz),
            matrices(3),
            matrices(ny, 3),
            matrices(pair),
            matrices(pair),
            matrices(pair, kind=F32),
            matrices(pair),
            matrices(pair),
            matrices(2, pair),
            matrices(2, pair),
            pltpu.VMEM((heads, DH, tokens), BF16),
            pltpu.VMEM((tokens, width), F32),
            matrices(2, pair, kind=F32),
            pltpu.VMEM((tokens, width), F32),
            matrices(2),
            pltpu.VMEM((nx, tokens // nx, width), BF16),
            pltpu.VMEM((nx, tokens // nx, width), BF16),
            pltpu.VMEM((tokens // nx, n_cols), F32),
            pltpu.SemaphoreType.DMA((5,)),
            pltpu.SemaphoreType.DMA((2 + 2 * pair,)),
            pltpu.SemaphoreType.DMA((2 + 2 * pair,)),
            pltpu.SemaphoreType.DMA((2, pair)),
            pltpu.SemaphoreType.DMA((2, nz)),
            pltpu.SemaphoreType.DMA((2, nz)),
            pltpu.SemaphoreType.DMA((2, pair)),
            pltpu.SemaphoreType.DMA((2, ny)),
            pltpu.SemaphoreType.DMA((2, ny)),
            pltpu.SemaphoreType.DMA((nx, heads)),
            pltpu.SemaphoreType.DMA((nx, heads)),
            pltpu.SemaphoreType.DMA((42,)),
            pltpu.SemaphoreType.DMA((42,)),
        ],
        compiler_params=pltpu.CompilerParams(
            collective_id=0, has_side_effects=True, vmem_limit_bytes=48 * 1024 * 1024
        ),
    )(*[pltpu.with_memory_space_constraint(array, pltpu.HBM) for array in operands])


def solution(mesh):
    seq, nx = mesh.shape["seq"], mesh.shape["head"]
    ny = 4 if seq == 64 else 2
    nz = seq // (2 * ny)
    split = Mesh(mesh.devices.reshape(ny, nz, 2, nx), SEQ_HEAD)
    in_specs = (P(SEQ, "head"), P(SEQ, "head"), P(SEQ, "head"), P("head"), P("head", None))
    out_specs = P(SEQ_HEAD, None)
    return jax.shard_map(
        functools.partial(shards, ny, nz, nx), mesh=split, in_specs=in_specs, out_specs=out_specs, check_vma=False
    )
```

```python
import functools

import jax
import jax.numpy as jnp
from jax import lax
from jax.experimental import pallas as pl
from jax.experimental.pallas import tpu as pltpu
from jax.sharding import Mesh
from jax.sharding import PartitionSpec as P

DH = 128
SEQ = ("seq_0", "seq_1", "seq_2")
SEQ_HEAD = ("seq_0", "seq_1", "seq_2", "head")
F32 = jnp.float32
BF16 = jnp.bfloat16
CHUNK = 256
EPS = 1e-06
FAR_FIRST = (4, 3, 5, 2, 6, 1, 7)

PARTS = ((0, 1), (0, 1), (None,), (None,), (0, 1), (0, 1))
X_PIECES = ((-1, 0), (1, 1), (-1, 1), (1, 0), (2, 0), (2, 1))


def dot(a, b, ca, cb):
    return lax.dot_general(a, b, (((ca,), (cb,)), ((), ())), preferred_element_type=F32)


def kernel(
    ny,
    nz,
    nx,
    q_hbm,
    k_hbm,
    v_hbm,
    gain_hbm,
    w_hbm,
    out_ref,
    q,
    k,
    v,
    w,
    gain,
    s_first,
    s_loc,
    cp_loc,
    s_sib,
    cp_sib,
    s_chip,
    cp_chip,
    s_arr,
    cp_arr,
    s_run,
    p_run,
    c_run,
    s_back,
    p_back,
    y_out,
    y_in,
    s_pre,
    p_pre,
    p_step,
    s_other,
    p_other,
    s_mine,
    p_mine,
    v_t,
    f_loc,
    p_first,
    o_part,
    p_fin,
    n_out,
    n_in,
    acc,
    load_sem,
    core_send,
    core_recv,
    in_send,
    in_recv,
    back_send,
    back_recv,
    y_send,
    y_recv,
    n_send,
    n_recv,
    w_send,
    w_recv,
):
    tokens, width = q.shape
    heads = width // DH
    pair = heads // 2
    y, z, c, x = (lax.axis_index(name) for name in SEQ_HEAD)

    def modx(i):
        return lax.rem(x + i + nx, nx)

    def mody(i):
        return lax.rem(y + i + ny, ny)

    def modz(i):
        return lax.rem(z + i, nz)

    pending = []

    def remote(src, dst, send_sem, recv_sem, device_id):
        return pltpu.make_async_remote_copy(
            src_ref=src,
            dst_ref=dst,
            send_sem=send_sem,
            recv_sem=recv_sem,
            device_id=device_id,
            device_id_type=pl.DeviceIdType.MESH,
        )

    def start(copy):
        copy.start()
        pending.append(copy.wait_send)

    spacing = nz // heads
    is_worker = (lax.rem(z, spacing) == 0) & (z // (spacing * pair) == c)
    my_head = lax.rem(z // spacing, pair)

    barrier = pltpu.get_barrier_semaphore()

    def greet(peer):
        pl.semaphore_signal(barrier, inc=1, device_id=peer, device_id_type=pl.DeviceIdType.MESH)

    for d in range(1, ny):
        greet({"seq_0": mody(d)})
    for d in range(1, nx):
        greet({"head": modx(d)})
    greet({"seq_2": 1 - c})

    is_first = (y == 0) & (z == 0)

    @pl.when((y == 0) & ((z == 1) | (z == nz - 1)))
    def _():
        greet({"seq_1": 0})

    @pl.when(is_worker)
    def _():
        for d in FAR_FIRST:
            if d < nz:
                greet({"seq_1": modz(d)})

    loads = [
        pltpu.make_async_copy(src, dst, load_sem.at[i])
        for i, (src, dst) in enumerate(((k_hbm, k), (q_hbm, q), (v_hbm, v), (w_hbm, w.at[x]), (gain_hbm, gain)))
    ]
    for copy in loads[:3]:
        copy.start()

    def chunk(ref, h, j):
        return ref[j * CHUNK : (j + 1) * CHUNK, h * DH : (h + 1) * DH]

    def worker_z(i):
        return (c * pair + i) * spacing

    def in_copy(kind, i, slot, device_id):
        src, dst = ((s_chip, s_arr), (cp_chip, cp_arr))[kind]
        return remote(src.at[i], dst.at[slot], in_send.at[kind, i], in_recv.at[kind, slot], device_id)

    def send_in(kind):
        for i in range(pair):
            here = z == worker_z(i)
            copy = in_copy(kind, i, z, {"seq_1": worker_z(i)})

            @pl.when(jnp.logical_not(here))
            def _(copy=copy):
                copy.start()

            @pl.when(here)
            def _(i=i):
                src, dst = ((s_chip, s_arr), (cp_chip, cp_arr))[kind]
                dst[z] = src[i]

    def drain_in(kind):
        for i in range(pair):
            @pl.when(z != worker_z(i))
            def _(i=i):
                in_copy(kind, i, z, {"seq_1": worker_z(i)}).wait_send()

    def wait_in(kind):
        for d in range(1, nz):
            in_copy(kind, 0, modz(d), {"seq_1": modz(d)}).wait_recv()

    def back_copy(kind, i, t):
        src, dst = ((s_back, s_pre), (p_back, p_pre))[kind]
        return remote(src.at[t], dst.at[i], back_send.at[kind, t], back_recv.at[kind, i], {"seq_1": t})

    def takes_back(t):
        return (z != t) & (y > 0) if t == 0 else z != t

    def send_back(kind):
        for t in range(nz):

            @pl.when(takes_back(t))
            def _(t=t):
                back_copy(kind, my_head, t).start()

        src, dst = ((s_back, s_pre), (p_back, p_pre))[kind]
        dst[my_head] = src[z]

    def drain_back(kind):
        for t in range(nz):

            @pl.when(takes_back(t))
            def _(t=t):
                back_copy(kind, my_head, t).wait_send()

    def wait_back(kind, i):
        @pl.when((z != worker_z(i)) & jnp.logical_not(is_first))
        def _():
            back_copy(kind, i, 0).wait_recv()

    def total_copy(kind, d, slot):
        part = (pl.ds(0, 1), pl.ds(1, 2))[kind]
        return remote(
            y_out.at[part], y_in.at[slot, part], y_send.at[kind, d], y_recv.at[kind, slot], {"seq_0": mody(d)}
        )

    def send_totals(kind):
        for d in FAR_FIRST:
            if d < ny:

                @pl.when(y + d < ny)
                def _(d=d):
                    total_copy(kind, d, y).start()

    def wait_totals(kind):
        for d in range(1, ny):

            @pl.when(y >= d)
            def _(d=d):
                total_copy(kind, d, y - d).wait_recv()

    def drain_totals(kind):
        for d in range(1, ny):

            @pl.when(y + d < ny)
            def _(d=d):
                total_copy(kind, d, y).wait_send()

    def s_base_until(limit):
        base = jnp.zeros((DH, DH), F32)
        for r in range(ny - 1):
            base = base + jnp.where(r < limit, y_in[r, 0].astype(F32), 0.0)
        return base

    colour = lax.rem(y + z, 2)
    piece_rows = w.shape[1] // 8

    def rows_of(colour_of, core_of, half, part=None):
        first = colour_of * (4 * piece_rows) + core_of * (2 * piece_rows) + half * piece_rows
        count = piece_rows
        if part is not None:
            count = piece_rows // 2
            first = first + part * count
        return pl.ds(pl.multiple_of(first, count), count)

    def piece(i, colour_of, core_of, part=None):
        offset, half = X_PIECES[i]
        return w.at[modx(offset), rows_of(colour_of, core_of, half, part)]

    def w_copy(number, src, dst, device_id):
        return remote(src, dst, w_send.at[number], w_recv.at[number], device_id)

    def unit(number, part):
        return 2 * number + (part or 0)

    def x_send(number, part):
        offset, half = X_PIECES[number]
        if number < 4:
            rows = rows_of(colour, c, half, part)
            return w_copy(unit(number, part), w_hbm.at[rows], w.at[x, rows], {"head": modx(-offset)})
        src = piece(number - 4, colour, c, part)
        return w_copy(unit(number, part), src, src, {"head": modx(1 if number == 4 else -1)})

    def x_arrival(number, part):
        ref = piece(number, colour, c, part)
        return w_copy(unit(number, part), ref, ref, {"head": modx(1)})

    def plane_copy(number, part, colour_of):
        ref = piece(number, colour_of, c, part)
        step = 1 if X_PIECES[number][1] == 0 else -1
        peer = {"seq_1": modz(step + nz)} if number >= 4 and part == 1 else {"seq_0": mody(step)}
        return w_copy(12 + unit(number, part), ref, ref, peer)

    def core_copy(number, core_of):
        ref = piece(number, colour, core_of)
        return w_copy(24 + number, ref, ref, {"seq_2": 1 - c})

    def core_plane_copy(number, part, core_of):
        ref = piece(number, 1 - colour, core_of, part)
        return w_copy(30 + unit(number, part), ref, ref, {"seq_2": 1 - c})

    def relay_x(*units):
        for number, part in units:
            x_arrival(number, part).wait_recv()
            if number < 2:
                start(x_send(4 + number, part))
            start(plane_copy(number, part, colour))
        for number, part in units:
            if part != 0:
                start(core_copy(number, c))

    def arrive_plane(number):
        for part in PARTS[number]:
            plane_copy(number, part, 1 - colour).wait_recv()
            if number >= 4:
                start(core_plane_copy(number, part, c))
        if number < 4:
            start(core_plane_copy(number, None, c))

    row = lax.broadcasted_iota(jnp.int32, (CHUNK, CHUNK), 0)
    col = lax.broadcasted_iota(jnp.int32, (CHUNK, CHUNK), 1)
    loads[0].wait()
    for h in range(heads):
        first = dot(chunk(k, h, 0), chunk(k, h, 0), 0, 0)
        s_first[h] = first.astype(BF16)
        s_loc[h // pair, h % pair] = (first + dot(chunk(k, h, 1), chunk(k, h, 1), 0, 0)).astype(BF16)
    loads[1].wait()
    loads[2].wait()
    strict, causal = col < row, col <= row
    blocks = [(h, j) for h in range(heads) for j in range(2)]
    for h in range(heads):
        v_t[h] = v[:, h * DH : (h + 1) * DH].T
    scores = [jnp.where(strict, dot(chunk(q, h, j), chunk(k, h, j), 1, 1), 0.0).astype(BF16) for h, j in blocks]
    fs = []
    for n, (h, j) in enumerate(blocks):
        f = dot(scores[n], chunk(k, h, j), 1, 0)
        if j == 1:
            f = f + dot(chunk(q, h, j), s_first[h], 1, 0)
        f_loc[j * CHUNK : (j + 1) * CHUNK, h * DH : (h + 1) * DH] = f
        fs.append(f.astype(BF16))
    for h in range(heads):
        cross = dot(v_t[h], q[:, h * DH : (h + 1) * DH], 1, 0)
        pairs = dot(v_t[h, :, :CHUNK], fs[2 * h], 1, 0) + dot(v_t[h, :, CHUNK:], fs[2 * h + 1], 1, 0)
        cp_loc[h // pair, h % pair, 0] = cross.astype(BF16)
        cp_loc[h // pair, h % pair, 1] = pairs.astype(BF16)

    pl.semaphore_wait(barrier, nx - 1 + ny - 1 + 1 + pair - is_worker.astype(jnp.int32) + 2 * is_first.astype(jnp.int32))
    for copy in loads[3:]:
        copy.start()
    sibling = {"seq_2": 1 - c}
    s_core = remote(s_loc.at[1 - c], s_sib, core_send.at[0], core_recv.at[0], sibling)
    cp_core = remote(cp_loc.at[1 - c], cp_sib, core_send.at[1], core_recv.at[1], sibling)
    start(s_core)
    start(cp_core)
    for number, part in ((0, 0), (1, 0), (0, 1), (1, 1), (2, None), (3, None)):
        start(x_send(number, part))
    s_core.wait_recv()
    for i in range(pair):
        s_chip[i] = (s_loc[c, i].astype(F32) + s_sib[i].astype(F32)).astype(BF16)
    send_in(0)
    cp_core.wait_recv()
    for i in range(pair):
        mine, other = cp_loc[c, i], cp_sib[i]
        early = jnp.where(c == 0, s_loc[c, i], s_sib[i])
        late = jnp.where(c == 0, other[0], mine[0])
        cp_chip[i, 0] = (mine[0].astype(F32) + other[0].astype(F32)).astype(BF16)
        cp_chip[i, 1] = (mine[1].astype(F32) + other[1].astype(F32) + dot(late, early, 1, 0)).astype(BF16)
    send_in(1)

    def by_core(i):
        own, other = cp_loc[c, i], cp_sib[i]
        return jnp.where(c == 0, s_loc[c, i], s_sib[i]), jnp.where(c == 0, own[0], other[0]), jnp.where(c == 0, own[1], other[1])

    def s_before_core(i, chip):
        s_early, c_early, p_early = by_core(i)
        later = (chip.astype(F32) + s_early.astype(F32)).astype(BF16)
        s_mine[c, i] = jnp.where(c == 0, chip, later)
        s_other[i] = jnp.where(c == 0, later, chip)
        p_step[i] = p_early.astype(F32) + dot(c_early, chip, 1, 0)

    def p_before_core(i, chip):
        later = (chip.astype(F32) + p_step[i]).astype(BF16)
        p_mine[c, i] = jnp.where(c == 0, chip, later)
        p_other[i] = jnp.where(c == 0, later, chip)

    swap_s = remote(s_other, s_mine.at[c], core_send.at[2], core_recv.at[2], sibling)

    def swap_p(i, slot):
        return remote(p_other.at[i], p_mine.at[slot, i], core_send.at[3 + i], core_recv.at[3 + i], sibling)

    swaps_p = [swap_p(i, c) for i in range(pair)]

    @pl.when(is_first)
    def _():
        nothing = jnp.zeros((DH, DH), BF16)
        for i in range(pair):
            s_before_core(i, nothing)
            p_before_core(i, nothing)
        swap_s.start()
        for copy in swaps_p:
            copy.start()

    relay_x((0, 0), (1, 0))

    @pl.when(is_worker)
    def _():
        wait_in(0)
        total = jnp.zeros((DH, DH), F32)
        for r in range(nz):
            s_run[r] = total
            total = total + s_arr[r].astype(F32)
        y_out[0] = total.astype(BF16)
        send_totals(0)
        y_in[y, 0] = total.astype(BF16)

    relay_x((0, 1), (1, 1))

    @pl.when(is_worker)
    def _():
        wait_in(1)
        pairs = jnp.zeros((DH, DH), F32)
        cross = jnp.zeros((DH, DH), F32)
        for r in range(nz):
            p_run[r] = pairs
            c_run[r] = cross.astype(BF16)
            pairs = pairs + (cp_arr[r, 1].astype(F32) + dot(cp_arr[r, 0], s_run[r].astype(BF16), 1, 0))
            cross = cross + cp_arr[r, 0].astype(F32)
        y_out[1] = cross.astype(BF16)
        y_out[2] = pairs.astype(BF16)
        send_totals(1)
        y_in[y, 1] = cross.astype(BF16)
        y_in[y, 2] = pairs.astype(BF16)
        wait_totals(0)
        s_base = s_base_until(y)
        for r in range(nz):
            s_back[r] = (s_run[r] + s_base).astype(BF16)
        send_back(0)
        s_base = s_base.astype(BF16)
        for r in range(nz):
            p_run[r] = p_run[r] + dot(c_run[r], s_base, 1, 0)
        before = [s_base_until(r).astype(BF16) for r in range(ny - 1)]
        wait_totals(1)
        p_base = jnp.zeros((DH, DH), F32)
        for r in range(ny - 1):
            line = y_in[r, 2].astype(F32) + dot(y_in[r, 1], before[r], 1, 0)
            p_base = p_base + jnp.where(r < y, line, 0.0)
        for r in range(nz):
            p_back[r] = (p_run[r] + p_base).astype(BF16)
        send_back(1)

    for i in range(pair):
        wait_back(0, i)

    @pl.when(jnp.logical_not(is_first))
    def _():
        for i in range(pair):
            s_before_core(i, s_pre[i])
        swap_s.start()

    pending.append(swap_s.wait_send)
    relay_x((2, None), (3, None))
    arrive_plane(0)
    arrive_plane(1)
    remote(s_other, s_mine.at[1 - c], core_send.at[2], core_recv.at[2], sibling).wait_recv()

    fs = []
    for h, j in blocks:
        f = chunk(f_loc, h, j) + dot(chunk(q, h, j), s_mine[h // pair, h % pair], 1, 0)
        fs.append(f.astype(BF16))
    mixing = [
        jnp.where(causal, dot(chunk(q, h, j), fs[n], 1, 1), 0.0).astype(BF16) for n, (h, j) in enumerate(blocks)
    ]
    for n, (h, j) in enumerate(blocks):
        o_part[j * CHUNK : (j + 1) * CHUNK, h * DH : (h + 1) * DH] = dot(mixing[n], chunk(v, h, j), 1, 0)
    for h in range(heads):
        p_first[h // pair, h % pair] = dot(v_t[h, :, :CHUNK], fs[2 * h], 1, 0)
    relay_x((4, 0), (5, 0), (4, 1), (5, 1))

    rows_x = tokens // nx
    loads[4].wait()

    def head_cols(g, i):
        return pl.ds(pl.multiple_of(g * (pair * DH) + i * DH, DH), DH)

    def n_copy(d, g, i, slot):
        cols = head_cols(g, i)
        number = g * pair + i
        return remote(
            n_out.at[d, :, cols], n_in.at[slot, :, cols], n_send.at[d, number], n_recv.at[slot, number], {"head": modx(d)}
        )

    for i in range(pair):
        wait_back(1, i)

        @pl.when(jnp.logical_not(is_first))
        def _(i=i):
            p_before_core(i, p_pre[i])
            swaps_p[i].start()

        pending.append(swaps_p[i].wait_send)
        for g in (c, 1 - c):
            if g is not c:
                swap_p(i, g).wait_recv()
            cols = head_cols(g, i)
            p_h = p_mine[g, i]
            p_fin[0] = p_h
            p_fin[1] = (p_h.astype(F32) + p_first[g, i]).astype(BF16)
            for d in (2, 1, 3, 0):
                target = modx(d)
                rows = pl.ds(pl.multiple_of(target * rows_x, rows_x), rows_x)
                part = target // (CHUNK // rows_x)
                attended = o_part[rows, cols] + dot(q[rows, cols], p_fin[part], 1, 1)
                mean_square = jnp.mean(attended * attended, axis=-1, keepdims=True)
                n_out[d, :, cols] = (attended * lax.rsqrt(mean_square + EPS) * gain[:, cols]).astype(BF16)
                if d:
                    start(n_copy(d, g, i, x))

    arrive_plane(2)
    arrive_plane(3)

    loads[3].wait()
    tile = 512
    n_cols = out_ref.shape[1]

    def project(rows_in, slot, quarter, first, last):
        for begin in range(0, n_cols, tile):
            cols = slice(begin, begin + tile)
            part = dot(rows_in[slot], w[quarter, :, cols], 1, 0)
            if not first:
                part = part + acc[:, cols]
            if last:
                out_ref[:, cols] = part.astype(BF16)
            else:
                acc[:, cols] = part

    project(n_out, 0, x, True, False)
    arrive_plane(4)
    arrive_plane(5)
    for offset in (-1, 1, 2):
        quarter = modx(offset)
        for number, (of, _) in enumerate(X_PIECES):
            if of == offset:
                core_copy(number, 1 - c).wait_recv()
                for part in PARTS[number] if number >= 4 else (None,):
                    core_plane_copy(number, part, 1 - c).wait_recv()
        for head in range(heads):
            n_copy(offset % nx, head // pair, head % pair, quarter).wait_recv()
        project(n_in, quarter, quarter, False, offset == 2)

    for wait in pending:
        wait()
    drain_in(0)
    drain_in(1)

    @pl.when(is_worker)
    def _():
        for kind in range(2):
            drain_back(kind)
            drain_totals(kind)


def shards(ny, nz, nx, queries, key_vectors, value_vectors, norm_gain, out_weight):
    tokens, width = queries.shape
    heads = width // DH
    pair = heads // 2
    depth, n_cols = out_weight.shape

    def matrices(*lead, kind=BF16):
        return pltpu.VMEM(lead + (DH, DH), kind)

    operands = (queries, key_vectors, value_vectors, norm_gain.reshape(1, width), out_weight)
    return pl.pallas_call(
        functools.partial(kernel, ny, nz, nx),
        out_shape=jax.ShapeDtypeStruct((tokens // nx, n_cols), BF16),
        in_specs=[pl.BlockSpec(memory_space=pltpu.HBM)] * 5,
        out_specs=pl.BlockSpec(memory_space=pltpu.VMEM),
        scratch_shapes=[
            pltpu.VMEM((tokens, width), BF16),
            pltpu.VMEM((tokens, width), BF16),
            pltpu.VMEM((tokens, width), BF16),
            pltpu.VMEM((nx, depth, n_cols), BF16),
            pltpu.VMEM((1, width), F32),
            matrices(heads),
            matrices(2, pair),
            matrices(2, pair, 2),
            matrices(pair),
            matrices(pair, 2),
            matrices(pair),
            matrices(pair, 2),
            matrices(nz),
            matrices(nz, 2),
            matrices(nz, kind=F32),
            matrices(nz, kind=F32),
            matrices(nz),
            matrices(nz),
            matrices(nz),
            matrices(3),
            matrices(ny, 3),
            matrices(pair),
            matrices(pair),
            matrices(pair, kind=F32),
            matrices(pair),
            matrices(pair),
            matrices(2, pair),
            matrices(2, pair),
            pltpu.VMEM((heads, DH, tokens), BF16),
            pltpu.VMEM((tokens, width), F32),
            matrices(2, pair, kind=F32),
            pltpu.VMEM((tokens, width), F32),
            matrices(2),
            pltpu.VMEM((nx, tokens // nx, width), BF16),
            pltpu.VMEM((nx, tokens // nx, width), BF16),
            pltpu.VMEM((tokens // nx, n_cols), F32),
            pltpu.SemaphoreType.DMA((5,)),
            pltpu.SemaphoreType.DMA((3 + pair,)),
            pltpu.SemaphoreType.DMA((3 + pair,)),
            pltpu.SemaphoreType.DMA((2, pair)),
            pltpu.SemaphoreType.DMA((2, nz)),
            pltpu.SemaphoreType.DMA((2, nz)),
            pltpu.SemaphoreType.DMA((2, pair)),
            pltpu.SemaphoreType.DMA((2, ny)),
            pltpu.SemaphoreType.DMA((2, ny)),
            pltpu.SemaphoreType.DMA((nx, heads)),
            pltpu.SemaphoreType.DMA((nx, heads)),
            pltpu.SemaphoreType.DMA((42,)),
            pltpu.SemaphoreType.DMA((42,)),
        ],
        compiler_params=pltpu.CompilerParams(
            collective_id=0, has_side_effects=True, vmem_limit_bytes=48 * 1024 * 1024
        ),
    )(*[pltpu.with_memory_space_constraint(array, pltpu.HBM) for array in operands])


def solution(mesh):
    seq, nx = mesh.shape["seq"], mesh.shape["head"]
    ny = 4 if seq == 64 else 2
    nz = seq // (2 * ny)
    split = Mesh(mesh.devices.reshape(ny, nz, 2, nx), SEQ_HEAD)
    in_specs = (P(SEQ, "head"), P(SEQ, "head"), P(SEQ, "head"), P("head"), P("head", None))
    out_specs = P(SEQ_HEAD, None)
    return jax.shard_map(
        functools.partial(shards, ny, nz, nx), mesh=split, in_specs=in_specs, out_specs=out_specs, check_vma=False
    )
```

```python
import functools

import jax
import jax.numpy as jnp
from jax import lax
from jax.experimental import pallas as pl
from jax.experimental.pallas import tpu as pltpu
from jax.sharding import Mesh
from jax.sharding import PartitionSpec as P

DH = 128
SEQ = ("seq_0", "seq_1", "seq_2")
SEQ_HEAD = ("seq_0", "seq_1", "seq_2", "head")
F32 = jnp.float32
BF16 = jnp.bfloat16
CHUNK = 256
EPS = 1e-06
FAR_FIRST = (4, 3, 5, 2, 6, 1, 7)

PARTS = ((0, 1), (0, 1), (None,), (None,), (0, 1), (0, 1))
X_PIECES = ((-1, 0), (1, 1), (-1, 1), (1, 0), (2, 0), (2, 1))


def dot(a, b, ca, cb):
    return lax.dot_general(a, b, (((ca,), (cb,)), ((), ())), preferred_element_type=F32)


def kernel(
    ny,
    nz,
    nx,
    q_hbm,
    k_hbm,
    v_hbm,
    gain_hbm,
    w_hbm,
    out_ref,
    q,
    k,
    v,
    w,
    gain,
    s_first,
    s_loc,
    cp_loc,
    s_sib,
    cp_sib,
    s_chip,
    cp_chip,
    s_arr,
    cp_arr,
    s_run,
    p_run,
    c_run,
    s_back,
    p_back,
    y_out,
    y_in,
    s_pre,
    p_pre,
    p_step,
    s_other,
    p_other,
    s_mine,
    p_mine,
    v_t,
    f_loc,
    p_first,
    o_part,
    p_fin,
    n_out,
    n_in,
    acc,
    load_sem,
    core_send,
    core_recv,
    in_send,
    in_recv,
    back_send,
    back_recv,
    y_send,
    y_recv,
    n_send,
    n_recv,
    w_send,
    w_recv,
):
    tokens, width = q.shape
    heads = width // DH
    pair = heads // 2
    y, z, c, x = (lax.axis_index(name) for name in SEQ_HEAD)

    def modx(i):
        return lax.rem(x + i + nx, nx)

    def mody(i):
        return lax.rem(y + i + ny, ny)

    def modz(i):
        return lax.rem(z + i, nz)

    pending = []

    def remote(src, dst, send_sem, recv_sem, device_id):
        return pltpu.make_async_remote_copy(
            src_ref=src,
            dst_ref=dst,
            send_sem=send_sem,
            recv_sem=recv_sem,
            device_id=device_id,
            device_id_type=pl.DeviceIdType.MESH,
        )

    def start(copy):
        copy.start()
        pending.append(copy.wait_send)

    spacing = nz // heads
    is_worker = (lax.rem(z, spacing) == 0) & (z // (spacing * pair) == c)
    my_head = lax.rem(z // spacing, pair)

    barrier = pltpu.get_barrier_semaphore()

    def greet(peer):
        pl.semaphore_signal(barrier, inc=1, device_id=peer, device_id_type=pl.DeviceIdType.MESH)

    for d in range(1, ny):
        greet({"seq_0": mody(d)})
    for d in range(1, nx):
        greet({"head": modx(d)})
    greet({"seq_2": 1 - c})

    is_first = (y == 0) & (z == 0)

    @pl.when((y == 0) & ((z == 1) | (z == nz - 1)))
    def _():
        greet({"seq_1": 0})

    @pl.when(is_worker)
    def _():
        for d in FAR_FIRST:
            if d < nz:
                greet({"seq_1": modz(d)})

    loads = [
        pltpu.make_async_copy(src, dst, load_sem.at[i])
        for i, (src, dst) in enumerate(((k_hbm, k), (q_hbm, q), (v_hbm, v), (w_hbm, w.at[x]), (gain_hbm, gain)))
    ]
    for copy in loads[:3]:
        copy.start()

    def chunk(ref, h, j):
        return ref[j * CHUNK : (j + 1) * CHUNK, h * DH : (h + 1) * DH]

    def worker_z(i):
        return (c * pair + i) * spacing

    def in_copy(kind, i, slot, device_id):
        src, dst = ((s_chip, s_arr), (cp_chip, cp_arr))[kind]
        return remote(src.at[i], dst.at[slot], in_send.at[kind, i], in_recv.at[kind, slot], device_id)

    def send_in(kind):
        for i in range(pair):
            here = z == worker_z(i)
            copy = in_copy(kind, i, z, {"seq_1": worker_z(i)})

            @pl.when(jnp.logical_not(here))
            def _(copy=copy):
                copy.start()

            @pl.when(here)
            def _(i=i):
                src, dst = ((s_chip, s_arr), (cp_chip, cp_arr))[kind]
                dst[z] = src[i]

    def drain_in(kind):
        for i in range(pair):
            @pl.when(z != worker_z(i))
            def _(i=i):
                in_copy(kind, i, z, {"seq_1": worker_z(i)}).wait_send()

    def wait_in(kind):
        for d in range(1, nz):
            in_copy(kind, 0, modz(d), {"seq_1": modz(d)}).wait_recv()

    def back_copy(kind, i, t):
        src, dst = ((s_back, s_pre), (p_back, p_pre))[kind]
        return remote(src.at[t], dst.at[i], back_send.at[kind, t], back_recv.at[kind, i], {"seq_1": t})

    def takes_back(t):
        return (z != t) & (y > 0) if t == 0 else z != t

    def send_back(kind):
        for t in range(nz):

            @pl.when(takes_back(t))
            def _(t=t):
                back_copy(kind, my_head, t).start()

        src, dst = ((s_back, s_pre), (p_back, p_pre))[kind]
        dst[my_head] = src[z]

    def drain_back(kind):
        for t in range(nz):

            @pl.when(takes_back(t))
            def _(t=t):
                back_copy(kind, my_head, t).wait_send()

    def wait_back(kind, i):
        @pl.when((z != worker_z(i)) & jnp.logical_not(is_first))
        def _():
            back_copy(kind, i, 0).wait_recv()

    def total_copy(kind, d, slot):
        part = (pl.ds(0, 1), pl.ds(1, 2))[kind]
        return remote(
            y_out.at[part], y_in.at[slot, part], y_send.at[kind, d], y_recv.at[kind, slot], {"seq_0": mody(d)}
        )

    def send_totals(kind):
        for d in FAR_FIRST:
            if d < ny:

                @pl.when(y + d < ny)
                def _(d=d):
                    total_copy(kind, d, y).start()

    def wait_totals(kind):
        for d in range(1, ny):

            @pl.when(y >= d)
            def _(d=d):
                total_copy(kind, d, y - d).wait_recv()

    def drain_totals(kind):
        for d in range(1, ny):

            @pl.when(y + d < ny)
            def _(d=d):
                total_copy(kind, d, y).wait_send()

    def s_base_until(limit):
        base = jnp.zeros((DH, DH), F32)
        for r in range(ny - 1):
            base = base + jnp.where(r < limit, y_in[r, 0].astype(F32), 0.0)
        return base

    colour = lax.rem(y + z, 2)
    piece_rows = w.shape[1] // 8

    def rows_of(colour_of, core_of, half, part=None):
        first = colour_of * (4 * piece_rows) + core_of * (2 * piece_rows) + half * piece_rows
        count = piece_rows
        if part is not None:
            count = piece_rows // 2
            first = first + part * count
        return pl.ds(pl.multiple_of(first, count), count)

    def piece(i, colour_of, core_of, part=None):
        offset, half = X_PIECES[i]
        return w.at[modx(offset), rows_of(colour_of, core_of, half, part)]

    def w_copy(number, src, dst, device_id):
        return remote(src, dst, w_send.at[number], w_recv.at[number], device_id)

    def unit(number, part):
        return 2 * number + (part or 0)

    def x_send(number, part):
        offset, half = X_PIECES[number]
        if number < 4:
            rows = rows_of(colour, c, half, part)
            return w_copy(unit(number, part), w_hbm.at[rows], w.at[x, rows], {"head": modx(-offset)})
        src = piece(number - 4, colour, c, part)
        return w_copy(unit(number, part), src, src, {"head": modx(1 if number == 4 else -1)})

    def x_arrival(number, part):
        ref = piece(number, colour, c, part)
        return w_copy(unit(number, part), ref, ref, {"head": modx(1)})

    def plane_copy(number, part, colour_of):
        ref = piece(number, colour_of, c, part)
        step = 1 if X_PIECES[number][1] == 0 else -1
        peer = {"seq_1": modz(step + nz)} if number >= 4 else {"seq_0": mody(step)}
        return w_copy(12 + unit(number, part), ref, ref, peer)

    def core_copy(number, core_of):
        ref = piece(number, colour, core_of)
        return w_copy(24 + number, ref, ref, {"seq_2": 1 - c})

    def core_plane_copy(number, part, core_of):
        ref = piece(number, 1 - colour, core_of, part)
        return w_copy(30 + unit(number, part), ref, ref, {"seq_2": 1 - c})

    def relay_x(*units):
        for number, part in units:
            x_arrival(number, part).wait_recv()
            if number < 2:
                start(x_send(4 + number, part))
            start(plane_copy(number, part, colour))
        for number, part in units:
            if part != 0:
                start(core_copy(number, c))

    def arrive_plane(number):
        for part in PARTS[number]:
            plane_copy(number, part, 1 - colour).wait_recv()
            if number >= 4:
                start(core_plane_copy(number, part, c))
        if number < 4:
            start(core_plane_copy(number, None, c))

    row = lax.broadcasted_iota(jnp.int32, (CHUNK, CHUNK), 0)
    col = lax.broadcasted_iota(jnp.int32, (CHUNK, CHUNK), 1)
    loads[0].wait()
    for h in range(heads):
        first = dot(chunk(k, h, 0), chunk(k, h, 0), 0, 0)
        s_first[h] = first.astype(BF16)
        s_loc[h // pair, h % pair] = (first + dot(chunk(k, h, 1), chunk(k, h, 1), 0, 0)).astype(BF16)
    loads[1].wait()
    loads[2].wait()
    strict, causal = col < row, col <= row
    blocks = [(h, j) for h in range(heads) for j in range(2)]
    for h in range(heads):
        v_t[h] = v[:, h * DH : (h + 1) * DH].T
    scores = [jnp.where(strict, dot(chunk(q, h, j), chunk(k, h, j), 1, 1), 0.0).astype(BF16) for h, j in blocks]
    fs = []
    for n, (h, j) in enumerate(blocks):
        f = dot(scores[n], chunk(k, h, j), 1, 0)
        if j == 1:
            f = f + dot(chunk(q, h, j), s_first[h], 1, 0)
        f_loc[j * CHUNK : (j + 1) * CHUNK, h * DH : (h + 1) * DH] = f
        fs.append(f.astype(BF16))
    for h in range(heads):
        cross = dot(v_t[h], q[:, h * DH : (h + 1) * DH], 1, 0)
        pairs = dot(v_t[h, :, :CHUNK], fs[2 * h], 1, 0) + dot(v_t[h, :, CHUNK:], fs[2 * h + 1], 1, 0)
        cp_loc[h // pair, h % pair, 0] = cross.astype(BF16)
        cp_loc[h // pair, h % pair, 1] = pairs.astype(BF16)

    pl.semaphore_wait(barrier, nx - 1 + ny - 1 + 1 + pair - is_worker.astype(jnp.int32) + 2 * is_first.astype(jnp.int32))
    for copy in loads[3:]:
        copy.start()
    sibling = {"seq_2": 1 - c}
    s_core = remote(s_loc.at[1 - c], s_sib, core_send.at[0], core_recv.at[0], sibling)
    cp_core = remote(cp_loc.at[1 - c], cp_sib, core_send.at[1], core_recv.at[1], sibling)
    start(s_core)
    start(cp_core)
    for number, part in ((0, 0), (1, 0), (0, 1), (1, 1), (2, None), (3, None)):
        start(x_send(number, part))
    s_core.wait_recv()
    for i in range(pair):
        s_chip[i] = (s_loc[c, i].astype(F32) + s_sib[i].astype(F32)).astype(BF16)
    send_in(0)
    cp_core.wait_recv()
    for i in range(pair):
        mine, other = cp_loc[c, i], cp_sib[i]
        early = jnp.where(c == 0, s_loc[c, i], s_sib[i])
        late = jnp.where(c == 0, other[0], mine[0])
        cp_chip[i, 0] = (mine[0].astype(F32) + other[0].astype(F32)).astype(BF16)
        cp_chip[i, 1] = (mine[1].astype(F32) + other[1].astype(F32) + dot(late, early, 1, 0)).astype(BF16)
    send_in(1)

    def by_core(i):
        own, other = cp_loc[c, i], cp_sib[i]
        return jnp.where(c == 0, s_loc[c, i], s_sib[i]), jnp.where(c == 0, own[0], other[0]), jnp.where(c == 0, own[1], other[1])

    def s_before_core(i, chip):
        s_early, c_early, p_early = by_core(i)
        later = (chip.astype(F32) + s_early.astype(F32)).astype(BF16)
        s_mine[c, i] = jnp.where(c == 0, chip, later)
        s_other[i] = jnp.where(c == 0, later, chip)
        p_step[i] = p_early.astype(F32) + dot(c_early, chip, 1, 0)

    def p_before_core(i, chip):
        later = (chip.astype(F32) + p_step[i]).astype(BF16)
        p_mine[c, i] = jnp.where(c == 0, chip, later)
        p_other[i] = jnp.where(c == 0, later, chip)

    swap_s = remote(s_other, s_mine.at[c], core_send.at[2], core_recv.at[2], sibling)

    def swap_p(i, slot):
        return remote(p_other.at[i], p_mine.at[slot, i], core_send.at[3 + i], core_recv.at[3 + i], sibling)

    swaps_p = [swap_p(i, c) for i in range(pair)]

    @pl.when(is_first)
    def _():
        nothing = jnp.zeros((DH, DH), BF16)
        for i in range(pair):
            s_before_core(i, nothing)
            p_before_core(i, nothing)
        swap_s.start()
        for copy in swaps_p:
            copy.start()

    relay_x((0, 0), (1, 0))

    @pl.when(is_worker)
    def _():
        wait_in(0)
        total = jnp.zeros((DH, DH), F32)
        for r in range(nz):
            s_run[r] = total
            total = total + s_arr[r].astype(F32)
        y_out[0] = total.astype(BF16)
        send_totals(0)
        y_in[y, 0] = total.astype(BF16)

    relay_x((0, 1), (1, 1))

    @pl.when(is_worker)
    def _():
        wait_in(1)
        pairs = jnp.zeros((DH, DH), F32)
        cross = jnp.zeros((DH, DH), F32)
        for r in range(nz):
            p_run[r] = pairs
            c_run[r] = cross.astype(BF16)
            pairs = pairs + (cp_arr[r, 1].astype(F32) + dot(cp_arr[r, 0], s_run[r].astype(BF16), 1, 0))
            cross = cross + cp_arr[r, 0].astype(F32)
        y_out[1] = cross.astype(BF16)
        y_out[2] = pairs.astype(BF16)
        send_totals(1)
        y_in[y, 1] = cross.astype(BF16)
        y_in[y, 2] = pairs.astype(BF16)
        wait_totals(0)
        s_base = s_base_until(y)
        for r in range(nz):
            s_back[r] = (s_run[r] + s_base).astype(BF16)
        send_back(0)
        s_base = s_base.astype(BF16)
        for r in range(nz):
            p_run[r] = p_run[r] + dot(c_run[r], s_base, 1, 0)
        before = [s_base_until(r).astype(BF16) for r in range(ny - 1)]
        wait_totals(1)
        p_base = jnp.zeros((DH, DH), F32)
        for r in range(ny - 1):
            line = y_in[r, 2].astype(F32) + dot(y_in[r, 1], before[r], 1, 0)
            p_base = p_base + jnp.where(r < y, line, 0.0)
        for r in range(nz):
            p_back[r] = (p_run[r] + p_base).astype(BF16)
        send_back(1)

    for i in range(pair):
        wait_back(0, i)

    @pl.when(jnp.logical_not(is_first))
    def _():
        for i in range(pair):
            s_before_core(i, s_pre[i])
        swap_s.start()

    pending.append(swap_s.wait_send)
    relay_x((2, None), (3, None))
    arrive_plane(0)
    arrive_plane(1)
    remote(s_other, s_mine.at[1 - c], core_send.at[2], core_recv.at[2], sibling).wait_recv()

    fs = []
    for h, j in blocks:
        f = chunk(f_loc, h, j) + dot(chunk(q, h, j), s_mine[h // pair, h % pair], 1, 0)
        fs.append(f.astype(BF16))
    mixing = [
        jnp.where(causal, dot(chunk(q, h, j), fs[n], 1, 1), 0.0).astype(BF16) for n, (h, j) in enumerate(blocks)
    ]
    for n, (h, j) in enumerate(blocks):
        o_part[j * CHUNK : (j + 1) * CHUNK, h * DH : (h + 1) * DH] = dot(mixing[n], chunk(v, h, j), 1, 0)
    for h in range(heads):
        p_first[h // pair, h % pair] = dot(v_t[h, :, :CHUNK], fs[2 * h], 1, 0)
    relay_x((4, 0), (5, 0), (4, 1), (5, 1))

    rows_x = tokens // nx
    loads[4].wait()

    def head_cols(g, i):
        return pl.ds(pl.multiple_of(g * (pair * DH) + i * DH, DH), DH)

    def n_copy(d, g, i, slot):
        cols = head_cols(g, i)
        number = g * pair + i
        return remote(
            n_out.at[d, :, cols], n_in.at[slot, :, cols], n_send.at[d, number], n_recv.at[slot, number], {"head": modx(d)}
        )

    for i in range(pair):
        wait_back(1, i)

        @pl.when(jnp.logical_not(is_first))
        def _(i=i):
            p_before_core(i, p_pre[i])
            swaps_p[i].start()

        pending.append(swaps_p[i].wait_send)
        for g in (c, 1 - c):
            if g is not c:
                swap_p(i, g).wait_recv()
            cols = head_cols(g, i)
            p_h = p_mine[g, i]
            p_fin[0] = p_h
            p_fin[1] = (p_h.astype(F32) + p_first[g, i]).astype(BF16)
            for d in (2, 1, 3, 0):
                target = modx(d)
                rows = pl.ds(pl.multiple_of(target * rows_x, rows_x), rows_x)
                part = target // (CHUNK // rows_x)
                attended = o_part[rows, cols] + dot(q[rows, cols], p_fin[part], 1, 1)
                mean_square = jnp.mean(attended * attended, axis=-1, keepdims=True)
                n_out[d, :, cols] = (attended * lax.rsqrt(mean_square + EPS) * gain[:, cols]).astype(BF16)
                if d:
                    start(n_copy(d, g, i, x))

    arrive_plane(2)
    arrive_plane(3)

    loads[3].wait()
    tile = 512
    n_cols = out_ref.shape[1]

    def project(rows_in, slot, quarter, first, last):
        for begin in range(0, n_cols, tile):
            cols = slice(begin, begin + tile)
            part = dot(rows_in[slot], w[quarter, :, cols], 1, 0)
            if not first:
                part = part + acc[:, cols]
            if last:
                out_ref[:, cols] = part.astype(BF16)
            else:
                acc[:, cols] = part

    project(n_out, 0, x, True, False)
    arrive_plane(4)
    arrive_plane(5)
    for offset in (-1, 1, 2):
        quarter = modx(offset)
        for number, (of, _) in enumerate(X_PIECES):
            if of == offset:
                core_copy(number, 1 - c).wait_recv()
                for part in PARTS[number] if number >= 4 else (None,):
                    core_plane_copy(number, part, 1 - c).wait_recv()
        for head in range(heads):
            n_copy(offset % nx, head // pair, head % pair, quarter).wait_recv()
        project(n_in, quarter, quarter, False, offset == 2)

    for wait in pending:
        wait()
    drain_in(0)
    drain_in(1)

    @pl.when(is_worker)
    def _():
        for kind in range(2):
            drain_back(kind)
            drain_totals(kind)


def shards(ny, nz, nx, queries, key_vectors, value_vectors, norm_gain, out_weight):
    tokens, width = queries.shape
    heads = width // DH
    pair = heads // 2
    depth, n_cols = out_weight.shape

    def matrices(*lead, kind=BF16):
        return pltpu.VMEM(lead + (DH, DH), kind)

    operands = (queries, key_vectors, value_vectors, norm_gain.reshape(1, width), out_weight)
    return pl.pallas_call(
        functools.partial(kernel, ny, nz, nx),
        out_shape=jax.ShapeDtypeStruct((tokens // nx, n_cols), BF16),
        in_specs=[pl.BlockSpec(memory_space=pltpu.HBM)] * 5,
        out_specs=pl.BlockSpec(memory_space=pltpu.VMEM),
        scratch_shapes=[
            pltpu.VMEM((tokens, width), BF16),
            pltpu.VMEM((tokens, width), BF16),
            pltpu.VMEM((tokens, width), BF16),
            pltpu.VMEM((nx, depth, n_cols), BF16),
            pltpu.VMEM((1, width), F32),
            matrices(heads),
            matrices(2, pair),
            matrices(2, pair, 2),
            matrices(pair),
            matrices(pair, 2),
            matrices(pair),
            matrices(pair, 2),
            matrices(nz),
            matrices(nz, 2),
            matrices(nz, kind=F32),
            matrices(nz, kind=F32),
            matrices(nz),
            matrices(nz),
            matrices(nz),
            matrices(3),
            matrices(ny, 3),
            matrices(pair),
            matrices(pair),
            matrices(pair, kind=F32),
            matrices(pair),
            matrices(pair),
            matrices(2, pair),
            matrices(2, pair),
            pltpu.VMEM((heads, DH, tokens), BF16),
            pltpu.VMEM((tokens, width), F32),
            matrices(2, pair, kind=F32),
            pltpu.VMEM((tokens, width), F32),
            matrices(2),
            pltpu.VMEM((nx, tokens // nx, width), BF16),
            pltpu.VMEM((nx, tokens // nx, width), BF16),
            pltpu.VMEM((tokens // nx, n_cols), F32),
            pltpu.SemaphoreType.DMA((5,)),
            pltpu.SemaphoreType.DMA((3 + pair,)),
            pltpu.SemaphoreType.DMA((3 + pair,)),
            pltpu.SemaphoreType.DMA((2, pair)),
            pltpu.SemaphoreType.DMA((2, nz)),
            pltpu.SemaphoreType.DMA((2, nz)),
            pltpu.SemaphoreType.DMA((2, pair)),
            pltpu.SemaphoreType.DMA((2, ny)),
            pltpu.SemaphoreType.DMA((2, ny)),
            pltpu.SemaphoreType.DMA((nx, heads)),
            pltpu.SemaphoreType.DMA((nx, heads)),
            pltpu.SemaphoreType.DMA((42,)),
            pltpu.SemaphoreType.DMA((42,)),
        ],
        compiler_params=pltpu.CompilerParams(
            collective_id=0, has_side_effects=True, vmem_limit_bytes=48 * 1024 * 1024
        ),
    )(*[pltpu.with_memory_space_constraint(array, pltpu.HBM) for array in operands])


def solution(mesh):
    seq, nx = mesh.shape["seq"], mesh.shape["head"]
    ny = 4 if seq == 64 else 2
    nz = seq // (2 * ny)
    split = Mesh(mesh.devices.reshape(ny, nz, 2, nx), SEQ_HEAD)
    in_specs = (P(SEQ, "head"), P(SEQ, "head"), P(SEQ, "head"), P("head"), P("head", None))
    out_specs = P(SEQ_HEAD, None)
    return jax.shard_map(
        functools.partial(shards, ny, nz, nx), mesh=split, in_specs=in_specs, out_specs=out_specs, check_vma=False
    )
```

```python
import functools

import jax
import jax.numpy as jnp
from jax import lax
from jax.experimental import pallas as pl
from jax.experimental.pallas import tpu as pltpu
from jax.sharding import Mesh
from jax.sharding import PartitionSpec as P

DH = 128
SEQ = ("seq_0", "seq_1", "seq_2")
SEQ_HEAD = ("seq_0", "seq_1", "seq_2", "head")
F32 = jnp.float32
BF16 = jnp.bfloat16
CHUNK = 256
EPS = 1e-06
FAR_FIRST = (4, 3, 5, 2, 6, 1, 7)

PARTS = ((0, 1), (0, 1), (None,), (None,), (0, 1), (0, 1))
X_PIECES = ((-1, 0), (1, 1), (-1, 1), (1, 0), (2, 0), (2, 1))


def dot(a, b, ca, cb):
    return lax.dot_general(a, b, (((ca,), (cb,)), ((), ())), preferred_element_type=F32)


def kernel(
    ny,
    nz,
    nx,
    q_hbm,
    k_hbm,
    v_hbm,
    gain_hbm,
    w_hbm,
    out_ref,
    q,
    k,
    v,
    w,
    gain,
    s_first,
    s_loc,
    cp_loc,
    s_sib,
    cp_sib,
    s_chip,
    cp_chip,
    s_arr,
    cp_arr,
    s_run,
    p_run,
    c_run,
    s_back,
    p_back,
    y_out,
    y_in,
    s_pre,
    p_pre,
    p_step,
    s_other,
    p_other,
    s_mine,
    p_mine,
    v_t,
    f_loc,
    p_first,
    o_part,
    p_fin,
    n_out,
    n_in,
    acc,
    load_sem,
    core_send,
    core_recv,
    in_send,
    in_recv,
    back_send,
    back_recv,
    y_send,
    y_recv,
    n_send,
    n_recv,
    w_send,
    w_recv,
):
    tokens, width = q.shape
    heads = width // DH
    pair = heads // 2
    y, z, c, x = (lax.axis_index(name) for name in SEQ_HEAD)

    def modx(i):
        return lax.rem(x + i + nx, nx)

    def mody(i):
        return lax.rem(y + i + ny, ny)

    def modz(i):
        return lax.rem(z + i, nz)

    pending = []

    def remote(src, dst, send_sem, recv_sem, device_id):
        return pltpu.make_async_remote_copy(
            src_ref=src,
            dst_ref=dst,
            send_sem=send_sem,
            recv_sem=recv_sem,
            device_id=device_id,
            device_id_type=pl.DeviceIdType.MESH,
        )

    def start(copy):
        copy.start()
        pending.append(copy.wait_send)

    spacing = nz // heads
    is_worker = (lax.rem(z, spacing) == 0) & (z // (spacing * pair) == c)
    my_head = lax.rem(z // spacing, pair)

    barrier = pltpu.get_barrier_semaphore()

    def greet(peer):
        pl.semaphore_signal(barrier, inc=1, device_id=peer, device_id_type=pl.DeviceIdType.MESH)

    for d in range(1, ny):
        greet({"seq_0": mody(d)})
    for d in range(1, nx):
        greet({"head": modx(d)})
    greet({"seq_2": 1 - c})

    is_first = (y == 0) & (z == 0)

    @pl.when((y == 0) & ((z == 1) | (z == nz - 1)))
    def _():
        greet({"seq_1": 0})

    @pl.when(is_worker)
    def _():
        for d in FAR_FIRST:
            if d < nz:
                greet({"seq_1": modz(d)})

    loads = [
        pltpu.make_async_copy(src, dst, load_sem.at[i])
        for i, (src, dst) in enumerate(((k_hbm, k), (q_hbm, q), (v_hbm, v), (w_hbm, w.at[x]), (gain_hbm, gain)))
    ]
    for copy in loads[:3]:
        copy.start()

    def chunk(ref, h, j):
        return ref[j * CHUNK : (j + 1) * CHUNK, h * DH : (h + 1) * DH]

    def worker_z(i):
        return (c * pair + i) * spacing

    def in_copy(kind, i, slot, device_id):
        src, dst = ((s_chip, s_arr), (cp_chip, cp_arr))[kind]
        return remote(src.at[i], dst.at[slot], in_send.at[kind, i], in_recv.at[kind, slot], device_id)

    def send_in(kind):
        for i in range(pair):
            here = z == worker_z(i)
            copy = in_copy(kind, i, z, {"seq_1": worker_z(i)})

            @pl.when(jnp.logical_not(here))
            def _(copy=copy):
                copy.start()

            @pl.when(here)
            def _(i=i):
                src, dst = ((s_chip, s_arr), (cp_chip, cp_arr))[kind]
                dst[z] = src[i]

    def drain_in(kind):
        for i in range(pair):
            @pl.when(z != worker_z(i))
            def _(i=i):
                in_copy(kind, i, z, {"seq_1": worker_z(i)}).wait_send()

    def wait_in(kind):
        for d in range(1, nz):
            in_copy(kind, 0, modz(d), {"seq_1": modz(d)}).wait_recv()

    def back_copy(kind, i, t):
        src, dst = ((s_back, s_pre), (p_back, p_pre))[kind]
        return remote(src.at[t], dst.at[i], back_send.at[kind, t], back_recv.at[kind, i], {"seq_1": t})

    def takes_back(t):
        return (z != t) & (y > 0) if t == 0 else z != t

    def send_back(kind):
        for t in range(nz):

            @pl.when(takes_back(t))
            def _(t=t):
                back_copy(kind, my_head, t).start()

        src, dst = ((s_back, s_pre), (p_back, p_pre))[kind]
        dst[my_head] = src[z]

    def drain_back(kind):
        for t in range(nz):

            @pl.when(takes_back(t))
            def _(t=t):
                back_copy(kind, my_head, t).wait_send()

    def wait_back(kind, i):
        @pl.when((z != worker_z(i)) & jnp.logical_not(is_first))
        def _():
            back_copy(kind, i, 0).wait_recv()

    def total_copy(kind, d, slot):
        part = (pl.ds(0, 1), pl.ds(1, 2))[kind]
        return remote(
            y_out.at[part], y_in.at[slot, part], y_send.at[kind, d], y_recv.at[kind, slot], {"seq_0": mody(d)}
        )

    def send_totals(kind):
        for d in FAR_FIRST:
            if d < ny:

                @pl.when(y + d < ny)
                def _(d=d):
                    total_copy(kind, d, y).start()

    def wait_totals(kind):
        for d in range(1, ny):

            @pl.when(y >= d)
            def _(d=d):
                total_copy(kind, d, y - d).wait_recv()

    def drain_totals(kind):
        for d in range(1, ny):

            @pl.when(y + d < ny)
            def _(d=d):
                total_copy(kind, d, y).wait_send()

    def s_base_until(limit):
        base = jnp.zeros((DH, DH), F32)
        for r in range(ny - 1):
            base = base + jnp.where(r < limit, y_in[r, 0].astype(F32), 0.0)
        return base

    colour = lax.rem(y + z, 2)
    piece_rows = w.shape[1] // 8

    def rows_of(colour_of, core_of, half, part=None):
        first = colour_of * (4 * piece_rows) + core_of * (2 * piece_rows) + half * piece_rows
        count = piece_rows
        if part is not None:
            count = piece_rows // 2
            first = first + part * count
        return pl.ds(pl.multiple_of(first, count), count)

    def piece(i, colour_of, core_of, part=None):
        offset, half = X_PIECES[i]
        return w.at[modx(offset), rows_of(colour_of, core_of, half, part)]

    def w_copy(number, src, dst, device_id):
        return remote(src, dst, w_send.at[number], w_recv.at[number], device_id)

    def unit(number, part):
        return 2 * number + (part or 0)

    def x_send(number, part):
        offset, half = X_PIECES[number]
        if number < 4:
            rows = rows_of(colour, c, half, part)
            return w_copy(unit(number, part), w_hbm.at[rows], w.at[x, rows], {"head": modx(-offset)})
        src = piece(number - 4, colour, c, part)
        return w_copy(unit(number, part), src, src, {"head": modx(1 if number == 4 else -1)})

    def x_arrival(number, part):
        ref = piece(number, colour, c, part)
        return w_copy(unit(number, part), ref, ref, {"head": modx(1)})

    def plane_copy(number, part, colour_of):
        ref = piece(number, colour_of, c, part)
        step = 1 if X_PIECES[number][1] == 0 else -1
        peer = {"seq_1": modz(step + nz)} if number >= 4 else {"seq_0": mody(step)}
        return w_copy(12 + unit(number, part), ref, ref, peer)

    def core_copy(number, core_of):
        ref = piece(number, colour, core_of)
        return w_copy(24 + number, ref, ref, {"seq_2": 1 - c})

    def core_plane_copy(number, part, core_of):
        ref = piece(number, 1 - colour, core_of, part)
        return w_copy(30 + unit(number, part), ref, ref, {"seq_2": 1 - c})

    def relay_x(*units):
        for number, part in units:
            x_arrival(number, part).wait_recv()
            if number < 2:
                start(x_send(4 + number, part))
            start(plane_copy(number, part, colour))
        for number, part in units:
            if part != 0:
                start(core_copy(number, c))

    def arrive_plane(number):
        for part in PARTS[number]:
            plane_copy(number, part, 1 - colour).wait_recv()
        start(core_plane_copy(number, None, c))

    def arrive_last():
        for part in range(2):
            for number in (5, 4):
                plane_copy(number, part, 1 - colour).wait_recv()
                start(core_plane_copy(number, part, c))

    row = lax.broadcasted_iota(jnp.int32, (CHUNK, CHUNK), 0)
    col = lax.broadcasted_iota(jnp.int32, (CHUNK, CHUNK), 1)
    loads[0].wait()
    for h in range(heads):
        first = dot(chunk(k, h, 0), chunk(k, h, 0), 0, 0)
        s_first[h] = first.astype(BF16)
        s_loc[h // pair, h % pair] = (first + dot(chunk(k, h, 1), chunk(k, h, 1), 0, 0)).astype(BF16)
    loads[1].wait()
    loads[2].wait()
    strict, causal = col < row, col <= row
    blocks = [(h, j) for h in range(heads) for j in range(2)]
    for h in range(heads):
        v_t[h] = v[:, h * DH : (h + 1) * DH].T
    scores = [jnp.where(strict, dot(chunk(q, h, j), chunk(k, h, j), 1, 1), 0.0).astype(BF16) for h, j in blocks]
    pl.semaphore_wait(barrier, nx - 1 + ny - 1 + 1 + pair - is_worker.astype(jnp.int32) + 2 * is_first.astype(jnp.int32))
    for copy in loads[3:]:
        copy.start()
    sibling = {"seq_2": 1 - c}
    s_core = remote(s_loc.at[1 - c], s_sib, core_send.at[0], core_recv.at[0], sibling)
    cp_core = remote(cp_loc.at[1 - c], cp_sib, core_send.at[1], core_recv.at[1], sibling)
    start(s_core)
    for number, part in ((0, 0), (1, 0), (0, 1), (1, 1), (2, None), (3, None)):
        start(x_send(number, part))

    fs = []
    for n, (h, j) in enumerate(blocks):
        f = dot(scores[n], chunk(k, h, j), 1, 0)
        if j == 1:
            f = f + dot(chunk(q, h, j), s_first[h], 1, 0)
        f_loc[j * CHUNK : (j + 1) * CHUNK, h * DH : (h + 1) * DH] = f
        fs.append(f.astype(BF16))
    for h in range(heads):
        cross = dot(v_t[h], q[:, h * DH : (h + 1) * DH], 1, 0)
        pairs = dot(v_t[h, :, :CHUNK], fs[2 * h], 1, 0) + dot(v_t[h, :, CHUNK:], fs[2 * h + 1], 1, 0)
        cp_loc[h // pair, h % pair, 0] = cross.astype(BF16)
        cp_loc[h // pair, h % pair, 1] = pairs.astype(BF16)

    start(cp_core)
    s_core.wait_recv()
    for i in range(pair):
        s_chip[i] = (s_loc[c, i].astype(F32) + s_sib[i].astype(F32)).astype(BF16)
    send_in(0)
    cp_core.wait_recv()
    for i in range(pair):
        mine, other = cp_loc[c, i], cp_sib[i]
        early = jnp.where(c == 0, s_loc[c, i], s_sib[i])
        late = jnp.where(c == 0, other[0], mine[0])
        cp_chip[i, 0] = (mine[0].astype(F32) + other[0].astype(F32)).astype(BF16)
        cp_chip[i, 1] = (mine[1].astype(F32) + other[1].astype(F32) + dot(late, early, 1, 0)).astype(BF16)
    send_in(1)

    def by_core(i):
        own, other = cp_loc[c, i], cp_sib[i]
        return jnp.where(c == 0, s_loc[c, i], s_sib[i]), jnp.where(c == 0, own[0], other[0]), jnp.where(c == 0, own[1], other[1])

    def s_before_core(i, chip):
        s_early, c_early, p_early = by_core(i)
        later = (chip.astype(F32) + s_early.astype(F32)).astype(BF16)
        s_mine[c, i] = jnp.where(c == 0, chip, later)
        s_other[i] = jnp.where(c == 0, later, chip)
        p_step[i] = p_early.astype(F32) + dot(c_early, chip, 1, 0)

    def p_before_core(i, chip):
        later = (chip.astype(F32) + p_step[i]).astype(BF16)
        p_mine[c, i] = jnp.where(c == 0, chip, later)
        p_other[i] = jnp.where(c == 0, later, chip)

    swap_s = remote(s_other, s_mine.at[c], core_send.at[2], core_recv.at[2], sibling)

    def swap_p(i, slot):
        return remote(p_other.at[i], p_mine.at[slot, i], core_send.at[3 + i], core_recv.at[3 + i], sibling)

    swaps_p = [swap_p(i, c) for i in range(pair)]

    @pl.when(is_first)
    def _():
        nothing = jnp.zeros((DH, DH), BF16)
        for i in range(pair):
            s_before_core(i, nothing)
            p_before_core(i, nothing)
        swap_s.start()
        for copy in swaps_p:
            copy.start()

    relay_x((0, 0), (1, 0))

    @pl.when(is_worker)
    def _():
        wait_in(0)
        total = jnp.zeros((DH, DH), F32)
        for r in range(nz):
            s_run[r] = total
            total = total + s_arr[r].astype(F32)
        y_out[0] = total.astype(BF16)
        send_totals(0)
        y_in[y, 0] = total.astype(BF16)

    relay_x((0, 1), (1, 1))

    @pl.when(is_worker)
    def _():
        wait_in(1)
        pairs = jnp.zeros((DH, DH), F32)
        cross = jnp.zeros((DH, DH), F32)
        for r in range(nz):
            p_run[r] = pairs
            c_run[r] = cross.astype(BF16)
            pairs = pairs + (cp_arr[r, 1].astype(F32) + dot(cp_arr[r, 0], s_run[r].astype(BF16), 1, 0))
            cross = cross + cp_arr[r, 0].astype(F32)
        y_out[1] = cross.astype(BF16)
        y_out[2] = pairs.astype(BF16)
        send_totals(1)
        y_in[y, 1] = cross.astype(BF16)
        y_in[y, 2] = pairs.astype(BF16)
        wait_totals(0)
        s_base = s_base_until(y)
        for r in range(nz):
            s_back[r] = (s_run[r] + s_base).astype(BF16)
        send_back(0)
        s_base = s_base.astype(BF16)
        for r in range(nz):
            p_run[r] = p_run[r] + dot(c_run[r], s_base, 1, 0)
        before = [s_base_until(r).astype(BF16) for r in range(ny - 1)]
        wait_totals(1)
        p_base = jnp.zeros((DH, DH), F32)
        for r in range(ny - 1):
            line = y_in[r, 2].astype(F32) + dot(y_in[r, 1], before[r], 1, 0)
            p_base = p_base + jnp.where(r < y, line, 0.0)
        for r in range(nz):
            p_back[r] = (p_run[r] + p_base).astype(BF16)
        send_back(1)

    for i in range(pair):
        wait_back(0, i)

    @pl.when(jnp.logical_not(is_first))
    def _():
        for i in range(pair):
            s_before_core(i, s_pre[i])
        swap_s.start()

    pending.append(swap_s.wait_send)
    relay_x((2, None), (3, None))
    arrive_plane(0)
    arrive_plane(1)
    remote(s_other, s_mine.at[1 - c], core_send.at[2], core_recv.at[2], sibling).wait_recv()

    fs = []
    for h, j in blocks:
        f = chunk(f_loc, h, j) + dot(chunk(q, h, j), s_mine[h // pair, h % pair], 1, 0)
        fs.append(f.astype(BF16))
    mixing = [
        jnp.where(causal, dot(chunk(q, h, j), fs[n], 1, 1), 0.0).astype(BF16) for n, (h, j) in enumerate(blocks)
    ]
    for n, (h, j) in enumerate(blocks):
        o_part[j * CHUNK : (j + 1) * CHUNK, h * DH : (h + 1) * DH] = dot(mixing[n], chunk(v, h, j), 1, 0)
    for h in range(heads):
        p_first[h // pair, h % pair] = dot(v_t[h, :, :CHUNK], fs[2 * h], 1, 0)
    relay_x((4, 0), (5, 0), (4, 1), (5, 1))

    rows_x = tokens // nx
    loads[4].wait()

    def head_cols(g, i):
        return pl.ds(pl.multiple_of(g * (pair * DH) + i * DH, DH), DH)

    def n_copy(d, g, i, slot):
        cols = head_cols(g, i)
        number = g * pair + i
        return remote(
            n_out.at[d, :, cols], n_in.at[slot, :, cols], n_send.at[d, number], n_recv.at[slot, number], {"head": modx(d)}
        )

    for i in range(pair):
        wait_back(1, i)

        @pl.when(jnp.logical_not(is_first))
        def _(i=i):
            p_before_core(i, p_pre[i])
            swaps_p[i].start()

        pending.append(swaps_p[i].wait_send)
        for g in (c, 1 - c):
            if g is not c:
                swap_p(i, g).wait_recv()
            cols = head_cols(g, i)
            p_h = p_mine[g, i]
            p_fin[0] = p_h
            p_fin[1] = (p_h.astype(F32) + p_first[g, i]).astype(BF16)
            for d in (2, 1, 3, 0):
                target = modx(d)
                rows = pl.ds(pl.multiple_of(target * rows_x, rows_x), rows_x)
                part = target // (CHUNK // rows_x)
                attended = o_part[rows, cols] + dot(q[rows, cols], p_fin[part], 1, 1)
                mean_square = jnp.mean(attended * attended, axis=-1, keepdims=True)
                n_out[d, :, cols] = (attended * lax.rsqrt(mean_square + EPS) * gain[:, cols]).astype(BF16)
                if d:
                    start(n_copy(d, g, i, x))

    loads[3].wait()
    tile = 512
    n_cols = out_ref.shape[1]

    def project(rows_in, slot, quarter, first, last):
        for begin in range(0, n_cols, tile):
            cols = slice(begin, begin + tile)
            part = dot(rows_in[slot], w[quarter, :, cols], 1, 0)
            if not first:
                part = part + acc[:, cols]
            if last:
                out_ref[:, cols] = part.astype(BF16)
            else:
                acc[:, cols] = part

    project(n_out, 0, x, True, False)
    arrive_plane(2)
    arrive_plane(3)
    arrive_last()
    for offset in (-1, 1, 2):
        quarter = modx(offset)
        for number, (of, _) in enumerate(X_PIECES):
            if of == offset:
                core_copy(number, 1 - c).wait_recv()
                for part in PARTS[number] if number >= 4 else (None,):
                    core_plane_copy(number, part, 1 - c).wait_recv()
        for head in range(heads):
            n_copy(offset % nx, head // pair, head % pair, quarter).wait_recv()
        project(n_in, quarter, quarter, False, offset == 2)

    for wait in pending:
        wait()
    drain_in(0)
    drain_in(1)

    @pl.when(is_worker)
    def _():
        for kind in range(2):
            drain_back(kind)
            drain_totals(kind)


def shards(ny, nz, nx, queries, key_vectors, value_vectors, norm_gain, out_weight):
    tokens, width = queries.shape
    heads = width // DH
    pair = heads // 2
    depth, n_cols = out_weight.shape

    def matrices(*lead, kind=BF16):
        return pltpu.VMEM(lead + (DH, DH), kind)

    operands = (queries, key_vectors, value_vectors, norm_gain.reshape(1, width), out_weight)
    return pl.pallas_call(
        functools.partial(kernel, ny, nz, nx),
        out_shape=jax.ShapeDtypeStruct((tokens // nx, n_cols), BF16),
        in_specs=[pl.BlockSpec(memory_space=pltpu.HBM)] * 5,
        out_specs=pl.BlockSpec(memory_space=pltpu.VMEM),
        scratch_shapes=[
            pltpu.VMEM((tokens, width), BF16),
            pltpu.VMEM((tokens, width), BF16),
            pltpu.VMEM((tokens, width), BF16),
            pltpu.VMEM((nx, depth, n_cols), BF16),
            pltpu.VMEM((1, width), F32),
            matrices(heads),
            matrices(2, pair),
            matrices(2, pair, 2),
            matrices(pair),
            matrices(pair, 2),
            matrices(pair),
            matrices(pair, 2),
            matrices(nz),
            matrices(nz, 2),
            matrices(nz, kind=F32),
            matrices(nz, kind=F32),
            matrices(nz),
            matrices(nz),
            matrices(nz),
            matrices(3),
            matrices(ny, 3),
            matrices(pair),
            matrices(pair),
            matrices(pair, kind=F32),
            matrices(pair),
            matrices(pair),
            matrices(2, pair),
            matrices(2, pair),
            pltpu.VMEM((heads, DH, tokens), BF16),
            pltpu.VMEM((tokens, width), F32),
            matrices(2, pair, kind=F32),
            pltpu.VMEM((tokens, width), F32),
            matrices(2),
            pltpu.VMEM((nx, tokens // nx, width), BF16),
            pltpu.VMEM((nx, tokens // nx, width), BF16),
            pltpu.VMEM((tokens // nx, n_cols), F32),
            pltpu.SemaphoreType.DMA((5,)),
            pltpu.SemaphoreType.DMA((3 + pair,)),
            pltpu.SemaphoreType.DMA((3 + pair,)),
            pltpu.SemaphoreType.DMA((2, pair)),
            pltpu.SemaphoreType.DMA((2, nz)),
            pltpu.SemaphoreType.DMA((2, nz)),
            pltpu.SemaphoreType.DMA((2, pair)),
            pltpu.SemaphoreType.DMA((2, ny)),
            pltpu.SemaphoreType.DMA((2, ny)),
            pltpu.SemaphoreType.DMA((nx, heads)),
            pltpu.SemaphoreType.DMA((nx, heads)),
            pltpu.SemaphoreType.DMA((42,)),
            pltpu.SemaphoreType.DMA((42,)),
        ],
        compiler_params=pltpu.CompilerParams(
            collective_id=0, has_side_effects=True, vmem_limit_bytes=48 * 1024 * 1024
        ),
    )(*[pltpu.with_memory_space_constraint(array, pltpu.HBM) for array in operands])


def solution(mesh):
    seq, nx = mesh.shape["seq"], mesh.shape["head"]
    ny = 4 if seq == 64 else 2
    nz = seq // (2 * ny)
    split = Mesh(mesh.devices.reshape(ny, nz, 2, nx), SEQ_HEAD)
    in_specs = (P(SEQ, "head"), P(SEQ, "head"), P(SEQ, "head"), P("head"), P("head", None))
    out_specs = P(SEQ_HEAD, None)
    return jax.shard_map(
        functools.partial(shards, ny, nz, nx), mesh=split, in_specs=in_specs, out_specs=out_specs, check_vma=False
    )
```

```python
import functools

import jax
import jax.numpy as jnp
from jax import lax
from jax.experimental import pallas as pl
from jax.experimental.pallas import tpu as pltpu
from jax.sharding import Mesh
from jax.sharding import PartitionSpec as P

DH = 128
SEQ = ("seq_0", "seq_1", "seq_2")
SEQ_HEAD = ("seq_0", "seq_1", "seq_2", "head")
F32 = jnp.float32
BF16 = jnp.bfloat16
CHUNK = 256
EPS = 1e-06
FAR_FIRST = (4, 3, 5, 2, 6, 1, 7)

PARTS = ((0, 1), (0, 1), (None,), (None,), (0, 1), (0, 1))
X_PIECES = ((-1, 0), (1, 1), (-1, 1), (1, 0), (2, 0), (2, 1))


def dot(a, b, ca, cb):
    return lax.dot_general(a, b, (((ca,), (cb,)), ((), ())), preferred_element_type=F32)


def kernel(
    ny,
    nz,
    nx,
    q_hbm,
    k_hbm,
    v_hbm,
    gain_hbm,
    w_hbm,
    out_ref,
    q,
    k,
    v,
    w,
    gain,
    s_first,
    s_loc,
    cp_loc,
    s_sib,
    cp_sib,
    s_chip,
    cp_chip,
    s_arr,
    cp_arr,
    s_run,
    p_run,
    c_run,
    s_back,
    p_back,
    y_out,
    y_in,
    s_pre,
    p_pre,
    p_step,
    s_other,
    p_other,
    s_mine,
    p_mine,
    v_t,
    f_loc,
    p_first,
    o_part,
    p_fin,
    n_out,
    n_in,
    acc,
    load_sem,
    core_send,
    core_recv,
    in_send,
    in_recv,
    back_send,
    back_recv,
    y_send,
    y_recv,
    n_send,
    n_recv,
    w_send,
    w_recv,
):
    tokens, width = q.shape
    heads = width // DH
    pair = heads // 2
    y, z, c, x = (lax.axis_index(name) for name in SEQ_HEAD)

    def modx(i):
        return lax.rem(x + i + nx, nx)

    def mody(i):
        return lax.rem(y + i + ny, ny)

    def modz(i):
        return lax.rem(z + i, nz)

    pending = []

    def remote(src, dst, send_sem, recv_sem, device_id):
        return pltpu.make_async_remote_copy(
            src_ref=src,
            dst_ref=dst,
            send_sem=send_sem,
            recv_sem=recv_sem,
            device_id=device_id,
            device_id_type=pl.DeviceIdType.MESH,
        )

    def start(copy):
        copy.start()
        pending.append(copy.wait_send)

    spacing = nz // heads
    is_worker = (lax.rem(z, spacing) == 0) & (z // (spacing * pair) == c)
    my_head = lax.rem(z // spacing, pair)

    barrier = pltpu.get_barrier_semaphore()

    def greet(peer):
        pl.semaphore_signal(barrier, inc=1, device_id=peer, device_id_type=pl.DeviceIdType.MESH)

    for d in range(1, ny):
        greet({"seq_0": mody(d)})
    for d in range(1, nx):
        greet({"head": modx(d)})
    greet({"seq_2": 1 - c})

    is_first = (y == 0) & (z == 0)

    @pl.when((y == 0) & ((z == 1) | (z == nz - 1)))
    def _():
        greet({"seq_1": 0})

    @pl.when(is_worker)
    def _():
        for d in FAR_FIRST:
            if d < nz:
                greet({"seq_1": modz(d)})

    loads = [
        pltpu.make_async_copy(src, dst, load_sem.at[i])
        for i, (src, dst) in enumerate(((k_hbm, k), (q_hbm, q), (v_hbm, v), (w_hbm, w.at[x]), (gain_hbm, gain)))
    ]
    for copy in loads[:3]:
        copy.start()

    def chunk(ref, h, j):
        return ref[j * CHUNK : (j + 1) * CHUNK, h * DH : (h + 1) * DH]

    def worker_z(i):
        return (c * pair + i) * spacing

    def in_copy(kind, i, slot, device_id):
        src, dst = ((s_chip, s_arr), (cp_chip, cp_arr))[kind]
        return remote(src.at[i], dst.at[slot], in_send.at[kind, i], in_recv.at[kind, slot], device_id)

    def send_in(kind):
        for i in range(pair):
            here = z == worker_z(i)
            copy = in_copy(kind, i, z, {"seq_1": worker_z(i)})

            @pl.when(jnp.logical_not(here))
            def _(copy=copy):
                copy.start()

            @pl.when(here)
            def _(i=i):
                src, dst = ((s_chip, s_arr), (cp_chip, cp_arr))[kind]
                dst[z] = src[i]

    def drain_in(kind):
        for i in range(pair):
            @pl.when(z != worker_z(i))
            def _(i=i):
                in_copy(kind, i, z, {"seq_1": worker_z(i)}).wait_send()

    def wait_in(kind):
        for d in range(1, nz):
            in_copy(kind, 0, modz(d), {"seq_1": modz(d)}).wait_recv()

    def back_copy(kind, i, t):
        src, dst = ((s_back, s_pre), (p_back, p_pre))[kind]
        return remote(src.at[t], dst.at[i], back_send.at[kind, t], back_recv.at[kind, i], {"seq_1": t})

    def takes_back(t):
        return (z != t) & (y > 0) if t == 0 else z != t

    def send_back(kind):
        for t in range(nz):

            @pl.when(takes_back(t))
            def _(t=t):
                back_copy(kind, my_head, t).start()

        src, dst = ((s_back, s_pre), (p_back, p_pre))[kind]
        dst[my_head] = src[z]

    def drain_back(kind):
        for t in range(nz):

            @pl.when(takes_back(t))
            def _(t=t):
                back_copy(kind, my_head, t).wait_send()

    def wait_back(kind, i):
        @pl.when((z != worker_z(i)) & jnp.logical_not(is_first))
        def _():
            back_copy(kind, i, 0).wait_recv()

    def total_copy(kind, d, slot):
        part = (pl.ds(0, 1), pl.ds(1, 2))[kind]
        return remote(
            y_out.at[part], y_in.at[slot, part], y_send.at[kind, d], y_recv.at[kind, slot], {"seq_0": mody(d)}
        )

    def send_totals(kind):
        for d in FAR_FIRST:
            if d < ny:

                @pl.when(y + d < ny)
                def _(d=d):
                    total_copy(kind, d, y).start()

    def wait_totals(kind):
        for d in range(1, ny):

            @pl.when(y >= d)
            def _(d=d):
                total_copy(kind, d, y - d).wait_recv()

    def drain_totals(kind):
        for d in range(1, ny):

            @pl.when(y + d < ny)
            def _(d=d):
                total_copy(kind, d, y).wait_send()

    def s_base_until(limit):
        base = jnp.zeros((DH, DH), F32)
        for r in range(ny - 1):
            base = base + jnp.where(r < limit, y_in[r, 0].astype(F32), 0.0)
        return base

    colour = lax.rem(y + z, 2)
    piece_rows = w.shape[1] // 8

    def rows_of(colour_of, core_of, half, part=None):
        first = colour_of * (4 * piece_rows) + core_of * (2 * piece_rows) + half * piece_rows
        count = piece_rows
        if part is not None:
            count = piece_rows // 2
            first = first + part * count
        return pl.ds(pl.multiple_of(first, count), count)

    def piece(i, colour_of, core_of, part=None):
        offset, half = X_PIECES[i]
        return w.at[modx(offset), rows_of(colour_of, core_of, half, part)]

    def w_copy(number, src, dst, device_id):
        return remote(src, dst, w_send.at[number], w_recv.at[number], device_id)

    def unit(number, part):
        return 2 * number + (part or 0)

    def x_send(number, part):
        offset, half = X_PIECES[number]
        if number < 4:
            rows = rows_of(colour, c, half, part)
            return w_copy(unit(number, part), w_hbm.at[rows], w.at[x, rows], {"head": modx(-offset)})
        src = piece(number - 4, colour, c, part)
        return w_copy(unit(number, part), src, src, {"head": modx(1 if number == 4 else -1)})

    def x_arrival(number, part):
        ref = piece(number, colour, c, part)
        return w_copy(unit(number, part), ref, ref, {"head": modx(1)})

    def plane_copy(number, part, colour_of):
        ref = piece(number, colour_of, c, part)
        step = 1 if X_PIECES[number][1] == 0 else -1
        peer = {"seq_1": modz(step + nz)} if number >= 4 else {"seq_0": mody(step)}
        return w_copy(12 + unit(number, part), ref, ref, peer)

    def block_copy(n, colour_of, over_y=False):
        first = colour_of * (4 * piece_rows) + c * (2 * piece_rows) + piece_rows // 2 + n * (piece_rows // 4)
        ref = w.at[modx(2), pl.ds(pl.multiple_of(first, piece_rows // 4), piece_rows // 4)]
        if over_y:
            return remote(ref, ref, w_send.at[43], w_recv.at[12 + unit(4, 1)], {"seq_0": mody(-1)})
        return w_copy((12 + unit(4, 1), 42)[n], ref, ref, {"seq_1": modz(1)})

    def send_blocks():
        @pl.when(z == 0)
        def _():
            block_copy(0, colour, True).start()

        @pl.when(z != nz - 1)
        def _():
            block_copy(0, colour).start()

        start(block_copy(1, colour))
        pending.append(drain_blocks)

    def drain_blocks():
        @pl.when(z == 0)
        def _():
            block_copy(0, colour, True).wait_send()

        @pl.when(z != nz - 1)
        def _():
            block_copy(0, colour).wait_send()

    def core_copy(number, core_of):
        ref = piece(number, colour, core_of)
        return w_copy(24 + number, ref, ref, {"seq_2": 1 - c})

    def core_plane_copy(number, part, core_of):
        ref = piece(number, 1 - colour, core_of, part)
        return w_copy(30 + unit(number, part), ref, ref, {"seq_2": 1 - c})

    def relay_x(*units):
        for number, part in units:
            x_arrival(number, part).wait_recv()
            if number < 2:
                start(x_send(4 + number, part))
            if (number, part) == (4, 1):
                send_blocks()
            else:
                start(plane_copy(number, part, colour))
        for number, part in units:
            if part != 0:
                start(core_copy(number, c))

    def arrive_plane(number):
        for part in PARTS[number]:
            plane_copy(number, part, 1 - colour).wait_recv()
        start(core_plane_copy(number, None, c))

    def arrive_last():
        for part in range(2):
            for number in (5, 4):
                if (number, part) == (4, 1):
                    block_copy(0, 1 - colour).wait_recv()
                    block_copy(1, 1 - colour).wait_recv()
                else:
                    plane_copy(number, part, 1 - colour).wait_recv()
                start(core_plane_copy(number, part, c))

    row = lax.broadcasted_iota(jnp.int32, (CHUNK, CHUNK), 0)
    col = lax.broadcasted_iota(jnp.int32, (CHUNK, CHUNK), 1)
    loads[0].wait()
    for h in range(heads):
        first = dot(chunk(k, h, 0), chunk(k, h, 0), 0, 0)
        s_first[h] = first.astype(BF16)
        s_loc[h // pair, h % pair] = (first + dot(chunk(k, h, 1), chunk(k, h, 1), 0, 0)).astype(BF16)
    loads[1].wait()
    loads[2].wait()
    strict, causal = col < row, col <= row
    blocks = [(h, j) for h in range(heads) for j in range(2)]
    for h in range(heads):
        v_t[h] = v[:, h * DH : (h + 1) * DH].T
    scores = [jnp.where(strict, dot(chunk(q, h, j), chunk(k, h, j), 1, 1), 0.0).astype(BF16) for h, j in blocks]
    pl.semaphore_wait(barrier, nx - 1 + ny - 1 + 1 + pair - is_worker.astype(jnp.int32) + 2 * is_first.astype(jnp.int32))
    for copy in loads[3:]:
        copy.start()
    sibling = {"seq_2": 1 - c}
    s_core = remote(s_loc.at[1 - c], s_sib, core_send.at[0], core_recv.at[0], sibling)
    cp_core = remote(cp_loc.at[1 - c], cp_sib, core_send.at[1], core_recv.at[1], sibling)
    start(s_core)
    for number, part in ((0, 0), (1, 0), (0, 1), (1, 1), (2, None), (3, None)):
        start(x_send(number, part))

    fs = []
    for n, (h, j) in enumerate(blocks):
        f = dot(scores[n], chunk(k, h, j), 1, 0)
        if j == 1:
            f = f + dot(chunk(q, h, j), s_first[h], 1, 0)
        f_loc[j * CHUNK : (j + 1) * CHUNK, h * DH : (h + 1) * DH] = f
        fs.append(f.astype(BF16))
    for h in range(heads):
        cross = dot(v_t[h], q[:, h * DH : (h + 1) * DH], 1, 0)
        pairs = dot(v_t[h, :, :CHUNK], fs[2 * h], 1, 0) + dot(v_t[h, :, CHUNK:], fs[2 * h + 1], 1, 0)
        cp_loc[h // pair, h % pair, 0] = cross.astype(BF16)
        cp_loc[h // pair, h % pair, 1] = pairs.astype(BF16)

    start(cp_core)
    s_core.wait_recv()
    for i in range(pair):
        s_chip[i] = (s_loc[c, i].astype(F32) + s_sib[i].astype(F32)).astype(BF16)
    send_in(0)
    cp_core.wait_recv()
    for i in range(pair):
        mine, other = cp_loc[c, i], cp_sib[i]
        early = jnp.where(c == 0, s_loc[c, i], s_sib[i])
        late = jnp.where(c == 0, other[0], mine[0])
        cp_chip[i, 0] = (mine[0].astype(F32) + other[0].astype(F32)).astype(BF16)
        cp_chip[i, 1] = (mine[1].astype(F32) + other[1].astype(F32) + dot(late, early, 1, 0)).astype(BF16)
    send_in(1)

    def by_core(i):
        own, other = cp_loc[c, i], cp_sib[i]
        return jnp.where(c == 0, s_loc[c, i], s_sib[i]), jnp.where(c == 0, own[0], other[0]), jnp.where(c == 0, own[1], other[1])

    def s_before_core(i, chip):
        s_early, c_early, p_early = by_core(i)
        later = (chip.astype(F32) + s_early.astype(F32)).astype(BF16)
        s_mine[c, i] = jnp.where(c == 0, chip, later)
        s_other[i] = jnp.where(c == 0, later, chip)
        p_step[i] = p_early.astype(F32) + dot(c_early, chip, 1, 0)

    def p_before_core(i, chip):
        later = (chip.astype(F32) + p_step[i]).astype(BF16)
        p_mine[c, i] = jnp.where(c == 0, chip, later)
        p_other[i] = jnp.where(c == 0, later, chip)

    swap_s = remote(s_other, s_mine.at[c], core_send.at[2], core_recv.at[2], sibling)

    def swap_p(i, slot):
        return remote(p_other.at[i], p_mine.at[slot, i], core_send.at[3 + i], core_recv.at[3 + i], sibling)

    swaps_p = [swap_p(i, c) for i in range(pair)]

    @pl.when(is_first)
    def _():
        nothing = jnp.zeros((DH, DH), BF16)
        for i in range(pair):
            s_before_core(i, nothing)
            p_before_core(i, nothing)
        swap_s.start()
        for copy in swaps_p:
            copy.start()

    relay_x((0, 0), (1, 0))

    @pl.when(is_worker)
    def _():
        wait_in(0)
        total = jnp.zeros((DH, DH), F32)
        for r in range(nz):
            s_run[r] = total
            total = total + s_arr[r].astype(F32)
        y_out[0] = total.astype(BF16)
        send_totals(0)
        y_in[y, 0] = total.astype(BF16)

    relay_x((0, 1), (1, 1))

    @pl.when(is_worker)
    def _():
        wait_in(1)
        pairs = jnp.zeros((DH, DH), F32)
        cross = jnp.zeros((DH, DH), F32)
        for r in range(nz):
            p_run[r] = pairs
            c_run[r] = cross.astype(BF16)
            pairs = pairs + (cp_arr[r, 1].astype(F32) + dot(cp_arr[r, 0], s_run[r].astype(BF16), 1, 0))
            cross = cross + cp_arr[r, 0].astype(F32)
        y_out[1] = cross.astype(BF16)
        y_out[2] = pairs.astype(BF16)
        send_totals(1)
        y_in[y, 1] = cross.astype(BF16)
        y_in[y, 2] = pairs.astype(BF16)
        wait_totals(0)
        s_base = s_base_until(y)
        for r in range(nz):
            s_back[r] = (s_run[r] + s_base).astype(BF16)
        send_back(0)
        s_base = s_base.astype(BF16)
        for r in range(nz):
            p_run[r] = p_run[r] + dot(c_run[r], s_base, 1, 0)
        before = [s_base_until(r).astype(BF16) for r in range(ny - 1)]
        wait_totals(1)
        p_base = jnp.zeros((DH, DH), F32)
        for r in range(ny - 1):
            line = y_in[r, 2].astype(F32) + dot(y_in[r, 1], before[r], 1, 0)
            p_base = p_base + jnp.where(r < y, line, 0.0)
        for r in range(nz):
            p_back[r] = (p_run[r] + p_base).astype(BF16)
        send_back(1)

    for i in range(pair):
        wait_back(0, i)

    @pl.when(jnp.logical_not(is_first))
    def _():
        for i in range(pair):
            s_before_core(i, s_pre[i])
        swap_s.start()

    pending.append(swap_s.wait_send)
    relay_x((2, None), (3, None))
    arrive_plane(0)
    arrive_plane(1)
    remote(s_other, s_mine.at[1 - c], core_send.at[2], core_recv.at[2], sibling).wait_recv()

    fs = []
    for h, j in blocks:
        f = chunk(f_loc, h, j) + dot(chunk(q, h, j), s_mine[h // pair, h % pair], 1, 0)
        fs.append(f.astype(BF16))
    mixing = [
        jnp.where(causal, dot(chunk(q, h, j), fs[n], 1, 1), 0.0).astype(BF16) for n, (h, j) in enumerate(blocks)
    ]
    for n, (h, j) in enumerate(blocks):
        o_part[j * CHUNK : (j + 1) * CHUNK, h * DH : (h + 1) * DH] = dot(mixing[n], chunk(v, h, j), 1, 0)
    for h in range(heads):
        p_first[h // pair, h % pair] = dot(v_t[h, :, :CHUNK], fs[2 * h], 1, 0)
    relay_x((4, 0), (5, 0), (4, 1), (5, 1))

    rows_x = tokens // nx
    loads[4].wait()

    def head_cols(g, i):
        return pl.ds(pl.multiple_of(g * (pair * DH) + i * DH, DH), DH)

    def n_copy(d, g, i, slot):
        cols = head_cols(g, i)
        number = g * pair + i
        return remote(
            n_out.at[d, :, cols], n_in.at[slot, :, cols], n_send.at[d, number], n_recv.at[slot, number], {"head": modx(d)}
        )

    for i in range(pair):
        wait_back(1, i)

        @pl.when(jnp.logical_not(is_first))
        def _(i=i):
            p_before_core(i, p_pre[i])
            swaps_p[i].start()

        pending.append(swaps_p[i].wait_send)
        for g in (c, 1 - c):
            if g is not c:
                swap_p(i, g).wait_recv()
            cols = head_cols(g, i)
            p_h = p_mine[g, i]
            p_fin[0] = p_h
            p_fin[1] = (p_h.astype(F32) + p_first[g, i]).astype(BF16)
            for d in (2, 1, 3, 0):
                target = modx(d)
                rows = pl.ds(pl.multiple_of(target * rows_x, rows_x), rows_x)
                part = target // (CHUNK // rows_x)
                attended = o_part[rows, cols] + dot(q[rows, cols], p_fin[part], 1, 1)
                mean_square = jnp.mean(attended * attended, axis=-1, keepdims=True)
                n_out[d, :, cols] = (attended * lax.rsqrt(mean_square + EPS) * gain[:, cols]).astype(BF16)
                if d:
                    start(n_copy(d, g, i, x))

    loads[3].wait()
    tile = 512
    n_cols = out_ref.shape[1]

    def project(rows_in, slot, quarter, first, last):
        for begin in range(0, n_cols, tile):
            cols = slice(begin, begin + tile)
            part = dot(rows_in[slot], w[quarter, :, cols], 1, 0)
            if not first:
                part = part + acc[:, cols]
            if last:
                out_ref[:, cols] = part.astype(BF16)
            else:
                acc[:, cols] = part

    project(n_out, 0, x, True, False)
    arrive_plane(2)
    arrive_plane(3)
    arrive_last()
    for offset in (-1, 1, 2):
        quarter = modx(offset)
        for number, (of, _) in enumerate(X_PIECES):
            if of == offset:
                core_copy(number, 1 - c).wait_recv()
                for part in PARTS[number] if number >= 4 else (None,):
                    core_plane_copy(number, part, 1 - c).wait_recv()
        for head in range(heads):
            n_copy(offset % nx, head // pair, head % pair, quarter).wait_recv()
        project(n_in, quarter, quarter, False, offset == 2)

    for wait in pending:
        wait()
    drain_in(0)
    drain_in(1)

    @pl.when(is_worker)
    def _():
        for kind in range(2):
            drain_back(kind)
            drain_totals(kind)


def shards(ny, nz, nx, queries, key_vectors, value_vectors, norm_gain, out_weight):
    tokens, width = queries.shape
    heads = width // DH
    pair = heads // 2
    depth, n_cols = out_weight.shape

    def matrices(*lead, kind=BF16):
        return pltpu.VMEM(lead + (DH, DH), kind)

    operands = (queries, key_vectors, value_vectors, norm_gain.reshape(1, width), out_weight)
    return pl.pallas_call(
        functools.partial(kernel, ny, nz, nx),
        out_shape=jax.ShapeDtypeStruct((tokens // nx, n_cols), BF16),
        in_specs=[pl.BlockSpec(memory_space=pltpu.HBM)] * 5,
        out_specs=pl.BlockSpec(memory_space=pltpu.VMEM),
        scratch_shapes=[
            pltpu.VMEM((tokens, width), BF16),
            pltpu.VMEM((tokens, width), BF16),
            pltpu.VMEM((tokens, width), BF16),
            pltpu.VMEM((nx, depth, n_cols), BF16),
            pltpu.VMEM((1, width), F32),
            matrices(heads),
            matrices(2, pair),
            matrices(2, pair, 2),
            matrices(pair),
            matrices(pair, 2),
            matrices(pair),
            matrices(pair, 2),
            matrices(nz),
            matrices(nz, 2),
            matrices(nz, kind=F32),
            matrices(nz, kind=F32),
            matrices(nz),
            matrices(nz),
            matrices(nz),
            matrices(3),
            matrices(ny, 3),
            matrices(pair),
            matrices(pair),
            matrices(pair, kind=F32),
            matrices(pair),
            matrices(pair),
            matrices(2, pair),
            matrices(2, pair),
            pltpu.VMEM((heads, DH, tokens), BF16),
            pltpu.VMEM((tokens, width), F32),
            matrices(2, pair, kind=F32),
            pltpu.VMEM((tokens, width), F32),
            matrices(2),
            pltpu.VMEM((nx, tokens // nx, width), BF16),
            pltpu.VMEM((nx, tokens // nx, width), BF16),
            pltpu.VMEM((tokens // nx, n_cols), F32),
            pltpu.SemaphoreType.DMA((5,)),
            pltpu.SemaphoreType.DMA((3 + pair,)),
            pltpu.SemaphoreType.DMA((3 + pair,)),
            pltpu.SemaphoreType.DMA((2, pair)),
            pltpu.SemaphoreType.DMA((2, nz)),
            pltpu.SemaphoreType.DMA((2, nz)),
            pltpu.SemaphoreType.DMA((2, pair)),
            pltpu.SemaphoreType.DMA((2, ny)),
            pltpu.SemaphoreType.DMA((2, ny)),
            pltpu.SemaphoreType.DMA((nx, heads)),
            pltpu.SemaphoreType.DMA((nx, heads)),
            pltpu.SemaphoreType.DMA((44,)),
            pltpu.SemaphoreType.DMA((44,)),
        ],
        compiler_params=pltpu.CompilerParams(
            collective_id=0, has_side_effects=True, vmem_limit_bytes=48 * 1024 * 1024
        ),
    )(*[pltpu.with_memory_space_constraint(array, pltpu.HBM) for array in operands])


def solution(mesh):
    seq, nx = mesh.shape["seq"], mesh.shape["head"]
    ny = 4 if seq == 64 else 2
    nz = seq // (2 * ny)
    split = Mesh(mesh.devices.reshape(ny, nz, 2, nx), SEQ_HEAD)
    in_specs = (P(SEQ, "head"), P(SEQ, "head"), P(SEQ, "head"), P("head"), P("head", None))
    out_specs = P(SEQ_HEAD, None)
    return jax.shard_map(
        functools.partial(shards, ny, nz, nx), mesh=split, in_specs=in_specs, out_specs=out_specs, check_vma=False
    )
```

```python
import functools

import jax
import jax.numpy as jnp
from jax import lax
from jax.experimental import pallas as pl
from jax.experimental.pallas import tpu as pltpu
from jax.sharding import Mesh
from jax.sharding import PartitionSpec as P

DH = 128
SEQ = ("seq_0", "seq_1", "seq_2")
SEQ_HEAD = ("seq_0", "seq_1", "seq_2", "head")
F32 = jnp.float32
BF16 = jnp.bfloat16
CHUNK = 256
EPS = 1e-06
FAR_FIRST = (4, 3, 5, 2, 6, 1, 7)

PARTS = ((0, 1), (0, 1), (None,), (None,), (0, 1), (0, 1))
X_PIECES = ((-1, 0), (1, 1), (-1, 1), (1, 0), (2, 0), (2, 1))


def dot(a, b, ca, cb):
    return lax.dot_general(a, b, (((ca,), (cb,)), ((), ())), preferred_element_type=F32)


def kernel(
    ny,
    nz,
    nx,
    q_hbm,
    k_hbm,
    v_hbm,
    gain_hbm,
    w_hbm,
    out_ref,
    q,
    k,
    v,
    w,
    gain,
    s_first,
    s_loc,
    cp_loc,
    s_sib,
    cp_sib,
    s_chip,
    cp_chip,
    s_arr,
    cp_arr,
    s_run,
    p_run,
    c_run,
    s_back,
    p_back,
    y_out,
    y_in,
    s_pre,
    p_pre,
    p_step,
    s_other,
    p_other,
    s_mine,
    p_mine,
    v_t,
    f_loc,
    p_first,
    o_part,
    p_fin,
    n_out,
    n_in,
    acc,
    load_sem,
    core_send,
    core_recv,
    in_send,
    in_recv,
    back_send,
    back_recv,
    y_send,
    y_recv,
    n_send,
    n_recv,
    w_send,
    w_recv,
):
    tokens, width = q.shape
    heads = width // DH
    pair = heads // 2
    y, z, c, x = (lax.axis_index(name) for name in SEQ_HEAD)

    def modx(i):
        return lax.rem(x + i + nx, nx)

    def mody(i):
        return lax.rem(y + i + ny, ny)

    def modz(i):
        return lax.rem(z + i, nz)

    pending = []

    def remote(src, dst, send_sem, recv_sem, device_id):
        return pltpu.make_async_remote_copy(
            src_ref=src,
            dst_ref=dst,
            send_sem=send_sem,
            recv_sem=recv_sem,
            device_id=device_id,
            device_id_type=pl.DeviceIdType.MESH,
        )

    def start(copy):
        copy.start()
        pending.append(copy.wait_send)

    spacing = nz // heads
    is_worker = (lax.rem(z, spacing) == 0) & (z // (spacing * pair) == c)
    my_head = lax.rem(z // spacing, pair)

    barrier = pltpu.get_barrier_semaphore()

    def greet(peer):
        pl.semaphore_signal(barrier, inc=1, device_id=peer, device_id_type=pl.DeviceIdType.MESH)

    for d in range(1, ny):
        greet({"seq_0": mody(d)})
    for d in range(1, nx):
        greet({"head": modx(d)})
    greet({"seq_2": 1 - c})

    is_first = (y == 0) & (z == 0)

    @pl.when((y == 0) & ((z == 1) | (z == nz - 1)))
    def _():
        greet({"seq_1": 0})

    @pl.when(is_worker)
    def _():
        for d in FAR_FIRST:
            if d < nz:
                greet({"seq_1": modz(d)})

    loads = [
        pltpu.make_async_copy(src, dst, load_sem.at[i])
        for i, (src, dst) in enumerate(((k_hbm, k), (q_hbm, q), (v_hbm, v), (w_hbm, w.at[x]), (gain_hbm, gain)))
    ]
    for copy in loads[:3]:
        copy.start()

    def chunk(ref, h, j):
        return ref[j * CHUNK : (j + 1) * CHUNK, h * DH : (h + 1) * DH]

    def worker_z(i):
        return (c * pair + i) * spacing

    def in_copy(kind, i, slot, device_id):
        src, dst = ((s_chip, s_arr), (cp_chip, cp_arr))[kind]
        return remote(src.at[i], dst.at[slot], in_send.at[kind, i], in_recv.at[kind, slot], device_id)

    def send_in(kind):
        for i in range(pair):
            here = z == worker_z(i)
            copy = in_copy(kind, i, z, {"seq_1": worker_z(i)})

            @pl.when(jnp.logical_not(here))
            def _(copy=copy):
                copy.start()

            @pl.when(here)
            def _(i=i):
                src, dst = ((s_chip, s_arr), (cp_chip, cp_arr))[kind]
                dst[z] = src[i]

    def drain_in(kind):
        for i in range(pair):
            @pl.when(z != worker_z(i))
            def _(i=i):
                in_copy(kind, i, z, {"seq_1": worker_z(i)}).wait_send()

    def wait_in(kind):
        for d in range(1, nz):
            in_copy(kind, 0, modz(d), {"seq_1": modz(d)}).wait_recv()

    def back_copy(kind, i, t):
        src, dst = ((s_back, s_pre), (p_back, p_pre))[kind]
        return remote(src.at[t], dst.at[i], back_send.at[kind, t], back_recv.at[kind, i], {"seq_1": t})

    def takes_back(t):
        return (z != t) & (y > 0) if t == 0 else z != t

    def send_back(kind):
        for t in range(nz):

            @pl.when(takes_back(t))
            def _(t=t):
                back_copy(kind, my_head, t).start()

        src, dst = ((s_back, s_pre), (p_back, p_pre))[kind]
        dst[my_head] = src[z]

    def drain_back(kind):
        for t in range(nz):

            @pl.when(takes_back(t))
            def _(t=t):
                back_copy(kind, my_head, t).wait_send()

    def wait_back(kind, i):
        @pl.when((z != worker_z(i)) & jnp.logical_not(is_first))
        def _():
            back_copy(kind, i, 0).wait_recv()

    def total_copy(kind, d, slot):
        part = (pl.ds(0, 1), pl.ds(1, 2))[kind]
        return remote(
            y_out.at[part], y_in.at[slot, part], y_send.at[kind, d], y_recv.at[kind, slot], {"seq_0": mody(d)}
        )

    def send_totals(kind):
        for d in FAR_FIRST:
            if d < ny:

                @pl.when(y + d < ny)
                def _(d=d):
                    total_copy(kind, d, y).start()

    def wait_totals(kind):
        for d in range(1, ny):

            @pl.when(y >= d)
            def _(d=d):
                total_copy(kind, d, y - d).wait_recv()

    def drain_totals(kind):
        for d in range(1, ny):

            @pl.when(y + d < ny)
            def _(d=d):
                total_copy(kind, d, y).wait_send()

    def s_base_until(limit):
        base = jnp.zeros((DH, DH), F32)
        for r in range(ny - 1):
            base = base + jnp.where(r < limit, y_in[r, 0].astype(F32), 0.0)
        return base

    colour = lax.rem(y + z, 2)
    piece_rows = w.shape[1] // 8

    def rows_of(colour_of, core_of, half, part=None):
        first = colour_of * (4 * piece_rows) + core_of * (2 * piece_rows) + half * piece_rows
        count = piece_rows
        if part is not None:
            count = piece_rows // 2
            first = first + part * count
        return pl.ds(pl.multiple_of(first, count), count)

    def piece(i, colour_of, core_of, part=None):
        offset, half = X_PIECES[i]
        return w.at[modx(offset), rows_of(colour_of, core_of, half, part)]

    def w_copy(number, src, dst, device_id):
        return remote(src, dst, w_send.at[number], w_recv.at[number], device_id)

    def unit(number, part):
        return 2 * number + (part or 0)

    def x_send(number, part):
        offset, half = X_PIECES[number]
        if number < 4:
            rows = rows_of(colour, c, half, part)
            return w_copy(unit(number, part), w_hbm.at[rows], w.at[x, rows], {"head": modx(-offset)})
        src = piece(number - 4, colour, c, part)
        return w_copy(unit(number, part), src, src, {"head": modx(1 if number == 4 else -1)})

    def x_arrival(number, part):
        ref = piece(number, colour, c, part)
        return w_copy(unit(number, part), ref, ref, {"head": modx(1)})

    def plane_copy(number, part, colour_of):
        ref = piece(number, colour_of, c, part)
        step = 1 if X_PIECES[number][1] == 0 else -1
        peer = {"seq_1": modz(step + nz)} if number >= 4 else {"seq_0": mody(step)}
        return w_copy(12 + unit(number, part), ref, ref, peer)

    def block_copy(n, colour_of, over_y=False):
        first = colour_of * (4 * piece_rows) + c * (2 * piece_rows) + piece_rows // 2 + n * (piece_rows // 4)
        ref = w.at[modx(2), pl.ds(pl.multiple_of(first, piece_rows // 4), piece_rows // 4)]
        if over_y:
            return remote(ref, ref, w_send.at[43], w_recv.at[12 + unit(4, 1)], {"seq_0": mody(-1)})
        return w_copy((12 + unit(4, 1), 42)[n], ref, ref, {"seq_1": modz(1)})

    def send_blocks():
        @pl.when(z == 0)
        def _():
            block_copy(0, colour, True).start()

        @pl.when(z != nz - 1)
        def _():
            block_copy(0, colour).start()

        start(block_copy(1, colour))
        pending.append(drain_blocks)

    def drain_blocks():
        @pl.when(z == 0)
        def _():
            block_copy(0, colour, True).wait_send()

        @pl.when(z != nz - 1)
        def _():
            block_copy(0, colour).wait_send()

    def core_copy(number, core_of):
        ref = piece(number, colour, core_of)
        return w_copy(24 + number, ref, ref, {"seq_2": 1 - c})

    def core_plane_copy(number, part, core_of):
        ref = piece(number, 1 - colour, core_of, part)
        return w_copy(30 + unit(number, part), ref, ref, {"seq_2": 1 - c})

    def relay_x(*units):
        for number, part in units:
            x_arrival(number, part).wait_recv()
            if number < 2:
                start(x_send(4 + number, part))
            if (number, part) == (4, 1):
                send_blocks()
            else:
                start(plane_copy(number, part, colour))
        for number, part in units:
            if part != 0:
                start(core_copy(number, c))

    def arrive_plane(number):
        for part in PARTS[number]:
            plane_copy(number, part, 1 - colour).wait_recv()
        start(core_plane_copy(number, None, c))

    def arrive_last():
        for part in range(2):
            for number in (5, 4):
                if (number, part) == (4, 1):
                    block_copy(0, 1 - colour).wait_recv()
                    block_copy(1, 1 - colour).wait_recv()
                else:
                    plane_copy(number, part, 1 - colour).wait_recv()
                start(core_plane_copy(number, part, c))

    row = lax.broadcasted_iota(jnp.int32, (CHUNK, CHUNK), 0)
    col = lax.broadcasted_iota(jnp.int32, (CHUNK, CHUNK), 1)
    loads[0].wait()
    for h in range(heads):
        first = dot(chunk(k, h, 0), chunk(k, h, 0), 0, 0)
        s_first[h] = first.astype(BF16)
        s_loc[h // pair, h % pair] = (first + dot(chunk(k, h, 1), chunk(k, h, 1), 0, 0)).astype(BF16)
    loads[1].wait()
    loads[2].wait()
    strict, causal = col < row, col <= row
    blocks = [(h, j) for h in range(heads) for j in range(2)]
    for h in range(heads):
        v_t[h] = v[:, h * DH : (h + 1) * DH].T
    scores = [jnp.where(strict, dot(chunk(q, h, j), chunk(k, h, j), 1, 1), 0.0).astype(BF16) for h, j in blocks]
    pl.semaphore_wait(barrier, nx - 1 + ny - 1 + 1 + pair - is_worker.astype(jnp.int32) + 2 * is_first.astype(jnp.int32))
    for copy in loads[3:]:
        copy.start()
    sibling = {"seq_2": 1 - c}
    s_core = remote(s_loc.at[1 - c], s_sib, core_send.at[0], core_recv.at[0], sibling)
    cp_core = remote(cp_loc.at[1 - c], cp_sib, core_send.at[1], core_recv.at[1], sibling)
    start(s_core)
    for number, part in ((0, 0), (1, 0), (0, 1), (1, 1), (2, None), (3, None)):
        start(x_send(number, part))

    fs = []
    for n, (h, j) in enumerate(blocks):
        f = dot(scores[n], chunk(k, h, j), 1, 0)
        if j == 1:
            f = f + dot(chunk(q, h, j), s_first[h], 1, 0)
        f_loc[j * CHUNK : (j + 1) * CHUNK, h * DH : (h + 1) * DH] = f
        fs.append(f.astype(BF16))
    for h in range(heads):
        cross = dot(v_t[h], q[:, h * DH : (h + 1) * DH], 1, 0)
        pairs = dot(v_t[h, :, :CHUNK], fs[2 * h], 1, 0) + dot(v_t[h, :, CHUNK:], fs[2 * h + 1], 1, 0)
        cp_loc[h // pair, h % pair, 0] = cross.astype(BF16)
        cp_loc[h // pair, h % pair, 1] = pairs.astype(BF16)

    start(cp_core)
    s_core.wait_recv()
    for i in range(pair):
        s_chip[i] = (s_loc[c, i].astype(F32) + s_sib[i].astype(F32)).astype(BF16)
    send_in(0)
    cp_core.wait_recv()
    for i in range(pair):
        mine, other = cp_loc[c, i], cp_sib[i]
        early = jnp.where(c == 0, s_loc[c, i], s_sib[i])
        late = jnp.where(c == 0, other[0], mine[0])
        cp_chip[i, 0] = (mine[0].astype(F32) + other[0].astype(F32)).astype(BF16)
        cp_chip[i, 1] = (mine[1].astype(F32) + other[1].astype(F32) + dot(late, early, 1, 0)).astype(BF16)
    send_in(1)

    def by_core(i):
        own, other = cp_loc[c, i], cp_sib[i]
        return jnp.where(c == 0, s_loc[c, i], s_sib[i]), jnp.where(c == 0, own[0], other[0]), jnp.where(c == 0, own[1], other[1])

    def s_before_core(i, chip):
        s_early, c_early, p_early = by_core(i)
        later = (chip.astype(F32) + s_early.astype(F32)).astype(BF16)
        s_mine[c, i] = jnp.where(c == 0, chip, later)
        s_other[i] = jnp.where(c == 0, later, chip)
        p_step[i] = p_early.astype(F32) + dot(c_early, chip, 1, 0)

    def p_before_core(i, chip):
        later = (chip.astype(F32) + p_step[i]).astype(BF16)
        p_mine[c, i] = jnp.where(c == 0, chip, later)
        p_other[i] = jnp.where(c == 0, later, chip)

    swap_s = remote(s_other, s_mine.at[c], core_send.at[2], core_recv.at[2], sibling)

    def swap_p(i, slot):
        return remote(p_other.at[i], p_mine.at[slot, i], core_send.at[3 + i], core_recv.at[3 + i], sibling)

    swaps_p = [swap_p(i, c) for i in range(pair)]

    @pl.when(is_first)
    def _():
        nothing = jnp.zeros((DH, DH), BF16)
        for i in range(pair):
            s_before_core(i, nothing)
            p_before_core(i, nothing)
        swap_s.start()
        for copy in swaps_p:
            copy.start()

    relay_x((0, 0), (1, 0))

    @pl.when(is_worker)
    def _():
        wait_in(0)
        total = jnp.zeros((DH, DH), F32)
        for r in range(nz):
            s_run[r] = total
            total = total + s_arr[r].astype(F32)
        y_out[0] = total.astype(BF16)
        send_totals(0)
        y_in[y, 0] = total.astype(BF16)

    relay_x((0, 1), (1, 1))

    @pl.when(is_worker)
    def _():
        wait_in(1)
        pairs = jnp.zeros((DH, DH), F32)
        cross = jnp.zeros((DH, DH), F32)
        for r in range(nz):
            p_run[r] = pairs
            c_run[r] = cross.astype(BF16)
            pairs = pairs + (cp_arr[r, 1].astype(F32) + dot(cp_arr[r, 0], s_run[r].astype(BF16), 1, 0))
            cross = cross + cp_arr[r, 0].astype(F32)
        y_out[1] = cross.astype(BF16)
        y_out[2] = pairs.astype(BF16)
        send_totals(1)
        y_in[y, 1] = cross.astype(BF16)
        y_in[y, 2] = pairs.astype(BF16)
        wait_totals(0)
        s_base = s_base_until(y)
        for r in range(nz):
            s_back[r] = (s_run[r] + s_base).astype(BF16)
        send_back(0)
        s_base = s_base.astype(BF16)
        for r in range(nz):
            p_run[r] = p_run[r] + dot(c_run[r], s_base, 1, 0)
        before = [s_base_until(r).astype(BF16) for r in range(ny - 1)]
        wait_totals(1)
        p_base = jnp.zeros((DH, DH), F32)
        for r in range(ny - 1):
            line = y_in[r, 2].astype(F32) + dot(y_in[r, 1], before[r], 1, 0)
            p_base = p_base + jnp.where(r < y, line, 0.0)
        for r in range(nz):
            p_back[r] = (p_run[r] + p_base).astype(BF16)
        send_back(1)

    @pl.when(y == ny - 1)
    def _():
        x_arrival(3, None).wait_recv()
        plane_copy(3, None, colour).start()

    for i in range(pair):
        wait_back(0, i)

    @pl.when(jnp.logical_not(is_first))
    def _():
        for i in range(pair):
            s_before_core(i, s_pre[i])
        swap_s.start()

    pending.append(swap_s.wait_send)
    relay_x((2, None))

    @pl.when(y != ny - 1)
    def _():
        x_arrival(3, None).wait_recv()
        plane_copy(3, None, colour).start()

    pending.append(plane_copy(3, None, colour).wait_send)
    start(core_copy(3, c))
    arrive_plane(0)
    arrive_plane(1)
    remote(s_other, s_mine.at[1 - c], core_send.at[2], core_recv.at[2], sibling).wait_recv()

    fs = []
    for h, j in blocks:
        f = chunk(f_loc, h, j) + dot(chunk(q, h, j), s_mine[h // pair, h % pair], 1, 0)
        fs.append(f.astype(BF16))
    mixing = [
        jnp.where(causal, dot(chunk(q, h, j), fs[n], 1, 1), 0.0).astype(BF16) for n, (h, j) in enumerate(blocks)
    ]
    for n, (h, j) in enumerate(blocks):
        o_part[j * CHUNK : (j + 1) * CHUNK, h * DH : (h + 1) * DH] = dot(mixing[n], chunk(v, h, j), 1, 0)
    for h in range(heads):
        p_first[h // pair, h % pair] = dot(v_t[h, :, :CHUNK], fs[2 * h], 1, 0)
    relay_x((4, 0), (5, 0), (4, 1), (5, 1))

    rows_x = tokens // nx
    loads[4].wait()

    def head_cols(g, i):
        return pl.ds(pl.multiple_of(g * (pair * DH) + i * DH, DH), DH)

    def n_copy(d, g, i, slot):
        cols = head_cols(g, i)
        number = g * pair + i
        return remote(
            n_out.at[d, :, cols], n_in.at[slot, :, cols], n_send.at[d, number], n_recv.at[slot, number], {"head": modx(d)}
        )

    for i in range(pair):
        wait_back(1, i)

        @pl.when(jnp.logical_not(is_first))
        def _(i=i):
            p_before_core(i, p_pre[i])
            swaps_p[i].start()

        pending.append(swaps_p[i].wait_send)
        for g in (c, 1 - c):
            if g is not c:
                swap_p(i, g).wait_recv()
            cols = head_cols(g, i)
            p_h = p_mine[g, i]
            p_fin[0] = p_h
            p_fin[1] = (p_h.astype(F32) + p_first[g, i]).astype(BF16)
            for d in (2, 1, 3, 0):
                target = modx(d)
                rows = pl.ds(pl.multiple_of(target * rows_x, rows_x), rows_x)
                part = target // (CHUNK // rows_x)
                attended = o_part[rows, cols] + dot(q[rows, cols], p_fin[part], 1, 1)
                mean_square = jnp.mean(attended * attended, axis=-1, keepdims=True)
                n_out[d, :, cols] = (attended * lax.rsqrt(mean_square + EPS) * gain[:, cols]).astype(BF16)
                if d:
                    start(n_copy(d, g, i, x))

    loads[3].wait()
    tile = 512
    n_cols = out_ref.shape[1]

    def project(rows_in, slot, quarter, first, last):
        for begin in range(0, n_cols, tile):
            cols = slice(begin, begin + tile)
            part = dot(rows_in[slot], w[quarter, :, cols], 1, 0)
            if not first:
                part = part + acc[:, cols]
            if last:
                out_ref[:, cols] = part.astype(BF16)
            else:
                acc[:, cols] = part

    project(n_out, 0, x, True, False)
    arrive_plane(2)
    arrive_plane(3)
    arrive_last()
    for offset in (-1, 1, 2):
        quarter = modx(offset)
        for number, (of, _) in enumerate(X_PIECES):
            if of == offset:
                core_copy(number, 1 - c).wait_recv()
                for part in PARTS[number] if number >= 4 else (None,):
                    core_plane_copy(number, part, 1 - c).wait_recv()
        for head in range(heads):
            n_copy(offset % nx, head // pair, head % pair, quarter).wait_recv()
        project(n_in, quarter, quarter, False, offset == 2)

    for wait in pending:
        wait()
    drain_in(0)
    drain_in(1)

    @pl.when(is_worker)
    def _():
        for kind in range(2):
            drain_back(kind)
            drain_totals(kind)


def shards(ny, nz, nx, queries, key_vectors, value_vectors, norm_gain, out_weight):
    tokens, width = queries.shape
    heads = width // DH
    pair = heads // 2
    depth, n_cols = out_weight.shape

    def matrices(*lead, kind=BF16):
        return pltpu.VMEM(lead + (DH, DH), kind)

    operands = (queries, key_vectors, value_vectors, norm_gain.reshape(1, width), out_weight)
    return pl.pallas_call(
        functools.partial(kernel, ny, nz, nx),
        out_shape=jax.ShapeDtypeStruct((tokens // nx, n_cols), BF16),
        in_specs=[pl.BlockSpec(memory_space=pltpu.HBM)] * 5,
        out_specs=pl.BlockSpec(memory_space=pltpu.VMEM),
        scratch_shapes=[
            pltpu.VMEM((tokens, width), BF16),
            pltpu.VMEM((tokens, width), BF16),
            pltpu.VMEM((tokens, width), BF16),
            pltpu.VMEM((nx, depth, n_cols), BF16),
            pltpu.VMEM((1, width), F32),
            matrices(heads),
            matrices(2, pair),
            matrices(2, pair, 2),
            matrices(pair),
            matrices(pair, 2),
            matrices(pair),
            matrices(pair, 2),
            matrices(nz),
            matrices(nz, 2),
            matrices(nz, kind=F32),
            matrices(nz, kind=F32),
            matrices(nz),
            matrices(nz),
            matrices(nz),
            matrices(3),
            matrices(ny, 3),
            matrices(pair),
            matrices(pair),
            matrices(pair, kind=F32),
            matrices(pair),
            matrices(pair),
            matrices(2, pair),
            matrices(2, pair),
            pltpu.VMEM((heads, DH, tokens), BF16),
            pltpu.VMEM((tokens, width), F32),
            matrices(2, pair, kind=F32),
            pltpu.VMEM((tokens, width), F32),
            matrices(2),
            pltpu.VMEM((nx, tokens // nx, width), BF16),
            pltpu.VMEM((nx, tokens // nx, width), BF16),
            pltpu.VMEM((tokens // nx, n_cols), F32),
            pltpu.SemaphoreType.DMA((5,)),
            pltpu.SemaphoreType.DMA((3 + pair,)),
            pltpu.SemaphoreType.DMA((3 + pair,)),
            pltpu.SemaphoreType.DMA((2, pair)),
            pltpu.SemaphoreType.DMA((2, nz)),
            pltpu.SemaphoreType.DMA((2, nz)),
            pltpu.SemaphoreType.DMA((2, pair)),
            pltpu.SemaphoreType.DMA((2, ny)),
            pltpu.SemaphoreType.DMA((2, ny)),
            pltpu.SemaphoreType.DMA((nx, heads)),
            pltpu.SemaphoreType.DMA((nx, heads)),
            pltpu.SemaphoreType.DMA((44,)),
            pltpu.SemaphoreType.DMA((44,)),
        ],
        compiler_params=pltpu.CompilerParams(
            collective_id=0, has_side_effects=True, vmem_limit_bytes=48 * 1024 * 1024
        ),
    )(*[pltpu.with_memory_space_constraint(array, pltpu.HBM) for array in operands])


def solution(mesh):
    seq, nx = mesh.shape["seq"], mesh.shape["head"]
    ny = 4 if seq == 64 else 2
    nz = seq // (2 * ny)
    split = Mesh(mesh.devices.reshape(ny, nz, 2, nx), SEQ_HEAD)
    in_specs = (P(SEQ, "head"), P(SEQ, "head"), P(SEQ, "head"), P("head"), P("head", None))
    out_specs = P(SEQ_HEAD, None)
    return jax.shard_map(
        functools.partial(shards, ny, nz, nx), mesh=split, in_specs=in_specs, out_specs=out_specs, check_vma=False
    )
```
